256 devices in a mesh: dp: 32 (over x, z), mp: 8 (over y, core).
Axes of the slice: x: 4, y: 4, z: 8, core: 2. Of those that a mesh axis runs over, the one named last changes fastest.
Arguments:
- vision: bfloat16 [8192, 3200], P(('dp', 'mp')), may hold values from -6 to 6
- vision_gain: float32 [3200], replicated, may hold values from 0.1 to 1.9
- image_slot: int32 [32], replicated, may hold values from 0 to 63, as said below
- text_embed: bfloat16 [16384, 8192], P('dp', 'mp'), may hold values from -6 to 6
- w_proj: bfloat16 [3200, 8192], P(None, 'mp'), may hold values from -0.109375 to 0.109375
- llm_gain: float32 [8192], P('mp'), may hold values from 0.1 to 1.9
- w_key: bfloat16 [8192, 1024], P('mp'), may hold values from -0.0625 to 0.0625
- w_value: bfloat16 [8192, 1024], P('mp'), may hold values from -0.0625 to 0.0625
- key_grad: bfloat16 [16384, 1024], P('dp', 'mp'), may hold values from -6 to 6
- value_grad: bfloat16 [16384, 1024], P('dp', 'mp'), may hold values from -6 to 6
Outputs:
- key_out: bfloat16 [16384, 1024], P('dp', 'mp')
- value_out: bfloat16 [16384, 1024], P('dp', 'mp')
- text_grad: bfloat16 [16384, 8192], P('dp', 'mp')
- vision_grad: bfloat16 [8192, 3200], P(('dp', 'mp'))
The draws below stay inside these ranges and needn't reach their ends.
Inputs may be any that keep to these rules, and one draw needn't show every extreme that they name: `image_slot`: the 32 entries are different slots. Image i is encoded on index i of dp; slot j covers positions j * 256 to (j + 1) * 256 - 1, so it lies on index j // 2 of dp. One index of dp receives 2 images, every other one at most one.
All inputs are finite; a program needn't handle non-finite values.
Results may differ from the reference program's by a relative error of at most 0.0058.
Values may be sent and summed in bfloat16 or wider, within the bound.
No kernel may reach another device: no remote copies, remote signals or barrier semaphores. Data moves between devices by JAX's collectives and lax.ppermute only.
A program may use at most 128 MiB of HBM per device.

```python
import jax
import jax.numpy as jnp
from jax import lax

DV = 3200
D = 8192
KV = 1024
PATCH = 256
SLOT_DEV = 2
IMAGES = 32
TOKENS = 16384


def draw_image_slot(key, part):
    first_key, second_key, third_key, fourth_key = jax.random.split(key, 4)
    count = IMAGES
    sources = jnp.arange(count, dtype=jnp.int32)
    heavy = jax.random.randint(first_key, (), 0, count).astype(jnp.int32)
    before = (heavy - 1) % count
    across = (heavy + 1 - count // 2) % count
    forced = (sources == before) | (sources == across)
    shuffled = jax.random.permutation(second_key, count).astype(jnp.int32)
    score = jnp.where(forced, count + sources, shuffled)
    order = jnp.argsort(score, stable=True).astype(jnp.int32)
    rank = jnp.zeros((count,), jnp.int32).at[order].set(sources)
    other_dest = (heavy + 2 + jax.random.permutation(third_key, count - 2).astype(jnp.int32)) % count
    later = jnp.clip(rank - (SLOT_DEV - 1), 0, count - 3)
    random_within = jax.random.randint(fourth_key, (count,), 0, SLOT_DEV).astype(jnp.int32)
    to_heavy = rank < SLOT_DEV - 1
    dest_of = jnp.where(to_heavy, heavy, other_dest[later])
    within = jnp.where(to_heavy, rank + 1, random_within)
    dest_of = jnp.where(sources == before, heavy, dest_of)
    within = jnp.where(sources == before, 0, within)
    dest_of = jnp.where(sources == across, (heavy + 1) % count, dest_of)
    slots = dest_of * SLOT_DEV + within
    return slots.astype(jnp.int32)


def block_scale(own_key, dims, shards, smallest, high):
    gain = 1.0
    for position, shards_of in shards:
        draws = jax.random.uniform(jax.random.fold_in(jax.random.fold_in(own_key, 6), position), (shards_of,), jnp.float32, smallest / len(shards), high / len(shards))
        gain = gain * jnp.repeat(jnp.exp(draws), dims[position] // shards_of).reshape((-1,) + (1,) * (len(dims) - 1 - position))
    return gain


def noise(stream_key, dims, spread, most, cuts=(), held_as=jnp.bfloat16):
    drawn = jax.random.normal(stream_key, dims, jnp.float32) * spread
    if len(cuts) > 0:
        drawn = block_scale(stream_key, dims, cuts, -0.22, 0.18) * drawn
    return jnp.clip(drawn, min=-most, max=most).astype(held_as)


def setup_inputs(seed: int = 0) -> dict:
    arg_keys = jax.random.split(jax.random.key(seed), 11)
    vision = noise(arg_keys[0], (IMAGES * PATCH, DV), 1.0, 6.0, ((0, 256),))
    vision_gain = jnp.clip(1.0 + 0.18 * jax.random.normal(arg_keys[1], (DV,), jnp.float32), 0.1, 1.9)
    image_slot = draw_image_slot(jax.random.fold_in(arg_keys[10], 71), 0)
    text_embed = noise(arg_keys[3], (TOKENS, D), 1.0, 6.0, ((0, 32), (1, 8)))
    w_proj = noise(arg_keys[4], (DV, D), DV ** -0.5, 0.109375, ((1, 8),))
    llm_gain = jnp.clip(1.0 + 0.18 * jax.random.normal(arg_keys[5], (D,), jnp.float32), 0.1, 1.9)
    w_key = noise(arg_keys[6], (D, KV), D ** -0.5, 0.0625, ((0, 8),))
    w_value = noise(arg_keys[7], (D, KV), D ** -0.5, 0.0625, ((0, 8),))
    key_grad = noise(arg_keys[8], (TOKENS, KV), 1.0, 6.0, ((0, 32), (1, 8)))
    value_grad = noise(arg_keys[9], (TOKENS, KV), 1.0, 6.0, ((0, 32), (1, 8)))
    return dict(vision=vision, vision_gain=vision_gain, image_slot=image_slot, text_embed=text_embed, w_proj=w_proj, llm_gain=llm_gain, w_key=w_key, w_value=w_value, key_grad=key_grad, value_grad=value_grad)


def reference(vision, vision_gain, image_slot, text_embed, w_proj, llm_gain, w_key, w_value, key_grad, value_grad):
    vision_f = vision.astype(jnp.float32)
    vis_scale = lax.rsqrt(lax.optimization_barrier(jnp.mean(vision_f * vision_f, axis=1, keepdims=True)) + 1e-06)
    vis_normed = (vision_f * vis_scale * vision_gain.astype(jnp.float32)).astype(jnp.bfloat16)
    slot_count = TOKENS // PATCH
    onehot = image_slot[:, None] == jnp.arange(slot_count, dtype=jnp.int32)[None, :]
    filled = jnp.any(onehot, axis=0)
    owner = lax.optimization_barrier(jnp.sum(jnp.where(onehot, jnp.arange(IMAGES, dtype=jnp.int32)[:, None], 0), axis=0)).astype(jnp.int32)
    projected = jnp.dot(vis_normed, w_proj, preferred_element_type=jnp.float32).astype(jnp.bfloat16)
    projected = projected.reshape(IMAGES, PATCH, D)
    placed = projected[owner]
    text_blocks = text_embed.reshape(slot_count, PATCH, D)
    embed = jnp.where(filled[:, None, None], placed, text_blocks).reshape(TOKENS, D)
    embed_f = embed.astype(jnp.float32)
    scale = lax.rsqrt(lax.optimization_barrier(jnp.mean(embed_f * embed_f, axis=1, keepdims=True)) + 1e-05)
    gain_f = llm_gain.astype(jnp.float32)
    llm_normed = (embed_f * scale * gain_f).astype(jnp.bfloat16)
    key_out = jnp.dot(llm_normed, w_key, preferred_element_type=jnp.float32).astype(jnp.bfloat16)
    value_out = jnp.dot(llm_normed, w_value, preferred_element_type=jnp.float32).astype(jnp.bfloat16)
    d_normed = jnp.dot(key_grad, w_key.T, preferred_element_type=jnp.float32)
    d_normed = d_normed + jnp.dot(value_grad, w_value.T, preferred_element_type=jnp.float32)
    grad_g = d_normed * gain_f
    inner = lax.optimization_barrier(jnp.sum(grad_g * embed_f, axis=1, keepdims=True))
    d_embed = scale * grad_g - embed_f * scale * scale * scale * (inner / D)
    d_blocks = d_embed.reshape(slot_count, PATCH, D)
    text_grad = jnp.where(filled[:, None, None], 0.0, d_blocks).reshape(TOKENS, D).astype(jnp.bfloat16)
    image_grad = d_blocks[image_slot].reshape(IMAGES * PATCH, D).astype(jnp.bfloat16)
    d_vis = jnp.dot(image_grad, w_proj.T, preferred_element_type=jnp.float32).astype(jnp.bfloat16)
    grad_h = d_vis.astype(jnp.float32) * vision_gain.astype(jnp.float32)
    vis_inner = lax.optimization_barrier(jnp.mean(grad_h * vision_f, axis=1, keepdims=True))
    vision_grad = vis_scale * grad_h - vision_f * vis_scale * vis_scale * vis_scale * vis_inner
    return (key_out, value_out, text_grad, vision_grad.astype(jnp.bfloat16))
```

```python
import functools

import jax
import jax.numpy as jnp
from jax import lax
from jax.experimental import pallas as pl
from jax.experimental.pallas import tpu as pltpu
from jax.sharding import PartitionSpec as P

D = 8192
DV = 3200
PATCH = 256
BF = jnp.bfloat16
F32 = jnp.float32

RING = 4
UP = [(2 * y + c, 2 * ((y + 1) % RING) + c) for y in range(RING) for c in range(2)]
DOWN = [(2 * y + c, 2 * ((y + 3) % RING) + c) for y in range(RING) for c in range(2)]
ACROSS = [(2 * y + c, 2 * ((y + 2) % RING) + c) for y in range(RING) for c in range(2)]
PEER = [(2 * y + c, 2 * y + 1 - c) for y in range(RING) for c in range(2)]


def up(x):
    return lax.ppermute(x, "mp", UP)


def down(x):
    return lax.ppermute(x, "mp", DOWN)


def across(x):
    return lax.ppermute(x, "mp", ACROSS)


def peer(x):
    return lax.ppermute(x, "mp", PEER)


def ring_gather(x):
    half = x.shape[0] // 2
    below, above = up(x), down(x)
    far = [up(below[:half]), down(above[half:])]
    mine = [[x], [above], far, [below]]
    other = [[peer(t) for t in part] for part in mine]
    return mine + other


def ring_scatter(parts):
    here, above, far, below = parts
    half = here.shape[0] // 2
    above_b, far_b, below_b = (t.astype(BF) for t in (above, far, below))
    up1 = up(jnp.concatenate([far_b[:half], above_b[half:]]))
    down1 = down(jnp.concatenate([below_b[:half], far_b[half:]]))
    up2 = up((above[:half] + up1[:half].astype(F32)).astype(BF))
    down2 = down((below[half:] + down1[half:].astype(F32)).astype(BF))
    first = here[:half] + down1[:half].astype(F32) + up2.astype(F32)
    second = here[half:] + up1[half:].astype(F32) + down2.astype(F32)
    return jnp.concatenate([first, second])


def small_sum(x):
    pair = x + peer(x)
    return (pair + up(pair)) + (down(pair) + across(pair))


def permute_weights(order, w_key, w_value):
    rows, cols = w_key.shape
    blk = cols // 8

    def kernel(order_ref, k_ref, v_ref, o_ref):
        o_ref[:, :blk] = k_ref[...]
        o_ref[:, blk:] = v_ref[...]

    return pl.pallas_call(
        kernel,
        grid_spec=pltpu.PrefetchScalarGridSpec(
            num_scalar_prefetch=1,
            grid=(8,),
            in_specs=[
                pl.BlockSpec((rows, blk), lambda b, order: (0, order[b])),
                pl.BlockSpec((rows, blk), lambda b, order: (0, order[b])),
            ],
            out_specs=pl.BlockSpec((rows, 2 * blk), lambda b, order: (0, b)),
        ),
        out_shape=jax.ShapeDtypeStruct((rows, 2 * cols), BF),
        name="permute_weights",
    )(order, w_key, w_value)


def take_blocks(index, x):
    count = index.shape[0]

    def kernel(index_ref, x_ref, o_ref):
        for j in range(count):
            o_ref[j] = x_ref[index_ref[j]]

    return pl.pallas_call(
        kernel,
        in_specs=[
            pl.BlockSpec(memory_space=pltpu.SMEM),
            pl.BlockSpec(memory_space=pltpu.VMEM),
        ],
        out_specs=pl.BlockSpec(memory_space=pltpu.VMEM),
        out_shape=jax.ShapeDtypeStruct((count,) + x.shape[1:], x.dtype),
        name="take_blocks",
    )(index, x)


def dot_t(a, b):
    return lax.dot_general(a, b, (((1,), (1,)), ((), ())), preferred_element_type=F32)


def shards(
    vision,
    vision_gain,
    image_slot,
    text_embed,
    w_proj,
    llm_gain,
    w_key,
    w_value,
    key_grad,
    value_grad,
):
    dp = lax.axis_size("dp")
    here = lax.axis_index("dp")
    m = lax.axis_index("mp")
    y, c = m // 2, m % 2
    slots = text_embed.shape[0] // PATCH
    rows = vision.shape[0]
    step = PATCH // dp

    rel = jnp.arange(8, dtype=jnp.int32)
    order = ((y + rel % RING) % RING) * 2 + (c ^ (rel // RING))
    row = jnp.arange(PATCH, dtype=jnp.int32)
    source = order[row // rows] * rows + row % rows
    place = (source[None, :] == row[:, None]).astype(BF)

    slot_ids = jnp.arange(dp * slots, dtype=jnp.int32)
    onehot = slot_ids[:, None] == image_slot[None, :]
    owner = jnp.sum(jnp.where(onehot, jnp.arange(dp, dtype=jnp.int32)[None, :], 0), axis=1)
    mine = slot_ids[:slots] + here * slots
    filled = jnp.any(mine[:, None] == image_slot[None, :], axis=1)

    grads = jnp.stack([key_grad.reshape(slots, dp, step, -1), value_grad.reshape(slots, dp, step, -1)], axis=2)
    grads = grads.transpose(1, 0, 2, 3, 4).reshape(dp, slots, 2 * step, 128)
    with jax.named_scope("slot_grads_spread"):
        spread = lax.all_to_all(grads, "dp", split_axis=0, concat_axis=0, tiled=True)
    picked = take_blocks(image_slot, spread.reshape(dp * slots, 2 * step, 128))
    with jax.named_scope("slot_grads_collect"):
        image_kv_grad = lax.all_to_all(picked, "dp", split_axis=0, concat_axis=0, tiled=True)
    image_kv_grad = image_kv_grad.reshape(dp, 2, step, 128)
    image_kv_grad = jnp.concatenate(
        [image_kv_grad[:, 0].reshape(PATCH, 128), image_kv_grad[:, 1].reshape(PATCH, 128)], axis=1
    )

    vision_f = vision.astype(F32)
    vis_scale = lax.rsqrt(jnp.mean(vision_f * vision_f, axis=1, keepdims=True) + 1e-06)
    vis_normed = (vision_f * vis_scale * vision_gain).astype(BF)
    with jax.named_scope("vision_gather"):
        parts = ring_gather(vis_normed)
    vis_all = jnp.concatenate([t for part in parts for t in part])
    projected = jnp.dot(vis_all, w_proj, preferred_element_type=F32).astype(BF)
    image_embed = jnp.dot(place, projected, preferred_element_type=F32).astype(BF)

    weights = permute_weights(order, w_key, w_value)
    text_kv_grad = jnp.concatenate([key_grad, value_grad], axis=1)
    with jax.named_scope("text_grad_gather"):
        text_g = ring_gather(text_kv_grad)
    text_g = jnp.concatenate([jnp.concatenate(part) for part in text_g], axis=1)

    def forward(embed):
        scaled = (embed.astype(F32) * llm_gain).astype(BF)
        far = jnp.dot(scaled, weights[:, 1024:], preferred_element_type=F32).astype(BF)
        near = jnp.dot(scaled, weights[:, :1024], preferred_element_type=F32)
        near = near + peer(far).astype(F32)
        return ring_scatter(lax.optimization_barrier([near[:, 256 * k : 256 * (k + 1)] for k in range(RING)]))

    def squares(embed):
        e = embed.astype(F32)
        return jnp.sum(e * e, axis=1)

    with jax.named_scope("text_forward"):
        text_kv = forward(text_embed)
    with jax.named_scope("image_forward"):
        image_kv = forward(image_embed)
        image_square = small_sum(squares(image_embed).reshape(2, 128)).reshape(PATCH, 1)
        image_scale = lax.rsqrt(image_square / D + 1e-05)
        image_kv = (image_kv * image_scale).astype(BF)

    image_kv = jnp.stack([image_kv[:, :128].reshape(dp, step, 128), image_kv[:, 128:].reshape(dp, step, 128)], axis=1)
    with jax.named_scope("image_out_spread"):
        spread = lax.all_to_all(image_kv.reshape(dp, 2 * step, 128), "dp", split_axis=0, concat_axis=0, tiled=True)
    packed = take_blocks(owner, spread).reshape(dp, slots, 2 * step, 128)
    with jax.named_scope("image_out_collect"):
        arrived = lax.all_to_all(packed, "dp", split_axis=0, concat_axis=0, tiled=True)
    arrived = arrived.reshape(dp, slots, 2, step, 128).transpose(2, 1, 0, 3, 4).reshape(2, slots, PATCH, 128)

    with jax.named_scope("image_grad_gather"):
        image_g = ring_gather(image_kv_grad)
    image_g = jnp.concatenate([jnp.concatenate(part) for part in image_g], axis=1)
    text_d = dot_t(text_g, weights) * llm_gain
    image_d = dot_t(image_g, weights) * llm_gain
    text_f = text_embed.astype(F32)
    image_f = image_embed.astype(F32)
    stats = jnp.concatenate(
        [
            squares(text_embed).reshape(4, 128),
            jnp.sum(text_d * text_f, axis=1).reshape(4, 128),
            jnp.sum(image_d * image_f, axis=1).reshape(2, 128),
        ]
    )
    with jax.named_scope("row_sums"):
        stats = small_sum(stats)
    text_scale = lax.rsqrt(stats[:4].reshape(-1, 1) / D + 1e-05)
    text_inner = stats[4:8].reshape(-1, 1)
    image_inner = stats[8:].reshape(-1, 1)

    image_grad = image_scale * image_d - image_f * (image_scale * image_scale * image_scale * (image_inner / D))
    image_grad = image_grad.astype(BF)
    image_grad = lax.dot_general(place, image_grad, (((0,), (0,)), ((), ())), preferred_element_type=F32).astype(BF)
    half = PATCH // 2
    d_far = dot_t(image_grad[half:], w_proj).astype(BF)
    d_near = dot_t(image_grad[:half], w_proj) + peer(d_far).astype(F32)
    with jax.named_scope("d_vis_sum"):
        d_vis = ring_scatter([d_near[rows * k : rows * (k + 1)] for k in range(RING)])
    grad_h = d_vis.astype(BF).astype(F32) * vision_gain
    vis_inner = jnp.mean(grad_h * vision_f, axis=1, keepdims=True)
    vision_grad = vis_scale * grad_h - vision_f * vis_scale * vis_scale * vis_scale * vis_inner

    text_grad = text_scale * text_d - text_f * (text_scale * text_scale * text_scale * (text_inner / D))
    keep = jnp.repeat(filled, PATCH)[:, None]
    text_grad = jnp.where(keep, 0.0, text_grad).astype(BF)
    text_kv = (text_kv * text_scale).astype(BF)
    key_out = jnp.where(keep, arrived[0].reshape(-1, 128), text_kv[:, :128])
    value_out = jnp.where(keep, arrived[1].reshape(-1, 128), text_kv[:, 128:])
    return key_out, value_out, text_grad, vision_grad.astype(BF)


def solution(mesh):
    placed = (
        P(("dp", "mp"), None),
        P(),
        P(),
        P("dp", "mp"),
        P(None, "mp"),
        P("mp"),
        P("mp", None),
        P("mp", None),
        P("dp", "mp"),
        P("dp", "mp"),
    )
    return jax.shard_map(
        shards,
        mesh=mesh,
        in_specs=placed,
        out_specs=(P("dp", "mp"), P("dp", "mp"), P("dp", "mp"), P(("dp", "mp"), None)),
        check_vma=False,
    )
```

```python
import jax
import jax.numpy as jnp
from jax import lax
from jax.experimental import pallas as pl
from jax.experimental.pallas import tpu as pltpu
from jax.sharding import PartitionSpec as P

D = 8192
DV = 3200
PATCH = 256
LANE = 128
CHUNK = 16
BF = jnp.bfloat16
F32 = jnp.float32
VMEM = pl.BlockSpec(memory_space=pltpu.VMEM)
SMEM = pl.BlockSpec(memory_space=pltpu.SMEM)

RING = 4
UP = [(2 * y + c, 2 * ((y + 1) % RING) + c) for y in range(RING) for c in range(2)]
DOWN = [(2 * y + c, 2 * ((y + 3) % RING) + c) for y in range(RING) for c in range(2)]
ACROSS = [(2 * y + c, 2 * ((y + 2) % RING) + c) for y in range(RING) for c in range(2)]
PEER = [(2 * y + c, 2 * y + 1 - c) for y in range(RING) for c in range(2)]


def up(x):
    return lax.ppermute(x, "mp", UP)


def down(x):
    return lax.ppermute(x, "mp", DOWN)


def across(x):
    return lax.ppermute(x, "mp", ACROSS)


def peer(x):
    return lax.ppermute(x, "mp", PEER)


def call(kernel, name, outs, args, scalars=0, scratch=(), flops=0, mib=40):
    size = sum(a.size * a.dtype.itemsize for a in args) + sum(o.size * o.dtype.itemsize for o in outs)
    return pl.pallas_call(
        kernel,
        in_specs=[SMEM] * scalars + [VMEM] * (len(args) - scalars),
        out_specs=[VMEM] * len(outs),
        out_shape=list(outs),
        scratch_shapes=list(scratch),
        compiler_params=pltpu.CompilerParams(vmem_limit_bytes=mib * 1024 * 1024),
        cost_estimate=pl.CostEstimate(flops=flops, bytes_accessed=size, transcendentals=0),
        name=name,
    )(*args)


def shape(dims, dtype):
    return jax.ShapeDtypeStruct(dims, dtype)


def dot(a, b):
    return jnp.dot(a, b, preferred_element_type=F32)


def dot_t(a, b):
    return lax.dot_general(a, b, (((1,), (1,)), ((), ())), preferred_element_type=F32)


def as_row(column):
    n = column.shape[0]
    return jnp.transpose(jnp.broadcast_to(column, (n, LANE)))[:1]


def as_column(row):
    n = row.shape[1]
    return jnp.transpose(jnp.broadcast_to(row, (LANE, n)))[:, :1]


def lane_block(ref, index, rows=slice(None)):
    return ref[rows, pl.ds(pl.multiple_of(index * LANE, LANE), LANE)]


def vision_norm(vision, gain):
    def kernel(v_ref, g_ref, o_ref, s_ref):
        v = v_ref[...].astype(F32)
        scale = lax.rsqrt(jnp.mean(v * v, axis=1, keepdims=True) + 1e-06)
        s_ref[...] = scale
        o_ref[...] = (v * scale * g_ref[...]).astype(BF)

    rows = vision.shape[0]
    return call(kernel, "vision_norm", [shape(vision.shape, BF), shape((rows, 1), F32)], [vision, gain])


def pack_grads(key_grad, value_grad):
    rows = key_grad.shape[0]
    slots = rows // PATCH
    per = PATCH // CHUNK

    def kernel(k_ref, v_ref, stack_ref, chunk_ref):
        stack_ref[:rows] = k_ref[...]
        stack_ref[rows:] = v_ref[...]
        for s in range(slots):
            for c in range(per):
                at = pl.ds(s * PATCH + c * CHUNK, CHUNK)
                chunk_ref[c, s] = k_ref[at]
                chunk_ref[per + c, s] = v_ref[at]

    return call(
        kernel,
        "pack_grads",
        [shape((2 * rows, LANE), BF), shape((2 * per, slots, CHUNK, LANE), BF)],
        [key_grad, value_grad],
    )


def take_blocks(index, x):
    count = index.shape[0]

    def kernel(index_ref, x_ref, o_ref):
        for j in range(count):
            o_ref[j] = x_ref[index_ref[j]]

    return call(kernel, "take_blocks", [shape((count,) + x.shape[1:], x.dtype)], [index, x], scalars=1)[0]


def text_forward(text, gain, w_key, w_value):
    rows, width = text.shape
    blocks = w_key.shape[1] // LANE

    def kernel(t_ref, g_ref, k_ref, v_ref, o_ref, q_ref, scaled):
        @pl.loop(0, rows // 64)
        def _(i):
            at = pl.ds(pl.multiple_of(i * 64, 64), 64)
            scaled[at] = (t_ref[at].astype(F32) * g_ref[...]).astype(BF)

        @pl.loop(0, rows // LANE)
        def _(i):
            t = t_ref[pl.ds(pl.multiple_of(i * LANE, LANE), LANE)].astype(F32)
            q_ref[pl.ds(i, 1)] = as_row(jnp.sum(t * t, axis=1, keepdims=True))

        @pl.loop(0, blocks)
        def _(b):
            w = jnp.concatenate([lane_block(k_ref, b), lane_block(v_ref, b)], axis=1)
            o_ref[b] = dot(scaled[...], w).astype(BF)

    return call(
        kernel,
        "text_forward",
        [shape((blocks, rows, 2 * LANE), BF), shape((rows // LANE, LANE), F32)],
        [text, gain, w_key, w_value],
        scratch=[pltpu.VMEM((rows, width), BF)],
        flops=4 * rows * width * w_key.shape[1],
    )


def image_forward(order, parts, w_proj, gain, w_key, w_value):
    pieces = [t for part in parts for t in part]
    starts = []
    for b, part in enumerate(parts):
        at = 0
        for t in part:
            starts.append((b, at))
            at += t.shape[0]
    rows_each = PATCH // len(parts)
    depth, width = w_proj.shape

    def kernel(order_ref, *refs):
        piece_refs = refs[: len(pieces)]
        p_ref, g_ref, k_ref, v_ref, e_ref, far_ref, near_ref, q_ref, vis, scaled = refs[len(pieces) :]
        for (b, at), ref in zip(starts, piece_refs):
            row = pl.multiple_of(order_ref[b] * rows_each + at, 16)
            vis[pl.ds(row, ref.shape[0])] = ref[...]

        @pl.loop(0, width // 256)
        def _(n):
            cols = pl.ds(pl.multiple_of(n * 256, 256), 256)
            e_ref[:, cols] = dot(vis[...], p_ref[:, cols]).astype(BF)

        @pl.loop(0, PATCH // LANE)
        def _(i):
            at = pl.ds(pl.multiple_of(i * LANE, LANE), LANE)
            e = e_ref[at].astype(F32)
            scaled[at] = (e * g_ref[...]).astype(BF)
            q_ref[pl.ds(i, 1)] = as_row(jnp.sum(e * e, axis=1, keepdims=True))

        @pl.loop(0, RING)
        def _(b):
            there = order_ref[RING + b]
            w = jnp.concatenate([lane_block(k_ref, there), lane_block(v_ref, there)], axis=1)
            far_ref[b] = dot(scaled[...], w).astype(BF)
            own = order_ref[b]
            w = jnp.concatenate([lane_block(k_ref, own), lane_block(v_ref, own)], axis=1)
            near_ref[b] = dot(scaled[...], w)

    return call(
        kernel,
        "image_forward",
        [
            shape((PATCH, width), BF),
            shape((RING, PATCH, 2 * LANE), BF),
            shape((RING, PATCH, 2 * LANE), F32),
            shape((PATCH // LANE, LANE), F32),
        ],
        [order, *pieces, w_proj, gain, w_key, w_value],
        scalars=1,
        scratch=[pltpu.VMEM((PATCH, depth), BF), pltpu.VMEM((PATCH, width), BF)],
        flops=2 * PATCH * width * (depth + 2 * w_key.shape[1]),
    )


def backward(order, pieces, w_key, w_value, gain, embed):
    rows, width = embed.shape
    cols = w_key.shape[1]

    def kernel(order_ref, *refs):
        piece_refs = refs[: len(pieces)]
        k_ref, v_ref, g_ref, e_ref, d_ref, i_ref, gk, gv = refs[len(pieces) :]
        b = 0
        for ref in piece_refs:
            for j in range(ref.shape[0] // (2 * rows)):
                at = pl.ds(pl.multiple_of(order_ref[b] * LANE, LANE), LANE)
                gk[:, at] = ref[2 * rows * j : 2 * rows * j + rows]
                gv[:, at] = ref[2 * rows * j + rows : 2 * rows * (j + 1)]
                b += 1

        @pl.loop(0, width // 256)
        def _(n):
            at = pl.ds(pl.multiple_of(n * 256, 256), 256)
            d = dot_t(gk[...], k_ref[at]) + dot_t(gv[...], v_ref[at])
            d_ref[:, at] = d * g_ref[:, at]

        @pl.loop(0, rows // LANE)
        def _(i):
            at = pl.ds(pl.multiple_of(i * LANE, LANE), LANE)
            i_ref[pl.ds(i, 1)] = as_row(jnp.sum(d_ref[at] * e_ref[at].astype(F32), axis=1, keepdims=True))

    return call(
        kernel,
        "backward",
        [shape((rows, width), F32), shape((rows // LANE, LANE), F32)],
        [order, *pieces, w_key, w_value, gain, embed],
        scalars=1,
        scratch=[pltpu.VMEM((rows, cols), BF), pltpu.VMEM((rows, cols), BF)],
        flops=4 * rows * width * cols,
    )


def embed_grad(d, e, square_row, inner_row):
    scale = lax.rsqrt(as_column(square_row) / D + 1e-05)
    inner = as_column(inner_row) / D
    return scale * d - e * (scale * scale * scale * inner)


def image_backward(order, image_d, embed, square, inner, w_proj):
    depth, width = w_proj.shape
    rows_each = PATCH // 8
    half = PATCH // 2
    cut = 640

    def kernel(order_ref, d_ref, e_ref, q_ref, i_ref, p_ref, far_ref, near_ref, grad, turned):
        @pl.loop(0, PATCH // LANE)
        def _(i):
            at = pl.ds(pl.multiple_of(i * LANE, LANE), LANE)
            row = pl.ds(i, 1)
            grad[at] = embed_grad(d_ref[at], e_ref[at].astype(F32), q_ref[row], i_ref[row]).astype(BF)

        for b in range(8):
            at = pl.ds(pl.multiple_of(order_ref[b] * rows_each, rows_each), rows_each)
            turned[b * rows_each : (b + 1) * rows_each] = grad[at]

        @pl.loop(0, depth // cut)
        def _(n):
            at = pl.ds(pl.multiple_of(n * cut, LANE), cut)
            r = dot_t(turned[...], p_ref[at])
            near_ref[:, at] = r[:half]
            far_ref[:, at] = r[half:].astype(BF)

    return call(
        kernel,
        "image_backward",
        [shape((half, depth), BF), shape((half, depth), F32)],
        [order, image_d, embed, square, inner, w_proj],
        scalars=1,
        scratch=[pltpu.VMEM((PATCH, width), BF), pltpu.VMEM((PATCH, width), BF)],
        flops=2 * PATCH * width * depth,
    )


def ring_first(near, other):
    _, n, c = near.shape
    h = n // 2

    def kernel(a_ref, b_ref, up_ref, down_ref, here_ref, above_ref, below_ref):
        def total(k, at):
            return a_ref[k, at] + b_ref[k, at].astype(F32)

        first, second = slice(0, h), slice(h, n)
        up_ref[first] = total(2, first).astype(BF)
        up_ref[second] = total(1, second).astype(BF)
        down_ref[first] = total(3, first).astype(BF)
        down_ref[second] = total(2, second).astype(BF)
        here_ref[...] = total(0, slice(0, n))
        above_ref[...] = total(1, first)
        below_ref[...] = total(3, second)

    return call(
        kernel,
        "ring_first",
        [shape((n, c), BF), shape((n, c), BF), shape((n, c), F32), shape((h, c), F32), shape((h, c), F32)],
        [near, other],
    )


def ring_sum(near, far):
    up1, down1, here, above, below = ring_first(near, peer(far).reshape(near.shape))
    h = above.shape[0]
    up1, down1 = up(up1), down(down1)
    up2 = up((above + up1[:h].astype(F32)).astype(BF))
    down2 = down((below + down1[h:].astype(F32)).astype(BF))
    return here, up1, down1, up2, down2


def ring_total(here_ref, up1_ref, down1_ref, up2_ref, down2_ref):
    h = up2_ref.shape[0]
    first = here_ref[:h] + down1_ref[:h].astype(F32) + up2_ref[...].astype(F32)
    second = here_ref[h:] + up1_ref[h:].astype(F32) + down2_ref[...].astype(F32)
    return first, second


def image_out(pieces, square):
    h = PATCH // 2

    def kernel(*refs):
        q_ref, o_ref = refs[5:]
        for j, t in enumerate(ring_total(*refs[:5])):
            scale = lax.rsqrt(as_column(q_ref[j : j + 1]) / D + 1e-05)
            t = (t * scale).astype(BF)
            o_ref[j * h : (j + 1) * h] = t[:, :LANE]
            o_ref[PATCH + j * h : PATCH + (j + 1) * h] = t[:, LANE:]

    return call(kernel, "image_out", [shape((2 * PATCH, LANE), BF)], [*pieces, square])[0]


def vision_out(pieces, vision, gain, scale):
    rows = vision.shape[0]
    h = rows // 2

    def kernel(*refs):
        v_ref, g_ref, s_ref, o_ref = refs[5:]
        for j, t in enumerate(ring_total(*refs[:5])):
            at = slice(j * h, (j + 1) * h)
            v, s = v_ref[at].astype(F32), s_ref[at]
            grad_h = t.astype(BF).astype(F32) * g_ref[...]
            inner = jnp.mean(grad_h * v, axis=1, keepdims=True)
            o_ref[at] = (s * grad_h - v * (s * s * s * inner)).astype(BF)

    return call(kernel, "vision_out", [shape(vision.shape, BF)], [*pieces, vision, gain, scale])[0]


def text_out(filled, text_d, text, square, inner):
    rows, width = text.shape

    def kernel(f_ref, d_ref, t_ref, q_ref, i_ref, o_ref):
        @pl.loop(0, rows // LANE)
        def _(i):
            at = pl.ds(pl.multiple_of(i * LANE, LANE), LANE)
            row = pl.ds(i, 1)
            grad = embed_grad(d_ref[at], t_ref[at].astype(F32), q_ref[row], i_ref[row])
            o_ref[at] = jnp.where(f_ref[i // (PATCH // LANE)] > 0, 0.0, grad).astype(BF)

    return call(
        kernel, "text_out", [shape((rows, width), BF)], [filled, text_d, text, square, inner], scalars=1
    )[0]


def key_value_out(filled, text_kv, square, arrived):
    rows = text_kv.shape[0]
    per = PATCH // CHUNK

    def kernel(f_ref, t_ref, q_ref, a_ref, k_ref, v_ref):
        for s in range(rows // PATCH):
            @pl.when(f_ref[s] > 0)
            def _():
                for c in range(per):
                    at = pl.ds(s * PATCH + c * CHUNK, CHUNK)
                    k_ref[at] = a_ref[c, s]
                    v_ref[at] = a_ref[per + c, s]

            @pl.when(f_ref[s] == 0)
            def _():
                for i in range(PATCH // LANE):
                    j = s * (PATCH // LANE) + i
                    at = pl.ds(j * LANE, LANE)
                    scale = lax.rsqrt(as_column(q_ref[j : j + 1]) / D + 1e-05)
                    t = (t_ref[at].astype(F32) * scale).astype(BF)
                    k_ref[at] = t[:, :LANE]
                    v_ref[at] = t[:, LANE:]

    return call(
        kernel,
        "key_value_out",
        [shape((rows, LANE), BF), shape((rows, LANE), BF)],
        [filled, text_kv, square, arrived],
        scalars=1,
    )


def ring_gather(x):
    half = x.shape[0] // 2
    below, above = up(x), down(x)
    far = [up(below[:half]), down(above[half:])]
    mine = [[x], [above], far, [below]]
    other = [[peer(t) for t in part] for part in mine]
    return mine + other


def short_gather(x):
    mine = [x, down(x), across(x), up(x)]
    return mine + [peer(t) for t in mine]


def small_sum(x):
    pair = x + peer(x)
    return (pair + up(pair)) + (down(pair) + across(pair))


def shards(
    vision,
    vision_gain,
    image_slot,
    text_embed,
    w_proj,
    llm_gain,
    w_key,
    w_value,
    key_grad,
    value_grad,
):
    dp = lax.axis_size("dp")
    here = lax.axis_index("dp")
    m = lax.axis_index("mp")
    y, c = m // 2, m % 2
    slots = text_embed.shape[0] // PATCH
    text_rows = text_embed.shape[0] // LANE

    rel = jnp.arange(8, dtype=jnp.int32)
    order = ((y + rel % RING) % RING) * 2 + (c ^ (rel // RING))
    slot_ids = jnp.arange(dp * slots, dtype=jnp.int32)
    onehot = slot_ids[:, None] == image_slot[None, :]
    owner = jnp.sum(jnp.where(onehot, jnp.arange(dp, dtype=jnp.int32)[None, :], 0), axis=1)
    mine = slot_ids[:slots] + here * slots
    filled = jnp.any(mine[:, None] == image_slot[None, :], axis=1).astype(jnp.int32)
    gain = llm_gain[None]
    vis_gain = vision_gain[None]

    vis_normed, vis_scale = vision_norm(vision, vis_gain)
    with jax.named_scope("vision_gather"):
        vis_parts = ring_gather(vis_normed)

    grad_stack, grad_chunks = pack_grads(key_grad, value_grad)
    with jax.named_scope("text_grad_gather"):
        text_g = lax.all_gather(grad_stack, "mp", axis=0, tiled=True)
    with jax.named_scope("slot_grads_spread"):
        spread = lax.all_to_all(grad_chunks, "dp", split_axis=0, concat_axis=0, tiled=True)
    picked = take_blocks(image_slot, spread.reshape(dp * slots, CHUNK, LANE))
    with jax.named_scope("slot_grads_collect"):
        image_kv_grad = lax.all_to_all(picked, "dp", split_axis=0, concat_axis=0, tiled=True)
    with jax.named_scope("image_grad_gather"):
        image_g = short_gather(image_kv_grad.reshape(2 * PATCH, LANE))

    text_part, text_square = text_forward(text_embed, gain, w_key, w_value)
    with jax.named_scope("text_key_value_sum"):
        text_kv = lax.psum_scatter(text_part, "mp", scatter_dimension=0, tiled=False)

    embed, far, near, image_square = image_forward(order, vis_parts, w_proj, gain, w_key, w_value)
    with jax.named_scope("image_key_value_sum"):
        pieces = ring_sum(near, far)
    with jax.named_scope("squares_sum"):
        squares = small_sum(jnp.concatenate([text_square, image_square]))
    text_square, image_square = squares[:text_rows], squares[text_rows:]

    image_kv = image_out(pieces, image_square).reshape(dp, CHUNK, LANE)
    with jax.named_scope("image_out_spread"):
        spread = lax.all_to_all(image_kv, "dp", split_axis=0, concat_axis=0, tiled=True)
    packed = take_blocks(owner, spread).reshape(dp, slots, CHUNK, LANE)
    with jax.named_scope("image_out_collect"):
        arrived = lax.all_to_all(packed, "dp", split_axis=0, concat_axis=0, tiled=True)

    text_d, text_inner = backward(rel, [text_g], w_key, w_value, gain, text_embed)
    image_d, image_inner = backward(order, image_g, w_key, w_value, gain, embed)
    with jax.named_scope("inner_sum"):
        inner = small_sum(jnp.concatenate([text_inner, image_inner]))
    d_far, d_near = image_backward(order, image_d, embed, image_square, inner[text_rows:], w_proj)
    with jax.named_scope("d_vis_sum"):
        d_pieces = ring_sum(d_near.reshape(RING, -1, DV), d_far)
    vision_grad = vision_out(d_pieces, vision, vis_gain, vis_scale)
    text_grad = text_out(filled, text_d, text_embed, text_square, inner[:text_rows])
    key_out, value_out = key_value_out(filled, text_kv, text_square, arrived)
    return key_out, value_out, text_grad, vision_grad


def solution(mesh):
    placed = (
        P(("dp", "mp"), None),
        P(),
        P(),
        P("dp", "mp"),
        P(None, "mp"),
        P("mp"),
        P("mp", None),
        P("mp", None),
        P("dp", "mp"),
        P("dp", "mp"),
    )
    return jax.shard_map(
        shards,
        mesh=mesh,
        in_specs=placed,
        out_specs=(P("dp", "mp"), P("dp", "mp"), P("dp", "mp"), P(("dp", "mp"), None)),
        check_vma=False,
    )
```

```python
import jax
import jax.numpy as jnp
from jax import lax
from jax.experimental import pallas as pl
from jax.experimental.pallas import tpu as pltpu
from jax.sharding import PartitionSpec as P

D = 8192
DV = 3200
PATCH = 256
LANE = 128
CHUNK = 16
BF = jnp.bfloat16
F32 = jnp.float32
VMEM = pl.BlockSpec(memory_space=pltpu.VMEM)
SMEM = pl.BlockSpec(memory_space=pltpu.SMEM)
HBM = pl.BlockSpec(memory_space=pltpu.HBM)
DMA = pltpu.SemaphoreType.DMA

RING = 4
UP = [(2 * y + c, 2 * ((y + 1) % RING) + c) for y in range(RING) for c in range(2)]
DOWN = [(2 * y + c, 2 * ((y + 3) % RING) + c) for y in range(RING) for c in range(2)]
ACROSS = [(2 * y + c, 2 * ((y + 2) % RING) + c) for y in range(RING) for c in range(2)]
PEER = [(2 * y + c, 2 * y + 1 - c) for y in range(RING) for c in range(2)]


def up(x):
    return lax.ppermute(x, "mp", UP)


def down(x):
    return lax.ppermute(x, "mp", DOWN)


def across(x):
    return lax.ppermute(x, "mp", ACROSS)


def peer(x):
    return lax.ppermute(x, "mp", PEER)


TOKEN = jax.ShapeDtypeStruct((8, LANE), F32)


def call(kernel, name, outs, args, scalars=0, far=(), far_outs=(), scratch=(), flops=0, after=(), token=False):
    size = sum(a.size * a.dtype.itemsize for a in args) + sum(o.size * o.dtype.itemsize for o in outs)
    args, outs = list(args), list(outs)
    ins, results = len(args), len(outs)

    def body(*refs):
        mine = refs[:ins] + refs[ins + len(after) : ins + len(after) + results]
        rest = refs[ins + len(after) + results :]
        if token:
            rest[0][...] = jnp.zeros(TOKEN.shape, F32)
            rest = rest[1:]
        kernel(*mine, *rest)

    return pl.pallas_call(
        body,
        in_specs=[SMEM if i < scalars else HBM if i in far else VMEM for i in range(ins)] + [VMEM] * len(after),
        out_specs=[HBM if i in far_outs else VMEM for i in range(results)] + [VMEM] * token,
        out_shape=outs + [TOKEN] * token,
        scratch_shapes=list(scratch),
        compiler_params=pltpu.CompilerParams(vmem_limit_bytes=(52 if far else 8) * 1024 * 1024),
        cost_estimate=pl.CostEstimate(flops=flops, bytes_accessed=size, transcendentals=0),
        name=name,
    )(*args, *after)


def shape(dims, dtype):
    return jax.ShapeDtypeStruct(dims, dtype)


def dot(a, b):
    return jnp.dot(a, b, preferred_element_type=F32)


def dot_t(a, b):
    return lax.dot_general(a, b, (((1,), (1,)), ((), ())), preferred_element_type=F32)


def as_row(column):
    n = column.shape[0]
    return jnp.transpose(jnp.broadcast_to(column, (n, LANE)))[:1]


def as_column(row):
    n = row.shape[1]
    return jnp.transpose(jnp.broadcast_to(row, (LANE, n)))[:, :1]


def lane_block(ref, index, rows=slice(None)):
    return ref[rows, pl.ds(pl.multiple_of(index * LANE, LANE), LANE)]


def vision_norm(vision, gain):
    def kernel(v_ref, g_ref, o_ref, s_ref):
        v = v_ref[...].astype(F32)
        scale = lax.rsqrt(jnp.mean(v * v, axis=1, keepdims=True) + 1e-06)
        s_ref[...] = scale
        o_ref[...] = (v * scale * g_ref[...]).astype(BF)

    rows = vision.shape[0]
    return call(
        kernel, "vision_norm", [shape(vision.shape, BF), shape((rows, 1), F32)], [vision, gain], token=True
    )


def pack_grads(key_grad, value_grad, after):
    rows = key_grad.shape[0]
    slots = rows // PATCH
    per = PATCH // CHUNK

    def kernel(k_ref, v_ref, stack_ref, chunk_ref):
        stack_ref[:rows] = k_ref[...]
        stack_ref[rows:] = v_ref[...]
        for s in range(slots):
            for c in range(per):
                at = pl.ds(s * PATCH + c * CHUNK, CHUNK)
                chunk_ref[c, s] = k_ref[at]
                chunk_ref[per + c, s] = v_ref[at]

    return call(
        kernel,
        "pack_grads",
        [shape((2 * rows, LANE), BF), shape((2 * per, slots, CHUNK, LANE), BF)],
        [key_grad, value_grad],
        after=after,
    )


def take_blocks(index, x):
    count = index.shape[0]

    def kernel(index_ref, x_ref, o_ref):
        for j in range(count):
            o_ref[j] = x_ref[index_ref[j]]

    return call(kernel, "take_blocks", [shape((count,) + x.shape[1:], x.dtype)], [index, x], scalars=1)[0]


def load_all(pairs, sems):
    copies = [pltpu.make_async_copy(src, dst, sems.at[i]) for i, (src, dst) in enumerate(pairs)]
    for copy in copies:
        copy.start()
    return [copy.wait for copy in copies]


def text_forward(text, gain, w_key, w_value):
    rows, width = text.shape
    blocks = w_key.shape[1] // LANE

    def kernel(t_far, g_ref, k_far, v_far, o_ref, q_ref, t_ref, k_ref, v_ref, scaled, sems):
        waits = load_all([(t_far, t_ref), (k_far, k_ref), (v_far, v_ref)], sems)
        waits[0]()

        @pl.loop(0, rows // LANE)
        def _(i):
            at = pl.ds(pl.multiple_of(i * LANE, LANE), LANE)
            t = t_ref[at].astype(F32)
            scaled[at] = (t * g_ref[...]).astype(BF)
            q_ref[pl.ds(i, 1)] = as_row(jnp.sum(t * t, axis=1, keepdims=True))

        waits[1]()
        waits[2]()

        @pl.loop(0, blocks)
        def _(b):
            w = jnp.concatenate([lane_block(k_ref, b), lane_block(v_ref, b)], axis=1)
            o_ref[b] = dot(scaled[...], w).astype(BF)

    return call(
        kernel,
        "text_forward",
        [shape((blocks, rows, 2 * LANE), BF), shape((rows // LANE, LANE), F32)],
        [text, gain, w_key, w_value],
        far=(0, 2, 3),
        scratch=[
            pltpu.VMEM(text.shape, BF),
            pltpu.VMEM(w_key.shape, BF),
            pltpu.VMEM(w_value.shape, BF),
            pltpu.VMEM((rows, width), BF),
            DMA((3,)),
        ],
        flops=4 * rows * width * w_key.shape[1],
    )


def image_forward(order, parts, w_proj, gain, w_key, w_value):
    pieces = [t for part in parts for t in part]
    starts = []
    for b, part in enumerate(parts):
        at = 0
        for t in part:
            starts.append((b, at))
            at += t.shape[0]
    rows_each = PATCH // len(parts)
    depth, width = w_proj.shape

    def kernel(order_ref, *refs):
        piece_refs = refs[: len(pieces)]
        p_far, g_ref, k_far, v_far, e_ref, far_ref, near_ref, q_ref, p_ref, k_ref, v_ref, vis, scaled, sems = refs[
            len(pieces) :
        ]
        cuts = [slice(n * 256, (n + 1) * 256) for n in range(width // 256)]
        waits = load_all(
            [(p_far.at[:, at], p_ref.at[n]) for n, at in enumerate(cuts)] + [(k_far, k_ref), (v_far, v_ref)], sems
        )
        for (b, at), ref in zip(starts, piece_refs):
            row = pl.multiple_of(order_ref[b] * rows_each + at, 16)
            vis[pl.ds(row, ref.shape[0])] = ref[...]

        for n, at in enumerate(cuts):
            waits[n]()
            e_ref[:, at] = dot(vis[...], p_ref[n]).astype(BF)

        @pl.loop(0, PATCH // LANE)
        def _(i):
            at = pl.ds(pl.multiple_of(i * LANE, LANE), LANE)
            e = e_ref[at].astype(F32)
            scaled[at] = (e * g_ref[...]).astype(BF)
            q_ref[pl.ds(i, 1)] = as_row(jnp.sum(e * e, axis=1, keepdims=True))

        waits[-2]()
        waits[-1]()

        @pl.loop(0, RING)
        def _(b):
            there = order_ref[RING + b]
            w = jnp.concatenate([lane_block(k_ref, there), lane_block(v_ref, there)], axis=1)
            far_ref[b] = dot(scaled[...], w).astype(BF)
            own = order_ref[b]
            w = jnp.concatenate([lane_block(k_ref, own), lane_block(v_ref, own)], axis=1)
            near_ref[b] = dot(scaled[...], w)

    return call(
        kernel,
        "image_forward",
        [
            shape((PATCH, width), BF),
            shape((RING, PATCH, 2 * LANE), BF),
            shape((RING, PATCH, 2 * LANE), F32),
            shape((PATCH // LANE, LANE), F32),
        ],
        [order, *pieces, w_proj, gain, w_key, w_value],
        scalars=1,
        far=(1 + len(pieces), 3 + len(pieces), 4 + len(pieces)),
        scratch=[
            pltpu.VMEM((width // 256, depth, 256), BF),
            pltpu.VMEM(w_key.shape, BF),
            pltpu.VMEM(w_value.shape, BF),
            pltpu.VMEM((PATCH, depth), BF),
            pltpu.VMEM((PATCH, width), BF),
            DMA((width // 256 + 2,)),
        ],
        flops=2 * PATCH * width * (depth + 2 * w_key.shape[1]),
    )


def backward(order, pieces, w_key, w_value, gain, embed, after):
    rows, width = embed.shape
    cols = w_key.shape[1]
    cuts = width // 256

    def kernel(order_ref, *refs):
        piece_refs = refs[: len(pieces)]
        k_far, v_far, g_ref, e_far, d_out, i_ref, k_ref, v_ref, e_ref, gk, gv, sems, d_held, out_sems = refs[len(pieces) :]
        d_ref = d_held if rows > PATCH else d_out
        outgoing = []
        pairs = []
        b = 0
        for ref in piece_refs:
            for j in range(ref.shape[0] // (2 * rows)):
                at = pl.ds(pl.multiple_of(order_ref[b] * LANE, LANE), LANE)
                pairs.append((ref.at[pl.ds(2 * rows * j, rows)], gk.at[:, at]))
                pairs.append((ref.at[pl.ds(2 * rows * j + rows, rows)], gv.at[:, at]))
                b += 1
        for n in range(cuts):
            at = pl.ds(n * 256, 256)
            pairs += [(k_far.at[at], k_ref.at[at]), (v_far.at[at], v_ref.at[at])]
        pairs.append((e_far, e_ref))
        waits = load_all(pairs, sems)
        for wait in waits[:16]:
            wait()
        for n in range(cuts):
            at = slice(n * 256, (n + 1) * 256)
            waits[16 + 2 * n]()
            waits[17 + 2 * n]()
            d = dot_t(gk[...], k_ref[at]) + dot_t(gv[...], v_ref[at])
            d_ref[:, at] = d * g_ref[:, at]
            if rows > PATCH:
                outgoing.append(pltpu.make_async_copy(d_ref.at[:, at], d_out.at[:, at], out_sems.at[n]))
                outgoing[-1].start()
        waits[-1]()

        @pl.loop(0, rows // LANE)
        def _(i):
            at = pl.ds(pl.multiple_of(i * LANE, LANE), LANE)
            i_ref[pl.ds(i, 1)] = as_row(jnp.sum(d_ref[at] * e_ref[at].astype(F32), axis=1, keepdims=True))

        for copy in outgoing:
            copy.wait()

    n = len(pieces)
    return call(
        kernel,
        "backward",
        [shape((rows, width), F32), shape((rows // LANE, LANE), F32)],
        [order, *pieces, w_key, w_value, gain, embed],
        scalars=1,
        far=tuple(range(1, n + 3)) + (n + 4,),
        scratch=[
            pltpu.VMEM(w_key.shape, BF),
            pltpu.VMEM(w_value.shape, BF),
            pltpu.VMEM(embed.shape, BF),
            pltpu.VMEM((rows, cols), BF),
            pltpu.VMEM((rows, cols), BF),
            DMA((17 + 2 * cuts,)),
            pltpu.VMEM(embed.shape if rows > PATCH else (8, LANE), F32),
            DMA((cuts,)),
        ],
        flops=4 * rows * width * cols,
        after=after,
        far_outs=(0,) if rows > PATCH else (),
        token=True,
    )


def embed_grad(d, e, square_row, inner_row):
    scale = lax.rsqrt(as_column(square_row) / D + 1e-05)
    inner = as_column(inner_row) / D
    return scale * d - e * (scale * scale * scale * inner)


def image_backward(order, image_d, embed, square, inner, w_proj, after):
    depth, width = w_proj.shape
    rows_each = PATCH // 8
    half = PATCH // 2
    cut = 640

    def kernel(order_ref, d_ref, e_ref, q_ref, i_ref, p_far, far_ref, near_ref, p_ref, grad, turned, sems):
        cuts = [slice(n * cut, (n + 1) * cut) for n in range(depth // cut)]
        waits = load_all([(p_far.at[at], p_ref.at[at]) for at in cuts], sems)

        @pl.loop(0, PATCH // LANE)
        def _(i):
            at = pl.ds(pl.multiple_of(i * LANE, LANE), LANE)
            row = pl.ds(i, 1)
            grad[at] = embed_grad(d_ref[at], e_ref[at].astype(F32), q_ref[row], i_ref[row]).astype(BF)

        for b in range(8):
            at = pl.ds(pl.multiple_of(order_ref[b] * rows_each, rows_each), rows_each)
            turned[b * rows_each : (b + 1) * rows_each] = grad[at]

        for n, at in enumerate(cuts):
            waits[n]()
            r = dot_t(turned[...], p_ref[at])
            near_ref[:, at] = r[:half]
            far_ref[:, at] = r[half:].astype(BF)

    return call(
        kernel,
        "image_backward",
        [shape((half, depth), BF), shape((half, depth), F32)],
        [order, image_d, embed, square, inner, w_proj],
        scalars=1,
        far=(5,),
        scratch=[
            pltpu.VMEM(w_proj.shape, BF),
            pltpu.VMEM((PATCH, width), BF),
            pltpu.VMEM((PATCH, width), BF),
            DMA((depth // cut,)),
        ],
        flops=2 * PATCH * width * depth,
        after=after,
        token=True,
    )


def ring_first(near, other, after):
    _, n, c = near.shape
    h = n // 2

    def kernel(a_ref, b_ref, up_ref, down_ref, here_ref, above_ref, below_ref):
        def total(k, at):
            return a_ref[k, at] + b_ref[k, at].astype(F32)

        first, second = slice(0, h), slice(h, n)
        up_ref[first] = total(2, first).astype(BF)
        up_ref[second] = total(1, second).astype(BF)
        down_ref[first] = total(3, first).astype(BF)
        down_ref[second] = total(2, second).astype(BF)
        here_ref[...] = total(0, slice(0, n))
        above_ref[...] = total(1, first)
        below_ref[...] = total(3, second)

    return call(
        kernel,
        "ring_first",
        [shape((n, c), BF), shape((n, c), BF), shape((n, c), F32), shape((h, c), F32), shape((h, c), F32)],
        [near, other],
        after=after,
        token=True,
    )


def ring_sum(near, far, after=()):
    up1, down1, here, above, below, token = ring_first(near, peer(far).reshape(near.shape), after)
    h = above.shape[0]
    up1, down1 = up(up1), down(down1)
    up2 = up((above + up1[:h].astype(F32)).astype(BF))
    down2 = down((below + down1[h:].astype(F32)).astype(BF))
    return (here, up1, down1, up2, down2), token


def ring_total(here_ref, up1_ref, down1_ref, up2_ref, down2_ref):
    h = up2_ref.shape[0]
    first = here_ref[:h] + down1_ref[:h].astype(F32) + up2_ref[...].astype(F32)
    second = here_ref[h:] + up1_ref[h:].astype(F32) + down2_ref[...].astype(F32)
    return first, second


def image_out(pieces, square, after):
    h = PATCH // 2

    def kernel(*refs):
        q_ref, o_ref = refs[5:7]
        for j, t in enumerate(ring_total(*refs[:5])):
            scale = lax.rsqrt(as_column(q_ref[j : j + 1]) / D + 1e-05)
            t = (t * scale).astype(BF)
            o_ref[j * h : (j + 1) * h] = t[:, :LANE]
            o_ref[PATCH + j * h : PATCH + (j + 1) * h] = t[:, LANE:]

    return call(kernel, "image_out", [shape((2 * PATCH, LANE), BF)], [*pieces, square], after=after, token=True)


def vision_out(pieces, vision, gain, scale):
    rows = vision.shape[0]
    h = rows // 2

    def kernel(*refs):
        v_ref, g_ref, s_ref, o_ref = refs[5:]
        for j, t in enumerate(ring_total(*refs[:5])):
            at = slice(j * h, (j + 1) * h)
            v, s = v_ref[at].astype(F32), s_ref[at]
            grad_h = t.astype(BF).astype(F32) * g_ref[...]
            inner = jnp.mean(grad_h * v, axis=1, keepdims=True)
            o_ref[at] = (s * grad_h - v * (s * s * s * inner)).astype(BF)

    return call(kernel, "vision_out", [shape(vision.shape, BF)], [*pieces, vision, gain, scale])[0]


def text_out(filled, text_d, text, square, inner, after):
    rows, width = text.shape
    parts = rows // LANE

    def kernel(f_ref, d_far, t_far, q_ref, i_ref, o_far, d_ref, t_ref, o_ref, sems, out_sems):
        cuts = [pl.ds(i * LANE, LANE) for i in range(parts)]
        waits = load_all([(d_far.at[at], d_ref.at[at]) for at in cuts] + [(t_far.at[at], t_ref.at[at]) for at in cuts], sems)
        outgoing = []
        for i, at in enumerate(cuts):
            waits[i]()
            waits[parts + i]()
            row = pl.ds(i, 1)
            grad = embed_grad(d_ref[at], t_ref[at].astype(F32), q_ref[row], i_ref[row])
            o_ref[at] = jnp.where(f_ref[i // (PATCH // LANE)] > 0, 0.0, grad).astype(BF)
            outgoing.append(pltpu.make_async_copy(o_ref.at[at], o_far.at[at], out_sems.at[i]))
            outgoing[-1].start()
        for copy in outgoing:
            copy.wait()

    return call(
        kernel,
        "text_out",
        [shape((rows, width), BF)],
        [filled, text_d, text, square, inner],
        scalars=1,
        far=(1, 2),
        far_outs=(0,),
        scratch=[
            pltpu.VMEM(text.shape, F32),
            pltpu.VMEM(text.shape, BF),
            pltpu.VMEM(text.shape, BF),
            DMA((2 * parts,)),
            DMA((parts,)),
        ],
        after=after,
    )[0]


def key_value_out(filled, text_kv, square, arrived):
    rows = text_kv.shape[0]
    per = PATCH // CHUNK

    def kernel(f_ref, t_ref, q_ref, a_ref, k_ref, v_ref):
        for s in range(rows // PATCH):
            @pl.when(f_ref[s] > 0)
            def _():
                for c in range(per):
                    at = pl.ds(s * PATCH + c * CHUNK, CHUNK)
                    k_ref[at] = a_ref[c, s]
                    v_ref[at] = a_ref[per + c, s]

            @pl.when(f_ref[s] == 0)
            def _():
                for i in range(PATCH // LANE):
                    j = s * (PATCH // LANE) + i
                    at = pl.ds(j * LANE, LANE)
                    scale = lax.rsqrt(as_column(q_ref[j : j + 1]) / D + 1e-05)
                    t = (t_ref[at].astype(F32) * scale).astype(BF)
                    k_ref[at] = t[:, :LANE]
                    v_ref[at] = t[:, LANE:]

    return call(
        kernel,
        "key_value_out",
        [shape((rows, LANE), BF), shape((rows, LANE), BF)],
        [filled, text_kv, square, arrived],
        scalars=1,
    )


def ring_gather(x):
    half = x.shape[0] // 2
    below, above = up(x), down(x)
    far = [up(below[:half]), down(above[half:])]
    mine = [[x], [above], far, [below]]
    other = [[peer(t) for t in part] for part in mine]
    return mine + other


def short_gather(x):
    mine = [x, down(x), across(x), up(x)]
    return mine + [peer(t) for t in mine]


def small_sum(x):
    pair = x + peer(x)
    return (pair + up(pair)) + (down(pair) + across(pair))


def shards(
    vision,
    vision_gain,
    image_slot,
    text_embed,
    w_proj,
    llm_gain,
    w_key,
    w_value,
    key_grad,
    value_grad,
):
    dp = lax.axis_size("dp")
    here = lax.axis_index("dp")
    m = lax.axis_index("mp")
    y, c = m // 2, m % 2
    slots = text_embed.shape[0] // PATCH
    text_rows = text_embed.shape[0] // LANE

    rel = jnp.arange(8, dtype=jnp.int32)
    order = ((y + rel % RING) % RING) * 2 + (c ^ (rel // RING))
    slot_ids = jnp.arange(dp * slots, dtype=jnp.int32)
    onehot = slot_ids[:, None] == image_slot[None, :]
    owner = jnp.sum(jnp.where(onehot, jnp.arange(dp, dtype=jnp.int32)[None, :], 0), axis=1)
    mine = slot_ids[:slots] + here * slots
    filled = jnp.any(mine[:, None] == image_slot[None, :], axis=1).astype(jnp.int32)
    gain = llm_gain[None]
    vis_gain = vision_gain[None]

    vis_normed, vis_scale, norm_done = vision_norm(vision, vis_gain)
    with jax.named_scope("vision_gather"):
        vis_parts = ring_gather(vis_normed)

    grad_stack, grad_chunks = pack_grads(key_grad, value_grad, [norm_done])
    with jax.named_scope("text_grad_gather"):
        text_g = lax.all_gather(grad_stack, "mp", axis=0, tiled=True)
    with jax.named_scope("slot_grads_spread"):
        spread = lax.all_to_all(grad_chunks, "dp", split_axis=0, concat_axis=0, tiled=True)
    picked = take_blocks(image_slot, spread.reshape(dp * slots, CHUNK, LANE))
    with jax.named_scope("slot_grads_collect"):
        image_kv_grad = lax.all_to_all(picked, "dp", split_axis=0, concat_axis=0, tiled=True)
    with jax.named_scope("image_grad_gather"):
        image_g = short_gather(image_kv_grad.reshape(2 * PATCH, LANE))

    text_part, text_square = text_forward(text_embed, gain, w_key, w_value)
    with jax.named_scope("text_key_value_sum"):
        text_kv = lax.psum_scatter(text_part, "mp", scatter_dimension=0, tiled=False)

    embed, far, near, image_square = image_forward(order, vis_parts, w_proj, gain, w_key, w_value)
    with jax.named_scope("image_key_value_sum"):
        pieces, kv_ring = ring_sum(near, far)
    with jax.named_scope("squares_sum"):
        squares = small_sum(jnp.concatenate([text_square, image_square]))
    text_square, image_square = squares[:text_rows], squares[text_rows:]

    image_kv, kv_out = image_out(pieces, image_square, ())
    image_kv = image_kv.reshape(dp, CHUNK, LANE)
    with jax.named_scope("image_out_spread"):
        spread = lax.all_to_all(image_kv, "dp", split_axis=0, concat_axis=0, tiled=True)
    packed = take_blocks(owner, spread).reshape(dp, slots, CHUNK, LANE)
    with jax.named_scope("image_out_collect"):
        arrived = lax.all_to_all(packed, "dp", split_axis=0, concat_axis=0, tiled=True)

    text_d, text_inner, _ = backward(rel, [text_g], w_key, w_value, gain, text_embed, [kv_ring])
    image_d, image_inner, _ = backward(order, image_g, w_key, w_value, gain, embed, [kv_ring])
    with jax.named_scope("inner_sum"):
        inner = small_sum(jnp.concatenate([text_inner, image_inner]))
    d_far, d_near, back_done = image_backward(
        order, image_d, embed, image_square, inner[text_rows:], w_proj, [kv_out]
    )
    with jax.named_scope("d_vis_sum"):
        d_pieces, d_ring = ring_sum(d_near.reshape(RING, -1, DV), d_far)
    vision_grad = vision_out(d_pieces, vision, vis_gain, vis_scale)
    text_grad = text_out(filled, text_d, text_embed, text_square, inner[:text_rows], [d_ring])
    key_out, value_out = key_value_out(filled, text_kv, text_square, arrived)
    return key_out, value_out, text_grad, vision_grad


def solution(mesh):
    placed = (
        P(("dp", "mp"), None),
        P(),
        P(),
        P("dp", "mp"),
        P(None, "mp"),
        P("mp"),
        P("mp", None),
        P("mp", None),
        P("dp", "mp"),
        P("dp", "mp"),
    )
    return jax.shard_map(
        shards,
        mesh=mesh,
        in_specs=placed,
        out_specs=(P("dp", "mp"), P("dp", "mp"), P("dp", "mp"), P(("dp", "mp"), None)),
        check_vma=False,
    )
```

```python
import jax
import jax.numpy as jnp
from jax import lax
from jax.experimental import pallas as pl
from jax.experimental.pallas import tpu as pltpu
from jax.sharding import PartitionSpec as P

D = 8192
DV = 3200
PATCH = 256
LANE = 128
CHUNK = 16
BF = jnp.bfloat16
F32 = jnp.float32
VMEM = pl.BlockSpec(memory_space=pltpu.VMEM)
SMEM = pl.BlockSpec(memory_space=pltpu.SMEM)
HBM = pl.BlockSpec(memory_space=pltpu.HBM)
ANY = pl.BlockSpec(memory_space=pl.ANY)
DMA = pltpu.SemaphoreType.DMA

RING = 4
UP = [(2 * y + c, 2 * ((y + 1) % RING) + c) for y in range(RING) for c in range(2)]
DOWN = [(2 * y + c, 2 * ((y + 3) % RING) + c) for y in range(RING) for c in range(2)]
ACROSS = [(2 * y + c, 2 * ((y + 2) % RING) + c) for y in range(RING) for c in range(2)]
PEER = [(2 * y + c, 2 * y + 1 - c) for y in range(RING) for c in range(2)]


def up(x):
    return lax.ppermute(x, "mp", UP)


def down(x):
    return lax.ppermute(x, "mp", DOWN)


def across(x):
    return lax.ppermute(x, "mp", ACROSS)


def peer(x):
    return lax.ppermute(x, "mp", PEER)


TOKEN = jax.ShapeDtypeStruct((8, LANE), F32)


def call(kernel, name, outs, args, scalars=0, far=(), far_outs=(), scratch=(), flops=0, after=(), token=False):
    size = sum(a.size * a.dtype.itemsize for a in args) + sum(o.size * o.dtype.itemsize for o in outs)
    args, outs = list(args), list(outs)
    ins, results = len(args), len(outs)

    def body(*refs):
        mine = refs[:ins] + refs[ins + len(after) : ins + len(after) + results]
        rest = refs[ins + len(after) + results :]
        if token:
            rest[0][...] = jnp.zeros(TOKEN.shape, F32)
            rest = rest[1:]
        kernel(*mine, *rest)

    return pl.pallas_call(
        body,
        in_specs=[SMEM if i < scalars else HBM if i in far else VMEM for i in range(ins)] + [ANY] * len(after),
        out_specs=[HBM if i in far_outs else VMEM for i in range(results)] + [VMEM] * token,
        out_shape=outs + [TOKEN] * token,
        scratch_shapes=list(scratch),
        compiler_params=pltpu.CompilerParams(vmem_limit_bytes=(52 if far else 8) * 1024 * 1024),
        cost_estimate=pl.CostEstimate(flops=flops, bytes_accessed=size, transcendentals=0),
        name=name,
    )(*args, *after)


def shape(dims, dtype):
    return jax.ShapeDtypeStruct(dims, dtype)


def dot(a, b):
    return jnp.dot(a, b, preferred_element_type=F32)


def dot_t(a, b):
    return lax.dot_general(a, b, (((1,), (1,)), ((), ())), preferred_element_type=F32)


def as_row(column):
    n = column.shape[0]
    return jnp.transpose(jnp.broadcast_to(column, (n, LANE)))[:1]


def as_column(row):
    n = row.shape[1]
    return jnp.transpose(jnp.broadcast_to(row, (LANE, n)))[:, :1]


def lane_block(ref, index, rows=slice(None)):
    return ref[rows, pl.ds(pl.multiple_of(index * LANE, LANE), LANE)]


def vision_norm(vision, gain):
    def kernel(v_ref, g_ref, o_ref, s_ref):
        v = v_ref[...].astype(F32)
        scale = lax.rsqrt(jnp.mean(v * v, axis=1, keepdims=True) + 1e-06)
        s_ref[...] = scale
        o_ref[...] = (v * scale * g_ref[...]).astype(BF)

    rows = vision.shape[0]
    return call(
        kernel, "vision_norm", [shape(vision.shape, BF), shape((rows, 1), F32)], [vision, gain], token=True
    )


def pack_grads(key_grad, value_grad, after):
    rows = key_grad.shape[0]
    slots = rows // PATCH
    per = PATCH // CHUNK
    grads = [g.reshape(slots, per, CHUNK, LANE) for g in (key_grad, value_grad)]

    def kernel(k_ref, v_ref, stack_ref, chunk_ref, sems):
        pairs = []
        for j, ref in enumerate((k_ref, v_ref)):
            for s in range(slots):
                pairs.append((ref.at[s], chunk_ref.at[pl.ds(j * per, per), s]))
            pairs.append((ref, stack_ref.at[j]))
        for wait in load_all(pairs, sems):
            wait()

    stack, chunks, token = call(
        kernel,
        "pack_grads",
        [shape((2, slots, per, CHUNK, LANE), BF), shape((2 * per, slots, CHUNK, LANE), BF)],
        grads,
        far=(0, 1),
        far_outs=(0, 1),
        scratch=[DMA((2 * slots + 2,))],
        after=after,
        token=True,
    )
    return stack.reshape(2 * rows, LANE), chunks, token


def take_blocks(index, x, after):
    count = index.shape[0]

    def kernel(index_ref, x_ref, o_ref):
        for j in range(count):
            o_ref[j] = x_ref[index_ref[j]]

    return call(kernel, "take_blocks", [shape((count,) + x.shape[1:], x.dtype)], [index, x], scalars=1, after=after, token=True)


def load_all(pairs, sems):
    copies = [pltpu.make_async_copy(src, dst, sems.at[i]) for i, (src, dst) in enumerate(pairs)]
    for copy in copies:
        copy.start()
    return [copy.wait for copy in copies]


def text_forward(order, text, gain, w_key, w_value, after):
    rows, width = text.shape

    def kernel(order_ref, t_far, g_ref, k_far, v_far, far_ref, near_ref, q_ref, t_ref, k_ref, v_ref, scaled, sems):
        waits = load_all([(t_far, t_ref), (k_far, k_ref), (v_far, v_ref)], sems)
        waits[0]()

        @pl.loop(0, rows // LANE)
        def _(i):
            at = pl.ds(pl.multiple_of(i * LANE, LANE), LANE)
            t = t_ref[at].astype(F32)
            scaled[at] = (t * g_ref[...]).astype(BF)
            q_ref[pl.ds(i, 1)] = as_row(jnp.sum(t * t, axis=1, keepdims=True))

        waits[1]()
        waits[2]()

        @pl.loop(0, RING)
        def _(b):
            there = order_ref[RING + b]
            w = jnp.concatenate([lane_block(k_ref, there), lane_block(v_ref, there)], axis=1)
            far_ref[b] = dot(scaled[...], w).astype(BF)
            own = order_ref[b]
            w = jnp.concatenate([lane_block(k_ref, own), lane_block(v_ref, own)], axis=1)
            near_ref[b] = dot(scaled[...], w)

    return call(
        kernel,
        "text_forward",
        [
            shape((RING, rows, 2 * LANE), BF),
            shape((RING, rows, 2 * LANE), F32),
            shape((rows // LANE, LANE), F32),
        ],
        [order, text, gain, w_key, w_value],
        scalars=1,
        far=(1, 3, 4),
        after=after,
        token=True,
        scratch=[
            pltpu.VMEM(text.shape, BF),
            pltpu.VMEM(w_key.shape, BF),
            pltpu.VMEM(w_value.shape, BF),
            pltpu.VMEM((rows, width), BF),
            DMA((3,)),
        ],
        flops=4 * rows * width * w_key.shape[1],
    )


def image_forward(order, parts, w_proj, gain, w_key, w_value, after):
    pieces = [t for part in parts for t in part]
    starts = []
    for b, part in enumerate(parts):
        at = 0
        for t in part:
            starts.append((b, at))
            at += t.shape[0]
    rows_each = PATCH // len(parts)
    depth, width = w_proj.shape

    def kernel(order_ref, *refs):
        piece_refs = refs[: len(pieces)]
        p_far, g_ref, k_far, v_far, e_ref, far_ref, near_ref, q_ref, p_ref, k_ref, v_ref, vis, scaled, sems = refs[
            len(pieces) :
        ]
        cuts = [slice(n * 256, (n + 1) * 256) for n in range(width // 256)]
        waits = load_all(
            [(p_far.at[:, at], p_ref.at[n]) for n, at in enumerate(cuts)] + [(k_far, k_ref), (v_far, v_ref)], sems
        )
        for (b, at), ref in zip(starts, piece_refs):
            row = pl.multiple_of(order_ref[b] * rows_each + at, 16)
            vis[pl.ds(row, ref.shape[0])] = ref[...]

        for n, at in enumerate(cuts):
            waits[n]()
            e_ref[:, at] = dot(vis[...], p_ref[n]).astype(BF)

        @pl.loop(0, PATCH // LANE)
        def _(i):
            at = pl.ds(pl.multiple_of(i * LANE, LANE), LANE)
            e = e_ref[at].astype(F32)
            scaled[at] = (e * g_ref[...]).astype(BF)
            q_ref[pl.ds(i, 1)] = as_row(jnp.sum(e * e, axis=1, keepdims=True))

        waits[-2]()
        waits[-1]()

        @pl.loop(0, RING)
        def _(b):
            there = order_ref[RING + b]
            w = jnp.concatenate([lane_block(k_ref, there), lane_block(v_ref, there)], axis=1)
            far_ref[b] = dot(scaled[...], w).astype(BF)
            own = order_ref[b]
            w = jnp.concatenate([lane_block(k_ref, own), lane_block(v_ref, own)], axis=1)
            near_ref[b] = dot(scaled[...], w)

    return call(
        kernel,
        "image_forward",
        [
            shape((PATCH, width), BF),
            shape((RING, PATCH, 2 * LANE), BF),
            shape((RING, PATCH, 2 * LANE), F32),
            shape((PATCH // LANE, LANE), F32),
        ],
        [order, *pieces, w_proj, gain, w_key, w_value],
        scalars=1,
        far=(1 + len(pieces), 3 + len(pieces), 4 + len(pieces)),
        scratch=[
            pltpu.VMEM((width // 256, depth, 256), BF),
            pltpu.VMEM(w_key.shape, BF),
            pltpu.VMEM(w_value.shape, BF),
            pltpu.VMEM((PATCH, depth), BF),
            pltpu.VMEM((PATCH, width), BF),
            DMA((width // 256 + 2,)),
        ],
        flops=2 * PATCH * width * (depth + 2 * w_key.shape[1]),
        after=after,
    )


def backward(order, pieces, w_key, w_value, gain, embed, after):
    rows, width = embed.shape
    cols = w_key.shape[1]
    cuts = width // 256

    def kernel(order_ref, *refs):
        piece_refs = refs[: len(pieces)]
        k_far, v_far, g_ref, e_far, d_out, i_ref, k_ref, v_ref, e_ref, gk, gv, sems, d_held, out_sems = refs[len(pieces) :]
        d_ref = d_held if rows > PATCH else d_out
        outgoing = []
        pairs = []
        b = 0
        for ref in piece_refs:
            for j in range(ref.shape[0] // (2 * rows)):
                at = pl.ds(pl.multiple_of(order_ref[b] * LANE, LANE), LANE)
                pairs.append((ref.at[pl.ds(2 * rows * j, rows)], gk.at[:, at]))
                pairs.append((ref.at[pl.ds(2 * rows * j + rows, rows)], gv.at[:, at]))
                b += 1
        for n in range(cuts):
            at = pl.ds(n * 256, 256)
            pairs += [(k_far.at[at], k_ref.at[at]), (v_far.at[at], v_ref.at[at])]
        pairs.append((e_far, e_ref))
        waits = load_all(pairs, sems)
        for wait in waits[:16]:
            wait()
        for n in range(cuts):
            at = slice(n * 256, (n + 1) * 256)
            waits[16 + 2 * n]()
            waits[17 + 2 * n]()
            d = dot_t(gk[...], k_ref[at]) + dot_t(gv[...], v_ref[at])
            d_ref[:, at] = d * g_ref[:, at]
            if rows > PATCH:
                outgoing.append(pltpu.make_async_copy(d_ref.at[:, at], d_out.at[:, at], out_sems.at[n]))
                outgoing[-1].start()
        waits[-1]()

        @pl.loop(0, rows // LANE)
        def _(i):
            at = pl.ds(pl.multiple_of(i * LANE, LANE), LANE)
            i_ref[pl.ds(i, 1)] = as_row(jnp.sum(d_ref[at] * e_ref[at].astype(F32), axis=1, keepdims=True))

        for copy in outgoing:
            copy.wait()

    n = len(pieces)
    return call(
        kernel,
        "backward",
        [shape((rows, width), F32), shape((rows // LANE, LANE), F32)],
        [order, *pieces, w_key, w_value, gain, embed],
        scalars=1,
        far=tuple(range(1, n + 3)) + (n + 4,),
        scratch=[
            pltpu.VMEM(w_key.shape, BF),
            pltpu.VMEM(w_value.shape, BF),
            pltpu.VMEM(embed.shape, BF),
            pltpu.VMEM((rows, cols), BF),
            pltpu.VMEM((rows, cols), BF),
            DMA((17 + 2 * cuts,)),
            pltpu.VMEM(embed.shape if rows > PATCH else (8, LANE), F32),
            DMA((cuts,)),
        ],
        flops=4 * rows * width * cols,
        after=after,
        far_outs=(0,) if rows > PATCH else (),
        token=True,
    )


def embed_grad(d, e, square_row, inner_row):
    scale = lax.rsqrt(as_column(square_row) / D + 1e-05)
    inner = as_column(inner_row) / D
    return scale * d - e * (scale * scale * scale * inner)


def image_backward(order, image_d, embed, square, inner, w_proj, after):
    depth, width = w_proj.shape
    rows_each = PATCH // 8
    half = PATCH // 2
    cut = 640

    def kernel(order_ref, d_ref, e_ref, q_ref, i_ref, p_far, far_ref, near_ref, p_ref, grad, turned, sems):
        cuts = [slice(n * cut, (n + 1) * cut) for n in range(depth // cut)]
        waits = load_all([(p_far.at[at], p_ref.at[at]) for at in cuts], sems)

        @pl.loop(0, PATCH // LANE)
        def _(i):
            at = pl.ds(pl.multiple_of(i * LANE, LANE), LANE)
            row = pl.ds(i, 1)
            grad[at] = embed_grad(d_ref[at], e_ref[at].astype(F32), q_ref[row], i_ref[row]).astype(BF)

        for b in range(8):
            at = pl.ds(pl.multiple_of(order_ref[b] * rows_each, rows_each), rows_each)
            turned[b * rows_each : (b + 1) * rows_each] = grad[at]

        for n, at in enumerate(cuts):
            waits[n]()
            r = dot_t(turned[...], p_ref[at])
            near_ref[:, at] = r[:half]
            far_ref[:, at] = r[half:].astype(BF)

    return call(
        kernel,
        "image_backward",
        [shape((half, depth), BF), shape((half, depth), F32)],
        [order, image_d, embed, square, inner, w_proj],
        scalars=1,
        far=(5,),
        scratch=[
            pltpu.VMEM(w_proj.shape, BF),
            pltpu.VMEM((PATCH, width), BF),
            pltpu.VMEM((PATCH, width), BF),
            DMA((depth // cut,)),
        ],
        flops=2 * PATCH * width * depth,
        after=after,
        token=True,
    )


def ring_first(near, other, after):
    _, n, c = near.shape
    h = n // 2

    def kernel(a_ref, b_ref, up_ref, down_ref, here_ref, above_ref, below_ref):
        def total(k, at):
            return a_ref[k, at] + b_ref[k, at].astype(F32)

        first, second = slice(0, h), slice(h, n)
        up_ref[first] = total(2, first).astype(BF)
        up_ref[second] = total(1, second).astype(BF)
        down_ref[first] = total(3, first).astype(BF)
        down_ref[second] = total(2, second).astype(BF)
        here_ref[...] = total(0, slice(0, n))
        above_ref[...] = total(1, first)
        below_ref[...] = total(3, second)

    return call(
        kernel,
        "ring_first",
        [shape((n, c), BF), shape((n, c), BF), shape((n, c), F32), shape((h, c), F32), shape((h, c), F32)],
        [near, other],
        after=after,
        token=True,
    )


def ring_sum(near, far, after=()):
    up1, down1, here, above, below, token = ring_first(near, peer(far).reshape(near.shape), after)
    h = above.shape[0]
    up1, down1 = up(up1), down(down1)
    up2 = up((above + up1[:h].astype(F32)).astype(BF))
    down2 = down((below + down1[h:].astype(F32)).astype(BF))
    return (here, up1, down1, up2, down2), token


def ring_total(here_ref, up1_ref, down1_ref, up2_ref, down2_ref):
    h = up2_ref.shape[0]
    first = here_ref[:h] + down1_ref[:h].astype(F32) + up2_ref[...].astype(F32)
    second = here_ref[h:] + up1_ref[h:].astype(F32) + down2_ref[...].astype(F32)
    return first, second


def image_out(pieces, square, after):
    h = PATCH // 2

    def kernel(*refs):
        q_ref, o_ref = refs[5:7]
        for j, t in enumerate(ring_total(*refs[:5])):
            scale = lax.rsqrt(as_column(q_ref[j : j + 1]) / D + 1e-05)
            t = (t * scale).astype(BF)
            o_ref[j * h : (j + 1) * h] = t[:, :LANE]
            o_ref[PATCH + j * h : PATCH + (j + 1) * h] = t[:, LANE:]

    return call(kernel, "image_out", [shape((2 * PATCH, LANE), BF)], [*pieces, square], after=after, token=True)


def vision_out(pieces, vision, gain, scale):
    rows = vision.shape[0]
    h = rows // 2

    def kernel(*refs):
        v_ref, g_ref, s_ref, o_ref = refs[5:]
        for j, t in enumerate(ring_total(*refs[:5])):
            at = slice(j * h, (j + 1) * h)
            v, s = v_ref[at].astype(F32), s_ref[at]
            grad_h = t.astype(BF).astype(F32) * g_ref[...]
            inner = jnp.mean(grad_h * v, axis=1, keepdims=True)
            o_ref[at] = (s * grad_h - v * (s * s * s * inner)).astype(BF)

    return call(kernel, "vision_out", [shape(vision.shape, BF)], [*pieces, vision, gain, scale])[0]


def text_out(filled, text_d, text, square, inner, after):
    rows, width = text.shape
    parts = rows // LANE

    def kernel(f_ref, d_far, t_far, q_ref, i_ref, o_far, d_ref, t_ref, o_ref, sems, out_sems):
        cuts = [pl.ds(i * LANE, LANE) for i in range(parts)]
        waits = load_all([(d_far.at[at], d_ref.at[at]) for at in cuts] + [(t_far.at[at], t_ref.at[at]) for at in cuts], sems)
        outgoing = []
        for i, at in enumerate(cuts):
            waits[i]()
            waits[parts + i]()
            row = pl.ds(i, 1)
            grad = embed_grad(d_ref[at], t_ref[at].astype(F32), q_ref[row], i_ref[row])
            o_ref[at] = jnp.where(f_ref[i // (PATCH // LANE)] > 0, 0.0, grad).astype(BF)
            outgoing.append(pltpu.make_async_copy(o_ref.at[at], o_far.at[at], out_sems.at[i]))
            outgoing[-1].start()
        for copy in outgoing:
            copy.wait()

    return call(
        kernel,
        "text_out",
        [shape((rows, width), BF)],
        [filled, text_d, text, square, inner],
        scalars=1,
        far=(1, 2),
        far_outs=(0,),
        scratch=[
            pltpu.VMEM(text.shape, F32),
            pltpu.VMEM(text.shape, BF),
            pltpu.VMEM(text.shape, BF),
            DMA((2 * parts,)),
            DMA((parts,)),
        ],
        after=after,
        token=True,
    )


def key_value_out(filled, pieces, square, arrived):
    rows = pieces[0].shape[0]
    half = rows // 2
    per = PATCH // CHUNK

    def kernel(f_ref, *refs):
        q_ref, a_ref, k_ref, v_ref = refs[5:9]
        totals = ring_total(*refs[:5])
        for s in range(rows // PATCH):
            @pl.when(f_ref[s] > 0)
            def _():
                for c in range(per):
                    at = pl.ds(s * PATCH + c * CHUNK, CHUNK)
                    k_ref[at] = a_ref[c, s]
                    v_ref[at] = a_ref[per + c, s]

            @pl.when(f_ref[s] == 0)
            def _():
                for i in range(PATCH // LANE):
                    j = s * (PATCH // LANE) + i
                    at = slice(j * LANE, (j + 1) * LANE)
                    scale = lax.rsqrt(as_column(q_ref[j : j + 1]) / D + 1e-05)
                    t = totals[at.start // half][at.start % half : at.start % half + LANE]
                    t = (t * scale).astype(BF)
                    k_ref[at] = t[:, :LANE]
                    v_ref[at] = t[:, LANE:]

    return call(
        kernel,
        "key_value_out",
        [shape((rows, LANE), BF), shape((rows, LANE), BF)],
        [filled, *pieces, square, arrived],
        scalars=1,
    )


def ring_gather(x):
    half = x.shape[0] // 2
    below, above = up(x), down(x)
    far = [up(below[:half]), down(above[half:])]
    mine = [[x], [above], far, [below]]
    other = [[peer(t) for t in part] for part in mine]
    return mine + other


def short_gather(x):
    mine = [x, down(x), across(x), up(x)]
    return mine + [peer(t) for t in mine]


def small_sum(x):
    pair = x + peer(x)
    return (pair + up(pair)) + (down(pair) + across(pair))


def shards(
    vision,
    vision_gain,
    image_slot,
    text_embed,
    w_proj,
    llm_gain,
    w_key,
    w_value,
    key_grad,
    value_grad,
):
    dp = lax.axis_size("dp")
    here = lax.axis_index("dp")
    m = lax.axis_index("mp")
    y, c = m // 2, m % 2
    slots = text_embed.shape[0] // PATCH
    text_rows = text_embed.shape[0] // LANE

    rel = jnp.arange(8, dtype=jnp.int32)
    order = ((y + rel % RING) % RING) * 2 + (c ^ (rel // RING))
    slot_ids = jnp.arange(dp * slots, dtype=jnp.int32)
    onehot = slot_ids[:, None] == image_slot[None, :]
    owner = jnp.sum(jnp.where(onehot, jnp.arange(dp, dtype=jnp.int32)[None, :], 0), axis=1)
    mine = slot_ids[:slots] + here * slots
    filled = jnp.any(mine[:, None] == image_slot[None, :], axis=1).astype(jnp.int32)
    gain = llm_gain[None]
    vis_gain = vision_gain[None]

    vis_normed, vis_scale, norm_done = vision_norm(vision, vis_gain)
    with jax.named_scope("vision_gather"):
        vis_parts = ring_gather(vis_normed)

    grad_stack, grad_chunks, packed_done = pack_grads(key_grad, value_grad, [norm_done])
    with jax.named_scope("slot_grads_spread"):
        spread = lax.all_to_all(grad_chunks, "dp", split_axis=0, concat_axis=0, tiled=True)
    with jax.named_scope("text_grad_gather"):
        text_g = short_gather(grad_stack)
    picked, picked_done = take_blocks(image_slot, spread.reshape(dp * slots, CHUNK, LANE), [packed_done])
    text_far, text_near, text_square, text_done = text_forward(
        order, text_embed, gain, w_key, w_value, [picked_done]
    )
    with jax.named_scope("slot_grads_collect"):
        image_kv_grad = lax.all_to_all(picked, "dp", split_axis=0, concat_axis=0, tiled=True)
    with jax.named_scope("text_key_value_sum"):
        text_pieces, text_ring = ring_sum(text_near, text_far)
    with jax.named_scope("image_grad_gather"):
        image_g = short_gather(image_kv_grad.reshape(2 * PATCH, LANE))

    embed, far, near, image_square = image_forward(
        order, vis_parts, w_proj, gain, w_key, w_value, [text_ring, image_kv_grad, *text_g[1:4]]
    )
    with jax.named_scope("image_key_value_sum"):
        pieces, kv_ring = ring_sum(near, far)
    with jax.named_scope("squares_sum"):
        squares = small_sum(jnp.concatenate([text_square, image_square]))
    text_square, image_square = squares[:text_rows], squares[text_rows:]

    image_kv, kv_out = image_out(pieces, image_square, ())
    with jax.named_scope("image_out_spread"):
        spread = lax.all_to_all(
            image_kv.reshape(dp, CHUNK, LANE), "dp", split_axis=0, concat_axis=0, tiled=True
        )

    packed, sent_done = take_blocks(owner, spread, ())
    with jax.named_scope("image_out_collect"):
        arrived = lax.all_to_all(
            packed.reshape(dp, slots, CHUNK, LANE), "dp", split_axis=0, concat_axis=0, tiled=True
        )

    text_d, text_inner, text_back = backward(order, text_g, w_key, w_value, gain, text_embed, [kv_ring])
    image_d, image_inner, _ = backward(order, image_g, w_key, w_value, gain, embed, [kv_out, text_back])
    with jax.named_scope("inner_sum"):
        inner = small_sum(jnp.concatenate([text_inner, image_inner]))
    d_far, d_near, back_done = image_backward(
        order, image_d, embed, image_square, inner[text_rows:], w_proj, [sent_done]
    )
    text_grad, text_grad_done = text_out(
        filled, text_d, text_embed, text_square, inner[:text_rows], [back_done]
    )
    with jax.named_scope("d_vis_sum"):
        d_pieces, _ = ring_sum(d_near.reshape(RING, -1, DV), d_far, [text_grad_done, arrived])
    key_out, value_out = key_value_out(filled, text_pieces, text_square, arrived)
    vision_grad = vision_out(d_pieces, vision, vis_gain, vis_scale)
    return key_out, value_out, text_grad, vision_grad


def solution(mesh):
    placed = (
        P(("dp", "mp"), None),
        P(),
        P(),
        P("dp", "mp"),
        P(None, "mp"),
        P("mp"),
        P("mp", None),
        P("mp", None),
        P("dp", "mp"),
        P("dp", "mp"),
    )
    return jax.shard_map(
        shards,
        mesh=mesh,
        in_specs=placed,
        out_specs=(P("dp", "mp"), P("dp", "mp"), P("dp", "mp"), P(("dp", "mp"), None)),
        check_vma=False,
    )
```

```python
import jax
import jax.numpy as jnp
from jax import lax
from jax.experimental import pallas as pl
from jax.experimental.pallas import tpu as pltpu
from jax.sharding import PartitionSpec as P

D = 8192
DV = 3200
PATCH = 256
LANE = 128
CHUNK = 16
BF = jnp.bfloat16
F32 = jnp.float32
VMEM = pl.BlockSpec(memory_space=pltpu.VMEM)
SMEM = pl.BlockSpec(memory_space=pltpu.SMEM)
HBM = pl.BlockSpec(memory_space=pltpu.HBM)
ANY = pl.BlockSpec(memory_space=pl.ANY)
DMA = pltpu.SemaphoreType.DMA

RING = 4
UP = [(2 * y + c, 2 * ((y + 1) % RING) + c) for y in range(RING) for c in range(2)]
DOWN = [(2 * y + c, 2 * ((y + 3) % RING) + c) for y in range(RING) for c in range(2)]
ACROSS = [(2 * y + c, 2 * ((y + 2) % RING) + c) for y in range(RING) for c in range(2)]
SPLIT = [(2 * y + c, 2 * ((y + 1 + 2 * c) % RING) + c) for y in range(RING) for c in range(2)]
PEER = [(2 * y + c, 2 * y + 1 - c) for y in range(RING) for c in range(2)]


def up(x):
    return lax.ppermute(x, "mp", UP)


def down(x):
    return lax.ppermute(x, "mp", DOWN)


def across(x):
    return lax.ppermute(x, "mp", ACROSS)


def peer(x):
    return lax.ppermute(x, "mp", PEER)


TOKEN = jax.ShapeDtypeStruct((8, LANE), F32)


def call(kernel, name, outs, args, scalars=0, far=(), far_outs=(), scratch=(), flops=0, after=(), token=False):
    size = sum(a.size * a.dtype.itemsize for a in args) + sum(o.size * o.dtype.itemsize for o in outs)
    args, outs = list(args), list(outs)
    ins, results = len(args), len(outs)

    def body(*refs):
        mine = refs[:ins] + refs[ins + len(after) : ins + len(after) + results]
        rest = refs[ins + len(after) + results :]
        if token:
            rest[0][...] = jnp.zeros(TOKEN.shape, F32)
            rest = rest[1:]
        kernel(*mine, *rest)

    return pl.pallas_call(
        body,
        in_specs=[SMEM if i < scalars else HBM if i in far else VMEM for i in range(ins)] + [ANY] * len(after),
        out_specs=[HBM if i in far_outs else VMEM for i in range(results)] + [VMEM] * token,
        out_shape=outs + [TOKEN] * token,
        scratch_shapes=list(scratch),
        compiler_params=pltpu.CompilerParams(vmem_limit_bytes=(52 if far else 8) * 1024 * 1024),
        cost_estimate=pl.CostEstimate(flops=flops, bytes_accessed=size, transcendentals=0),
        name=name,
    )(*args, *after)


def shape(dims, dtype):
    return jax.ShapeDtypeStruct(dims, dtype)


def dot(a, b):
    return jnp.dot(a, b, preferred_element_type=F32)


def dot_t(a, b):
    return lax.dot_general(a, b, (((1,), (1,)), ((), ())), preferred_element_type=F32)


def as_row(column):
    n = column.shape[0]
    return jnp.transpose(jnp.broadcast_to(column, (n, LANE)))[:1]


def as_column(row):
    n = row.shape[1]
    return jnp.transpose(jnp.broadcast_to(row, (LANE, n)))[:, :1]


def lane_block(ref, index, rows=slice(None)):
    return ref[rows, pl.ds(pl.multiple_of(index * LANE, LANE), LANE)]


def vision_norm(vision, gain):
    def kernel(v_ref, g_ref, o_ref, s_ref):
        v = v_ref[...].astype(F32)
        scale = lax.rsqrt(jnp.mean(v * v, axis=1, keepdims=True) + 1e-06)
        s_ref[...] = scale
        o_ref[...] = (v * scale * g_ref[...]).astype(BF)

    rows = vision.shape[0]
    return call(
        kernel, "vision_norm", [shape(vision.shape, BF), shape((rows, 1), F32)], [vision, gain], token=True
    )


def pack_grads(key_grad, value_grad, after):
    rows = key_grad.shape[0]
    slots = rows // PATCH
    per = PATCH // CHUNK
    grads = [g.reshape(slots, per, CHUNK, LANE) for g in (key_grad, value_grad)]

    def kernel(k_ref, v_ref, stack_ref, chunk_ref, sems):
        pairs = []
        for j, ref in enumerate((k_ref, v_ref)):
            for s in range(slots):
                pairs.append((ref.at[s], chunk_ref.at[pl.ds(j * per, per), s]))
            pairs.append((ref, stack_ref.at[j]))
        for wait in load_all(pairs, sems):
            wait()

    stack, chunks, token = call(
        kernel,
        "pack_grads",
        [shape((2, slots, per, CHUNK, LANE), BF), shape((2 * per, slots, CHUNK, LANE), BF)],
        grads,
        far=(0, 1),
        far_outs=(0, 1),
        scratch=[DMA((2 * slots + 2,))],
        after=after,
        token=True,
    )
    return stack.reshape(2 * rows, LANE), chunks, token


def take_blocks(index, x, after):
    count = index.shape[0]

    def kernel(index_ref, x_ref, o_ref):
        for j in range(count):
            o_ref[j] = x_ref[index_ref[j]]

    return call(kernel, "take_blocks", [shape((count,) + x.shape[1:], x.dtype)], [index, x], scalars=1, after=after, token=True)


def load_all(pairs, sems):
    copies = [pltpu.make_async_copy(src, dst, sems.at[i]) for i, (src, dst) in enumerate(pairs)]
    for copy in copies:
        copy.start()
    return [copy.wait for copy in copies]


def text_forward(order, text, gain, w_key, w_value, after):
    rows, width = text.shape

    def kernel(order_ref, t_far, g_ref, k_far, v_far, far_ref, near_ref, q_ref, t_ref, k_ref, v_ref, scaled, sems):
        waits = load_all([(t_far, t_ref), (k_far, k_ref), (v_far, v_ref)], sems)
        waits[0]()

        @pl.loop(0, rows // LANE)
        def _(i):
            at = pl.ds(pl.multiple_of(i * LANE, LANE), LANE)
            t = t_ref[at].astype(F32)
            scaled[at] = (t * g_ref[...]).astype(BF)
            q_ref[pl.ds(i, 1)] = as_row(jnp.sum(t * t, axis=1, keepdims=True))

        waits[1]()
        waits[2]()

        @pl.loop(0, RING)
        def _(b):
            there = order_ref[RING + b]
            w = jnp.concatenate([lane_block(k_ref, there), lane_block(v_ref, there)], axis=1)
            far_ref[b] = dot(scaled[...], w).astype(BF)
            own = order_ref[b]
            w = jnp.concatenate([lane_block(k_ref, own), lane_block(v_ref, own)], axis=1)
            near_ref[b] = dot(scaled[...], w)

    return call(
        kernel,
        "text_forward",
        [
            shape((RING, rows, 2 * LANE), BF),
            shape((RING, rows, 2 * LANE), F32),
            shape((rows // LANE, LANE), F32),
        ],
        [order, text, gain, w_key, w_value],
        scalars=1,
        far=(1, 3, 4),
        after=after,
        token=True,
        scratch=[
            pltpu.VMEM(text.shape, BF),
            pltpu.VMEM(w_key.shape, BF),
            pltpu.VMEM(w_value.shape, BF),
            pltpu.VMEM((rows, width), BF),
            DMA((3,)),
        ],
        flops=4 * rows * width * w_key.shape[1],
    )


def image_forward(where, order, pieces, w_proj, gain, w_key, w_value, after):
    rows_each = PATCH // 8
    depth, width = w_proj.shape

    def kernel(where_ref, order_ref, *refs):
        piece_refs = refs[: len(pieces)]
        p_far, g_ref, k_far, v_far, e_ref, far_ref, near_ref, q_ref, p_ref, k_ref, v_ref, vis, scaled, sems = refs[
            len(pieces) :
        ]
        cuts = [slice(n * 256, (n + 1) * 256) for n in range(width // 256)]
        waits = load_all(
            [(p_far.at[:, at], p_ref.at[n]) for n, at in enumerate(cuts)] + [(k_far, k_ref), (v_far, v_ref)], sems
        )
        b = 0
        for ref in piece_refs:
            vis[pl.ds(pl.multiple_of(where_ref[b] * rows_each, rows_each), ref.shape[0])] = ref[...]
            b += ref.shape[0] // rows_each

        for n, at in enumerate(cuts):
            waits[n]()
            e_ref[:, at] = dot(vis[...], p_ref[n]).astype(BF)

        @pl.loop(0, PATCH // LANE)
        def _(i):
            at = pl.ds(pl.multiple_of(i * LANE, LANE), LANE)
            e = e_ref[at].astype(F32)
            scaled[at] = (e * g_ref[...]).astype(BF)
            q_ref[pl.ds(i, 1)] = as_row(jnp.sum(e * e, axis=1, keepdims=True))

        waits[-2]()
        waits[-1]()

        @pl.loop(0, RING)
        def _(b):
            there = order_ref[RING + b]
            w = jnp.concatenate([lane_block(k_ref, there), lane_block(v_ref, there)], axis=1)
            far_ref[b] = dot(scaled[...], w).astype(BF)
            own = order_ref[b]
            w = jnp.concatenate([lane_block(k_ref, own), lane_block(v_ref, own)], axis=1)
            near_ref[b] = dot(scaled[...], w)

    return call(
        kernel,
        "image_forward",
        [
            shape((PATCH, width), BF),
            shape((RING, PATCH, 2 * LANE), BF),
            shape((RING, PATCH, 2 * LANE), F32),
            shape((PATCH // LANE, LANE), F32),
        ],
        [where, order, *pieces, w_proj, gain, w_key, w_value],
        scalars=2,
        token=True,
        far=(2 + len(pieces), 4 + len(pieces), 5 + len(pieces)),
        scratch=[
            pltpu.VMEM((width // 256, depth, 256), BF),
            pltpu.VMEM(w_key.shape, BF),
            pltpu.VMEM(w_value.shape, BF),
            pltpu.VMEM((PATCH, depth), BF),
            pltpu.VMEM((PATCH, width), BF),
            DMA((width // 256 + 2,)),
        ],
        flops=2 * PATCH * width * (depth + 2 * w_key.shape[1]),
        after=after,
    )


def backward(order, pieces, w_key, w_value, gain, embed, after):
    rows, width = embed.shape
    cols = w_key.shape[1]
    cuts = width // 256

    def kernel(order_ref, *refs):
        piece_refs = refs[: len(pieces)]
        k_far, v_far, g_ref, e_far, d_out, i_ref, k_ref, v_ref, e_ref, gk, gv, sems, d_held, out_sems = refs[len(pieces) :]
        d_ref = d_held if rows > PATCH else d_out
        outgoing = []
        pairs = []
        b = 0
        for ref in piece_refs:
            for j in range(ref.shape[0] // (2 * rows)):
                at = pl.ds(pl.multiple_of(order_ref[b] * LANE, LANE), LANE)
                pairs.append((ref.at[pl.ds(2 * rows * j, rows)], gk.at[:, at]))
                pairs.append((ref.at[pl.ds(2 * rows * j + rows, rows)], gv.at[:, at]))
                b += 1
        for n in range(cuts):
            at = pl.ds(n * 256, 256)
            pairs += [(k_far.at[at], k_ref.at[at]), (v_far.at[at], v_ref.at[at])]
        pairs.append((e_far, e_ref))
        waits = load_all(pairs, sems)
        for wait in waits[:16]:
            wait()
        for n in range(cuts):
            at = slice(n * 256, (n + 1) * 256)
            waits[16 + 2 * n]()
            waits[17 + 2 * n]()
            d = dot_t(gk[...], k_ref[at]) + dot_t(gv[...], v_ref[at])
            d_ref[:, at] = d * g_ref[:, at]
            if rows > PATCH:
                outgoing.append(pltpu.make_async_copy(d_ref.at[:, at], d_out.at[:, at], out_sems.at[n]))
                outgoing[-1].start()
        waits[-1]()

        @pl.loop(0, rows // LANE)
        def _(i):
            at = pl.ds(pl.multiple_of(i * LANE, LANE), LANE)
            i_ref[pl.ds(i, 1)] = as_row(jnp.sum(d_ref[at] * e_ref[at].astype(F32), axis=1, keepdims=True))

        for copy in outgoing:
            copy.wait()

    n = len(pieces)
    return call(
        kernel,
        "backward",
        [shape((rows, width), F32), shape((rows // LANE, LANE), F32)],
        [order, *pieces, w_key, w_value, gain, embed],
        scalars=1,
        far=tuple(range(1, n + 3)) + (n + 4,),
        scratch=[
            pltpu.VMEM(w_key.shape, BF),
            pltpu.VMEM(w_value.shape, BF),
            pltpu.VMEM(embed.shape, BF),
            pltpu.VMEM((rows, cols), BF),
            pltpu.VMEM((rows, cols), BF),
            DMA((17 + 2 * cuts,)),
            pltpu.VMEM(embed.shape if rows > PATCH else (8, LANE), F32),
            DMA((cuts,)),
        ],
        flops=4 * rows * width * cols,
        after=after,
        far_outs=(0,) if rows > PATCH else (),
        token=True,
    )


def embed_grad(d, e, square_row, inner_row):
    scale = lax.rsqrt(as_column(square_row) / D + 1e-05)
    inner = as_column(inner_row) / D
    return scale * d - e * (scale * scale * scale * inner)


def image_backward(order, image_d, embed, square, inner, w_proj, after):
    depth, width = w_proj.shape
    rows_each = PATCH // 8
    half = PATCH // 2
    cut = 640

    def kernel(order_ref, d_ref, e_ref, q_ref, i_ref, p_far, far_ref, near_ref, p_ref, grad, turned, sems):
        cuts = [slice(n * cut, (n + 1) * cut) for n in range(depth // cut)]
        waits = load_all([(p_far.at[at], p_ref.at[at]) for at in cuts], sems)

        @pl.loop(0, PATCH // LANE)
        def _(i):
            at = pl.ds(pl.multiple_of(i * LANE, LANE), LANE)
            row = pl.ds(i, 1)
            grad[at] = embed_grad(d_ref[at], e_ref[at].astype(F32), q_ref[row], i_ref[row]).astype(BF)

        for b in range(8):
            at = pl.ds(pl.multiple_of(order_ref[b] * rows_each, rows_each), rows_each)
            turned[b * rows_each : (b + 1) * rows_each] = grad[at]

        for n, at in enumerate(cuts):
            waits[n]()
            r = dot_t(turned[...], p_ref[at])
            near_ref[:, at] = r[:half]
            far_ref[:, at] = r[half:].astype(BF)

    return call(
        kernel,
        "image_backward",
        [shape((half, depth), BF), shape((half, depth), F32)],
        [order, image_d, embed, square, inner, w_proj],
        scalars=1,
        far=(5,),
        scratch=[
            pltpu.VMEM(w_proj.shape, BF),
            pltpu.VMEM((PATCH, width), BF),
            pltpu.VMEM((PATCH, width), BF),
            DMA((depth // cut,)),
        ],
        flops=2 * PATCH * width * depth,
        after=after,
        token=True,
    )


def ring_first(near, other, after):
    _, n, c = near.shape
    h = n // 2

    def kernel(a_ref, b_ref, up_ref, down_ref, here_ref, above_ref, below_ref):
        def total(k, at):
            return a_ref[k, at] + b_ref[k, at].astype(F32)

        first, second = slice(0, h), slice(h, n)
        up_ref[first] = total(2, first).astype(BF)
        up_ref[second] = total(1, second).astype(BF)
        down_ref[first] = total(3, first).astype(BF)
        down_ref[second] = total(2, second).astype(BF)
        here_ref[...] = total(0, slice(0, n))
        above_ref[...] = total(1, first)
        below_ref[...] = total(3, second)

    return call(
        kernel,
        "ring_first",
        [shape((n, c), BF), shape((n, c), BF), shape((n, c), F32), shape((h, c), F32), shape((h, c), F32)],
        [near, other],
        after=after,
        token=True,
    )


def ring_sum(near, far, after=()):
    up1, down1, here, above, below, token = ring_first(near, peer(far).reshape(near.shape), after)
    h = above.shape[0]
    up1, down1 = up(up1), down(down1)
    up2 = up((above + up1[:h].astype(F32)).astype(BF))
    down2 = down((below + down1[h:].astype(F32)).astype(BF))
    return (here, up1, down1, up2, down2), token


def ring_total(here_ref, up1_ref, down1_ref, up2_ref, down2_ref):
    h = up2_ref.shape[0]
    first = here_ref[:h] + down1_ref[:h].astype(F32) + up2_ref[...].astype(F32)
    second = here_ref[h:] + up1_ref[h:].astype(F32) + down2_ref[...].astype(F32)
    return first, second


def image_out(pieces, square, after):
    h = PATCH // 2

    def kernel(*refs):
        q_ref, o_ref = refs[5:7]
        for j, t in enumerate(ring_total(*refs[:5])):
            scale = lax.rsqrt(as_column(q_ref[j : j + 1]) / D + 1e-05)
            t = (t * scale).astype(BF)
            o_ref[j * h : (j + 1) * h] = t[:, :LANE]
            o_ref[PATCH + j * h : PATCH + (j + 1) * h] = t[:, LANE:]

    return call(kernel, "image_out", [shape((2 * PATCH, LANE), BF)], [*pieces, square], after=after, token=True)


def vision_out(pieces, vision, gain, scale):
    rows = vision.shape[0]
    h = rows // 2

    def kernel(*refs):
        v_ref, g_ref, s_ref, o_ref = refs[5:]
        for j, t in enumerate(ring_total(*refs[:5])):
            at = slice(j * h, (j + 1) * h)
            v, s = v_ref[at].astype(F32), s_ref[at]
            grad_h = t.astype(BF).astype(F32) * g_ref[...]
            inner = jnp.mean(grad_h * v, axis=1, keepdims=True)
            o_ref[at] = (s * grad_h - v * (s * s * s * inner)).astype(BF)

    return call(kernel, "vision_out", [shape(vision.shape, BF)], [*pieces, vision, gain, scale])[0]


def text_out(filled, text_d, text, square, inner, after):
    rows, width = text.shape
    parts = rows // LANE

    def kernel(f_ref, d_far, t_far, q_ref, i_ref, o_far, d_ref, t_ref, o_ref, sems, out_sems):
        cuts = [pl.ds(i * LANE, LANE) for i in range(parts)]
        waits = load_all([(d_far.at[at], d_ref.at[at]) for at in cuts] + [(t_far.at[at], t_ref.at[at]) for at in cuts], sems)
        outgoing = []
        for i, at in enumerate(cuts):
            waits[i]()
            waits[parts + i]()
            row = pl.ds(i, 1)
            grad = embed_grad(d_ref[at], t_ref[at].astype(F32), q_ref[row], i_ref[row])
            o_ref[at] = jnp.where(f_ref[i // (PATCH // LANE)] > 0, 0.0, grad).astype(BF)
            outgoing.append(pltpu.make_async_copy(o_ref.at[at], o_far.at[at], out_sems.at[i]))
            outgoing[-1].start()
        for copy in outgoing:
            copy.wait()

    return call(
        kernel,
        "text_out",
        [shape((rows, width), BF)],
        [filled, text_d, text, square, inner],
        scalars=1,
        far=(1, 2),
        far_outs=(0,),
        scratch=[
            pltpu.VMEM(text.shape, F32),
            pltpu.VMEM(text.shape, BF),
            pltpu.VMEM(text.shape, BF),
            DMA((2 * parts,)),
            DMA((parts,)),
        ],
        after=after,
        token=True,
    )


def key_value_out(filled, pieces, square, arrived):
    rows = pieces[0].shape[0]
    half = rows // 2
    per = PATCH // CHUNK

    def kernel(f_ref, *refs):
        q_ref, a_ref, k_ref, v_ref = refs[5:9]
        totals = ring_total(*refs[:5])
        for s in range(rows // PATCH):
            @pl.when(f_ref[s] > 0)
            def _():
                for c in range(per):
                    at = pl.ds(s * PATCH + c * CHUNK, CHUNK)
                    k_ref[at] = a_ref[c, s]
                    v_ref[at] = a_ref[per + c, s]

            @pl.when(f_ref[s] == 0)
            def _():
                for i in range(PATCH // LANE):
                    j = s * (PATCH // LANE) + i
                    at = slice(j * LANE, (j + 1) * LANE)
                    scale = lax.rsqrt(as_column(q_ref[j : j + 1]) / D + 1e-05)
                    t = totals[at.start // half][at.start % half : at.start % half + LANE]
                    t = (t * scale).astype(BF)
                    k_ref[at] = t[:, :LANE]
                    v_ref[at] = t[:, LANE:]

    return call(
        kernel,
        "key_value_out",
        [shape((rows, LANE), BF), shape((rows, LANE), BF)],
        [filled, *pieces, square, arrived],
        scalars=1,
    )


def join(core, x, other):
    rows = x.shape[0]

    def kernel(c_ref, x_ref, other_ref, o_ref):
        for c in range(2):
            @pl.when(c_ref[0] == c)
            def _():
                o_ref[c * rows : (c + 1) * rows] = x_ref[...]
                o_ref[(1 - c) * rows : (2 - c) * rows] = other_ref[...]

    return call(kernel, "join", [shape((2 * rows,) + x.shape[1:], x.dtype)], [core, x, other], scalars=1)[0]


def chip_gather(core, x):
    rows = x.shape[0]
    block = join(core, x, peer(x))
    near = lax.ppermute(block, "mp", SPLIT)
    far = lax.ppermute(lax.dynamic_slice_in_dim(near, core[0] * rows, rows), "mp", SPLIT)
    return [block, near, peer(near), far, peer(far)]


def small_sum(x):
    pair = x + peer(x)
    pair = pair + up(pair)
    return pair + across(pair)


def shards(
    vision,
    vision_gain,
    image_slot,
    text_embed,
    w_proj,
    llm_gain,
    w_key,
    w_value,
    key_grad,
    value_grad,
):
    dp = lax.axis_size("dp")
    here = lax.axis_index("dp")
    m = lax.axis_index("mp")
    y, c = m // 2, m % 2
    slots = text_embed.shape[0] // PATCH
    text_rows = text_embed.shape[0] // LANE

    rel = jnp.arange(8, dtype=jnp.int32)
    order = ((y + rel % RING) % RING) * 2 + (c ^ (rel // RING))
    core = c[None]
    near, next_, far = (y + 3 + 2 * c) % RING, (y + 1 + 2 * c) % RING, (y + 2) % RING
    where = jnp.stack(
        [2 * y, 2 * y + 1, 2 * near, 2 * near + 1, 2 * next_, 2 * next_ + 1, 2 * far + c, 2 * far + 1 - c]
    )
    slot_ids = jnp.arange(dp * slots, dtype=jnp.int32)
    onehot = slot_ids[:, None] == image_slot[None, :]
    owner = jnp.sum(jnp.where(onehot, jnp.arange(dp, dtype=jnp.int32)[None, :], 0), axis=1)
    mine = slot_ids[:slots] + here * slots
    filled = jnp.any(mine[:, None] == image_slot[None, :], axis=1).astype(jnp.int32)
    gain = llm_gain[None]
    vis_gain = vision_gain[None]

    vis_normed, vis_scale, norm_done = vision_norm(vision, vis_gain)
    with jax.named_scope("vision_gather"):
        vis_parts = chip_gather(core, vis_normed)

    grad_stack, grad_chunks, packed_done = pack_grads(key_grad, value_grad, [norm_done])
    with jax.named_scope("slot_grads_spread"):
        spread = lax.all_to_all(grad_chunks, "dp", split_axis=0, concat_axis=0, tiled=True)
    with jax.named_scope("text_grad_gather"):
        text_g = chip_gather(core, grad_stack)
    picked, picked_done = take_blocks(
        image_slot, spread.reshape(dp * slots, CHUNK, LANE), [packed_done, vis_parts[3]]
    )
    with jax.named_scope("slot_grads_collect"):
        image_kv_grad = lax.all_to_all(picked, "dp", split_axis=0, concat_axis=0, tiled=True)

    embed, far, near, image_square, image_done = image_forward(
        where, order, vis_parts, w_proj, gain, w_key, w_value, [picked_done]
    )
    text_far, text_near, text_square, text_done = text_forward(
        order, text_embed, gain, w_key, w_value, [image_done]
    )
    with jax.named_scope("image_key_value_sum"):
        pieces, kv_ring = ring_sum(near, far, [text_done, image_kv_grad])
    with jax.named_scope("image_grad_gather"):
        image_g = chip_gather(core, image_kv_grad.reshape(2 * PATCH, LANE))
    with jax.named_scope("text_key_value_sum"):
        text_pieces, text_ring = ring_sum(text_near, text_far, [kv_ring])
    with jax.named_scope("squares_sum"):
        squares = small_sum(jnp.concatenate([text_square, image_square]))
    text_square, image_square = squares[:text_rows], squares[text_rows:]

    image_kv, kv_out = image_out(pieces, image_square, ())
    with jax.named_scope("image_out_spread"):
        spread = lax.all_to_all(
            image_kv.reshape(dp, CHUNK, LANE), "dp", split_axis=0, concat_axis=0, tiled=True
        )

    packed, sent_done = take_blocks(owner, spread, ())
    with jax.named_scope("image_out_collect"):
        arrived = lax.all_to_all(
            packed.reshape(dp, slots, CHUNK, LANE), "dp", split_axis=0, concat_axis=0, tiled=True
        )

    text_d, text_inner, text_back = backward(
        where, text_g, w_key, w_value, gain, text_embed, [text_ring, pieces[1], pieces[2]]
    )
    image_d, image_inner, _ = backward(where, image_g, w_key, w_value, gain, embed, [text_back, kv_out])
    with jax.named_scope("inner_sum"):
        inner = small_sum(jnp.concatenate([text_inner, image_inner]))
    d_far, d_near, back_done = image_backward(
        order, image_d, embed, image_square, inner[text_rows:], w_proj, [sent_done]
    )
    text_grad, text_grad_done = text_out(
        filled, text_d, text_embed, text_square, inner[:text_rows], [back_done]
    )
    with jax.named_scope("d_vis_sum"):
        d_pieces, _ = ring_sum(d_near.reshape(RING, -1, DV), d_far, [text_grad_done, arrived])
    key_out, value_out = key_value_out(filled, text_pieces, text_square, arrived)
    vision_grad = vision_out(d_pieces, vision, vis_gain, vis_scale)
    return key_out, value_out, text_grad, vision_grad


def solution(mesh):
    placed = (
        P(("dp", "mp"), None),
        P(),
        P(),
        P("dp", "mp"),
        P(None, "mp"),
        P("mp"),
        P("mp", None),
        P("mp", None),
        P("dp", "mp"),
        P("dp", "mp"),
    )
    return jax.shard_map(
        shards,
        mesh=mesh,
        in_specs=placed,
        out_specs=(P("dp", "mp"), P("dp", "mp"), P("dp", "mp"), P(("dp", "mp"), None)),
        check_vma=False,
    )
```

```python
import jax
import jax.numpy as jnp
from jax import lax
from jax.experimental import pallas as pl
from jax.experimental.pallas import tpu as pltpu
from jax.sharding import PartitionSpec as P

D = 8192
DV = 3200
PATCH = 256
LANE = 128
CHUNK = 16
BF = jnp.bfloat16
F32 = jnp.float32
VMEM = pl.BlockSpec(memory_space=pltpu.VMEM)
SMEM = pl.BlockSpec(memory_space=pltpu.SMEM)
HBM = pl.BlockSpec(memory_space=pltpu.HBM)
ANY = pl.BlockSpec(memory_space=pl.ANY)
DMA = pltpu.SemaphoreType.DMA

RING = 4
UP = [(2 * y + c, 2 * ((y + 1) % RING) + c) for y in range(RING) for c in range(2)]
DOWN = [(2 * y + c, 2 * ((y + 3) % RING) + c) for y in range(RING) for c in range(2)]
ACROSS = [(2 * y + c, 2 * ((y + 2) % RING) + c) for y in range(RING) for c in range(2)]
SPLIT = [(2 * y + c, 2 * ((y + 1 + 2 * c) % RING) + c) for y in range(RING) for c in range(2)]
PEER = [(2 * y + c, 2 * y + 1 - c) for y in range(RING) for c in range(2)]


def up(x):
    return lax.ppermute(x, "mp", UP)


def down(x):
    return lax.ppermute(x, "mp", DOWN)


def across(x):
    return lax.ppermute(x, "mp", ACROSS)


def peer(x):
    return lax.ppermute(x, "mp", PEER)


TOKEN = jax.ShapeDtypeStruct((8, LANE), F32)


def call(kernel, name, outs, args, scalars=0, far=(), far_outs=(), scratch=(), flops=0, after=(), token=False):
    size = sum(a.size * a.dtype.itemsize for a in args) + sum(o.size * o.dtype.itemsize for o in outs)
    args, outs = list(args), list(outs)
    ins, results = len(args), len(outs)

    def body(*refs):
        mine = refs[:ins] + refs[ins + len(after) : ins + len(after) + results]
        rest = refs[ins + len(after) + results :]
        if token:
            rest[0][...] = jnp.zeros(TOKEN.shape, F32)
            rest = rest[1:]
        kernel(*mine, *rest)

    return pl.pallas_call(
        body,
        in_specs=[SMEM if i < scalars else HBM if i in far else VMEM for i in range(ins)] + [ANY] * len(after),
        out_specs=[HBM if i in far_outs else VMEM for i in range(results)] + [VMEM] * token,
        out_shape=outs + [TOKEN] * token,
        scratch_shapes=list(scratch),
        compiler_params=pltpu.CompilerParams(vmem_limit_bytes=(52 if far else 8) * 1024 * 1024),
        cost_estimate=pl.CostEstimate(flops=flops, bytes_accessed=size, transcendentals=0),
        name=name,
    )(*args, *after)


def shape(dims, dtype):
    return jax.ShapeDtypeStruct(dims, dtype)


def dot(a, b):
    return jnp.dot(a, b, preferred_element_type=F32)


def dot_t(a, b):
    return lax.dot_general(a, b, (((1,), (1,)), ((), ())), preferred_element_type=F32)


def as_row(column):
    n = column.shape[0]
    return jnp.transpose(jnp.broadcast_to(column, (n, LANE)))[:1]


def as_column(row):
    n = row.shape[1]
    return jnp.transpose(jnp.broadcast_to(row, (LANE, n)))[:, :1]


def lane_block(ref, index, rows=slice(None)):
    return ref[rows, pl.ds(pl.multiple_of(index * LANE, LANE), LANE)]


def vision_norm(vision, gain):
    def kernel(v_ref, g_ref, o_ref, s_ref):
        v = v_ref[...].astype(F32)
        scale = lax.rsqrt(jnp.mean(v * v, axis=1, keepdims=True) + 1e-06)
        s_ref[...] = scale
        o_ref[...] = (v * scale * g_ref[...]).astype(BF)

    rows = vision.shape[0]
    return call(
        kernel, "vision_norm", [shape(vision.shape, BF), shape((rows, 1), F32)], [vision, gain], token=True
    )


def pack_grads(key_grad, value_grad, after):
    rows = key_grad.shape[0]
    slots = rows // PATCH
    per = PATCH // CHUNK
    grads = [g.reshape(slots, per, CHUNK, LANE) for g in (key_grad, value_grad)]

    def kernel(k_ref, v_ref, stack_ref, chunk_ref, sems):
        pairs = []
        for j, ref in enumerate((k_ref, v_ref)):
            for s in range(slots):
                pairs.append((ref.at[s], chunk_ref.at[pl.ds(j * per, per), s]))
            pairs.append((ref, stack_ref.at[j]))
        for wait in load_all(pairs, sems):
            wait()

    stack, chunks, token = call(
        kernel,
        "pack_grads",
        [shape((2, slots, per, CHUNK, LANE), BF), shape((2 * per, slots, CHUNK, LANE), BF)],
        grads,
        far=(0, 1),
        far_outs=(0, 1),
        scratch=[DMA((2 * slots + 2,))],
        after=after,
        token=True,
    )
    return stack.reshape(2 * rows, LANE), chunks, token


def take_blocks(index, x, after):
    count = index.shape[0]

    def kernel(index_ref, x_ref, o_ref):
        for j in range(count):
            o_ref[j] = x_ref[index_ref[j]]

    return call(kernel, "take_blocks", [shape((count,) + x.shape[1:], x.dtype)], [index, x], scalars=1, after=after, token=True)


def load_all(pairs, sems):
    copies = [pltpu.make_async_copy(src, dst, sems.at[i]) for i, (src, dst) in enumerate(pairs)]
    for copy in copies:
        copy.start()
    return [copy.wait for copy in copies]


def text_forward(order, text, gain, w_key, w_value, after):
    rows, width = text.shape

    def kernel(order_ref, t_far, g_ref, k_far, v_far, far_ref, near_ref, q_ref, t_ref, k_ref, v_ref, scaled, sems):
        waits = load_all([(t_far, t_ref), (k_far, k_ref), (v_far, v_ref)], sems)
        waits[0]()

        @pl.loop(0, rows // LANE)
        def _(i):
            at = pl.ds(pl.multiple_of(i * LANE, LANE), LANE)
            t = t_ref[at].astype(F32)
            scaled[at] = (t * g_ref[...]).astype(BF)
            q_ref[pl.ds(i, 1)] = as_row(jnp.sum(t * t, axis=1, keepdims=True))

        waits[1]()
        waits[2]()

        @pl.loop(0, RING)
        def _(b):
            there = order_ref[RING + b]
            w = jnp.concatenate([lane_block(k_ref, there), lane_block(v_ref, there)], axis=1)
            far_ref[b] = dot(scaled[...], w).astype(BF)
            own = order_ref[b]
            w = jnp.concatenate([lane_block(k_ref, own), lane_block(v_ref, own)], axis=1)
            near_ref[b] = dot(scaled[...], w)

    return call(
        kernel,
        "text_forward",
        [
            shape((RING, rows, 2 * LANE), BF),
            shape((RING, rows, 2 * LANE), F32),
            shape((rows // LANE, LANE), F32),
        ],
        [order, text, gain, w_key, w_value],
        scalars=1,
        far=(1, 3, 4),
        after=after,
        token=True,
        scratch=[
            pltpu.VMEM(text.shape, BF),
            pltpu.VMEM(w_key.shape, BF),
            pltpu.VMEM(w_value.shape, BF),
            pltpu.VMEM((rows, width), BF),
            DMA((3,)),
        ],
        flops=4 * rows * width * w_key.shape[1],
    )


def image_forward(where, order, pieces, w_proj, gain, w_key, w_value, after):
    rows_each = PATCH // 8
    depth, width = w_proj.shape

    def kernel(where_ref, order_ref, *refs):
        piece_refs = refs[: len(pieces)]
        p_far, g_ref, k_far, v_far, e_ref, far_ref, near_ref, q_ref, p_ref, k_ref, v_ref, vis, scaled, sems = refs[
            len(pieces) :
        ]
        cuts = [slice(n * 256, (n + 1) * 256) for n in range(width // 256)]
        waits = load_all(
            [(p_far.at[:, at], p_ref.at[n]) for n, at in enumerate(cuts)] + [(k_far, k_ref), (v_far, v_ref)], sems
        )
        b = 0
        for ref in piece_refs:
            vis[pl.ds(pl.multiple_of(where_ref[b] * rows_each, rows_each), ref.shape[0])] = ref[...]
            b += ref.shape[0] // rows_each

        for n, at in enumerate(cuts):
            waits[n]()
            e_ref[:, at] = dot(vis[...], p_ref[n]).astype(BF)

        @pl.loop(0, PATCH // LANE)
        def _(i):
            at = pl.ds(pl.multiple_of(i * LANE, LANE), LANE)
            e = e_ref[at].astype(F32)
            scaled[at] = (e * g_ref[...]).astype(BF)
            q_ref[pl.ds(i, 1)] = as_row(jnp.sum(e * e, axis=1, keepdims=True))

        waits[-2]()
        waits[-1]()

        @pl.loop(0, RING)
        def _(b):
            there = order_ref[RING + b]
            w = jnp.concatenate([lane_block(k_ref, there), lane_block(v_ref, there)], axis=1)
            far_ref[b] = dot(scaled[...], w).astype(BF)
            own = order_ref[b]
            w = jnp.concatenate([lane_block(k_ref, own), lane_block(v_ref, own)], axis=1)
            near_ref[b] = dot(scaled[...], w)

    return call(
        kernel,
        "image_forward",
        [
            shape((PATCH, width), BF),
            shape((RING, PATCH, 2 * LANE), BF),
            shape((RING, PATCH, 2 * LANE), F32),
            shape((PATCH // LANE, LANE), F32),
        ],
        [where, order, *pieces, w_proj, gain, w_key, w_value],
        scalars=2,
        token=True,
        far=(2 + len(pieces), 4 + len(pieces), 5 + len(pieces)),
        scratch=[
            pltpu.VMEM((width // 256, depth, 256), BF),
            pltpu.VMEM(w_key.shape, BF),
            pltpu.VMEM(w_value.shape, BF),
            pltpu.VMEM((PATCH, depth), BF),
            pltpu.VMEM((PATCH, width), BF),
            DMA((width // 256 + 2,)),
        ],
        flops=2 * PATCH * width * (depth + 2 * w_key.shape[1]),
        after=after,
    )


def backward(order, pieces, w_key, w_value, gain, embed, after):
    rows, width = embed.shape
    cols = w_key.shape[1]
    cuts = width // 256

    def kernel(order_ref, *refs):
        piece_refs = refs[: len(pieces)]
        k_far, v_far, g_ref, e_far, d_out, i_ref, k_ref, v_ref, e_ref, gk, gv, sems, d_held, out_sems = refs[len(pieces) :]
        d_ref = d_held if rows > PATCH else d_out
        outgoing = []
        pairs = []
        b = 0
        for ref in piece_refs:
            for j in range(ref.shape[0] // (2 * rows)):
                at = pl.ds(pl.multiple_of(order_ref[b] * LANE, LANE), LANE)
                pairs.append((ref.at[pl.ds(2 * rows * j, rows)], gk.at[:, at]))
                pairs.append((ref.at[pl.ds(2 * rows * j + rows, rows)], gv.at[:, at]))
                b += 1
        for n in range(cuts):
            at = pl.ds(n * 256, 256)
            pairs += [(k_far.at[at], k_ref.at[at]), (v_far.at[at], v_ref.at[at])]
        pairs.append((e_far, e_ref))
        waits = load_all(pairs, sems)
        for wait in waits[:16]:
            wait()
        for n in range(cuts):
            at = slice(n * 256, (n + 1) * 256)
            waits[16 + 2 * n]()
            waits[17 + 2 * n]()
            d = dot_t(gk[...], k_ref[at]) + dot_t(gv[...], v_ref[at])
            d_ref[:, at] = d * g_ref[:, at]
            if rows > PATCH:
                outgoing.append(pltpu.make_async_copy(d_ref.at[:, at], d_out.at[:, at], out_sems.at[n]))
                outgoing[-1].start()
        waits[-1]()

        @pl.loop(0, rows // LANE)
        def _(i):
            at = pl.ds(pl.multiple_of(i * LANE, LANE), LANE)
            i_ref[pl.ds(i, 1)] = as_row(jnp.sum(d_ref[at] * e_ref[at].astype(F32), axis=1, keepdims=True))

        for copy in outgoing:
            copy.wait()

    n = len(pieces)
    return call(
        kernel,
        "backward",
        [shape((rows, width), F32), shape((rows // LANE, LANE), F32)],
        [order, *pieces, w_key, w_value, gain, embed],
        scalars=1,
        far=tuple(range(1, n + 3)) + (n + 4,),
        scratch=[
            pltpu.VMEM(w_key.shape, BF),
            pltpu.VMEM(w_value.shape, BF),
            pltpu.VMEM(embed.shape, BF),
            pltpu.VMEM((rows, cols), BF),
            pltpu.VMEM((rows, cols), BF),
            DMA((17 + 2 * cuts,)),
            pltpu.VMEM(embed.shape if rows > PATCH else (8, LANE), F32),
            DMA((cuts,)),
        ],
        flops=4 * rows * width * cols,
        after=after,
        far_outs=(0,) if rows > PATCH else (),
        token=True,
    )


def embed_grad(d, e, square_row, inner_row):
    scale = lax.rsqrt(as_column(square_row) / D + 1e-05)
    inner = as_column(inner_row) / D
    return scale * d - e * (scale * scale * scale * inner)


def image_backward(order, image_d, embed, square, inner, w_proj, after):
    depth, width = w_proj.shape
    rows_each = PATCH // 8
    half = PATCH // 2
    cut = 640

    def kernel(order_ref, d_ref, e_ref, q_ref, i_ref, p_far, far_ref, near_ref, p_ref, grad, turned, sems):
        cuts = [slice(n * cut, (n + 1) * cut) for n in range(depth // cut)]
        waits = load_all([(p_far.at[at], p_ref.at[at]) for at in cuts], sems)

        @pl.loop(0, PATCH // LANE)
        def _(i):
            at = pl.ds(pl.multiple_of(i * LANE, LANE), LANE)
            row = pl.ds(i, 1)
            grad[at] = embed_grad(d_ref[at], e_ref[at].astype(F32), q_ref[row], i_ref[row]).astype(BF)

        for b in range(8):
            at = pl.ds(pl.multiple_of(order_ref[b] * rows_each, rows_each), rows_each)
            turned[b * rows_each : (b + 1) * rows_each] = grad[at]

        for n, at in enumerate(cuts):
            waits[n]()
            r = dot_t(turned[...], p_ref[at])
            near_ref[:, at] = r[:half]
            far_ref[:, at] = r[half:].astype(BF)

    return call(
        kernel,
        "image_backward",
        [shape((half, depth), BF), shape((half, depth), F32)],
        [order, image_d, embed, square, inner, w_proj],
        scalars=1,
        far=(5,),
        scratch=[
            pltpu.VMEM(w_proj.shape, BF),
            pltpu.VMEM((PATCH, width), BF),
            pltpu.VMEM((PATCH, width), BF),
            DMA((depth // cut,)),
        ],
        flops=2 * PATCH * width * depth,
        after=after,
        token=True,
    )


def ring_first(near, other, after):
    _, n, c = near.shape
    h = n // 2

    def kernel(a_ref, b_ref, up_ref, down_ref, here_ref, above_ref, below_ref):
        def total(k, at):
            return a_ref[k, at] + b_ref[k, at].astype(F32)

        first, second = slice(0, h), slice(h, n)
        up_ref[first] = total(2, first).astype(BF)
        up_ref[second] = total(1, second).astype(BF)
        down_ref[first] = total(3, first).astype(BF)
        down_ref[second] = total(2, second).astype(BF)
        here_ref[...] = total(0, slice(0, n))
        above_ref[...] = total(1, first)
        below_ref[...] = total(3, second)

    return call(
        kernel,
        "ring_first",
        [shape((n, c), BF), shape((n, c), BF), shape((n, c), F32), shape((h, c), F32), shape((h, c), F32)],
        [near, other],
        after=after,
        token=True,
    )


def ring_sum(near, far, after=()):
    up1, down1, here, above, below, token = ring_first(near, peer(far).reshape(near.shape), after)
    h = above.shape[0]
    up1, down1 = up(up1), down(down1)
    up2 = up((above + up1[:h].astype(F32)).astype(BF))
    down2 = down((below + down1[h:].astype(F32)).astype(BF))
    return (here, up1, down1, up2, down2), token


def ring_total(here_ref, up1_ref, down1_ref, up2_ref, down2_ref):
    h = up2_ref.shape[0]
    first = here_ref[:h] + down1_ref[:h].astype(F32) + up2_ref[...].astype(F32)
    second = here_ref[h:] + up1_ref[h:].astype(F32) + down2_ref[...].astype(F32)
    return first, second


def image_out(pieces, square, after):
    h = PATCH // 2

    def kernel(*refs):
        q_ref, o_ref = refs[5:7]
        for j, t in enumerate(ring_total(*refs[:5])):
            scale = lax.rsqrt(as_column(q_ref[j : j + 1]) / D + 1e-05)
            t = (t * scale).astype(BF)
            o_ref[j * h : (j + 1) * h] = t[:, :LANE]
            o_ref[PATCH + j * h : PATCH + (j + 1) * h] = t[:, LANE:]

    return call(kernel, "image_out", [shape((2 * PATCH, LANE), BF)], [*pieces, square], after=after, token=True)


def vision_out(pieces, vision, gain, scale):
    rows = vision.shape[0]
    h = rows // 2

    def kernel(*refs):
        v_ref, g_ref, s_ref, o_ref = refs[5:]
        for j, t in enumerate(ring_total(*refs[:5])):
            at = slice(j * h, (j + 1) * h)
            v, s = v_ref[at].astype(F32), s_ref[at]
            grad_h = t.astype(BF).astype(F32) * g_ref[...]
            inner = jnp.mean(grad_h * v, axis=1, keepdims=True)
            o_ref[at] = (s * grad_h - v * (s * s * s * inner)).astype(BF)

    return call(kernel, "vision_out", [shape(vision.shape, BF)], [*pieces, vision, gain, scale])[0]


def text_out(filled, text_d, text, square, inner, after):
    rows, width = text.shape
    parts = rows // LANE

    def kernel(f_ref, d_far, t_far, q_ref, i_ref, o_far, d_ref, t_ref, o_ref, sems, out_sems):
        cuts = [pl.ds(i * LANE, LANE) for i in range(parts)]
        waits = load_all([(d_far.at[at], d_ref.at[at]) for at in cuts] + [(t_far.at[at], t_ref.at[at]) for at in cuts], sems)
        outgoing = []
        for i, at in enumerate(cuts):
            waits[i]()
            waits[parts + i]()
            row = pl.ds(i, 1)
            grad = embed_grad(d_ref[at], t_ref[at].astype(F32), q_ref[row], i_ref[row])
            o_ref[at] = jnp.where(f_ref[i // (PATCH // LANE)] > 0, 0.0, grad).astype(BF)
            outgoing.append(pltpu.make_async_copy(o_ref.at[at], o_far.at[at], out_sems.at[i]))
            outgoing[-1].start()
        for copy in outgoing:
            copy.wait()

    return call(
        kernel,
        "text_out",
        [shape((rows, width), BF)],
        [filled, text_d, text, square, inner],
        scalars=1,
        far=(1, 2),
        far_outs=(0,),
        scratch=[
            pltpu.VMEM(text.shape, F32),
            pltpu.VMEM(text.shape, BF),
            pltpu.VMEM(text.shape, BF),
            DMA((2 * parts,)),
            DMA((parts,)),
        ],
        after=after,
        token=True,
    )


def key_value_out(filled, pieces, square, arrived):
    rows = pieces[0].shape[0]
    half = rows // 2
    per = PATCH // CHUNK

    def kernel(f_ref, *refs):
        q_ref, a_ref, k_ref, v_ref = refs[5:9]
        totals = ring_total(*refs[:5])
        for s in range(rows // PATCH):
            @pl.when(f_ref[s] > 0)
            def _():
                for c in range(per):
                    at = pl.ds(s * PATCH + c * CHUNK, CHUNK)
                    k_ref[at] = a_ref[c, s]
                    v_ref[at] = a_ref[per + c, s]

            @pl.when(f_ref[s] == 0)
            def _():
                for i in range(PATCH // LANE):
                    j = s * (PATCH // LANE) + i
                    at = slice(j * LANE, (j + 1) * LANE)
                    scale = lax.rsqrt(as_column(q_ref[j : j + 1]) / D + 1e-05)
                    t = totals[at.start // half][at.start % half : at.start % half + LANE]
                    t = (t * scale).astype(BF)
                    k_ref[at] = t[:, :LANE]
                    v_ref[at] = t[:, LANE:]

    return call(
        kernel,
        "key_value_out",
        [shape((rows, LANE), BF), shape((rows, LANE), BF)],
        [filled, *pieces, square, arrived],
        scalars=1,
    )


def join(core, x, other):
    rows = x.shape[0]

    def kernel(c_ref, x_ref, other_ref, o_ref):
        for c in range(2):
            @pl.when(c_ref[0] == c)
            def _():
                o_ref[c * rows : (c + 1) * rows] = x_ref[...]
                o_ref[(1 - c) * rows : (2 - c) * rows] = other_ref[...]

    return call(kernel, "join", [shape((2 * rows,) + x.shape[1:], x.dtype)], [core, x, other], scalars=1)[0]


def chip_gather(core, x):
    rows = x.shape[0]
    block = join(core, x, peer(x))
    near = lax.ppermute(block, "mp", SPLIT)
    far = lax.ppermute(lax.dynamic_slice_in_dim(near, core[0] * rows, rows), "mp", SPLIT)
    return [block, near, peer(near), far, peer(far)]


def small_sum(x):
    pair = x + peer(x)
    pair = pair + up(pair)
    return pair + across(pair)


def shards(
    vision,
    vision_gain,
    image_slot,
    text_embed,
    w_proj,
    llm_gain,
    w_key,
    w_value,
    key_grad,
    value_grad,
):
    dp = lax.axis_size("dp")
    here = lax.axis_index("dp")
    m = lax.axis_index("mp")
    y, c = m // 2, m % 2
    slots = text_embed.shape[0] // PATCH
    text_rows = text_embed.shape[0] // LANE

    rel = jnp.arange(8, dtype=jnp.int32)
    order = ((y + rel % RING) % RING) * 2 + (c ^ (rel // RING))
    core = c[None]
    near, next_, far = (y + 3 + 2 * c) % RING, (y + 1 + 2 * c) % RING, (y + 2) % RING
    where = jnp.stack(
        [2 * y, 2 * y + 1, 2 * near, 2 * near + 1, 2 * next_, 2 * next_ + 1, 2 * far + c, 2 * far + 1 - c]
    )
    slot_ids = jnp.arange(dp * slots, dtype=jnp.int32)
    onehot = slot_ids[:, None] == image_slot[None, :]
    owner = jnp.sum(jnp.where(onehot, jnp.arange(dp, dtype=jnp.int32)[None, :], 0), axis=1)
    mine = slot_ids[:slots] + here * slots
    filled = jnp.any(mine[:, None] == image_slot[None, :], axis=1).astype(jnp.int32)
    gain = llm_gain[None]
    vis_gain = vision_gain[None]

    vis_normed, vis_scale, norm_done = vision_norm(vision, vis_gain)
    with jax.named_scope("vision_gather"):
        vis_parts = chip_gather(core, vis_normed)

    grad_stack, grad_chunks, packed_done = pack_grads(key_grad, value_grad, [norm_done])
    with jax.named_scope("slot_grads_spread"):
        spread = lax.all_to_all(grad_chunks, "dp", split_axis=0, concat_axis=0, tiled=True)
    with jax.named_scope("text_grad_gather"):
        text_g = chip_gather(core, grad_stack)
    picked, picked_done = take_blocks(
        image_slot, spread.reshape(dp * slots, CHUNK, LANE), [packed_done, vis_parts[3]]
    )
    with jax.named_scope("slot_grads_collect"):
        image_kv_grad = lax.all_to_all(picked, "dp", split_axis=0, concat_axis=0, tiled=True)

    embed, far, near, image_square, image_done = image_forward(
        where, order, vis_parts, w_proj, gain, w_key, w_value, [picked_done]
    )
    text_far, text_near, text_square, text_done = text_forward(
        order, text_embed, gain, w_key, w_value, [image_done, text_g[3]]
    )
    with jax.named_scope("image_key_value_sum"):
        pieces, kv_ring = ring_sum(near, far, [text_done, image_kv_grad])
    with jax.named_scope("image_grad_gather"):
        image_g = chip_gather(core, image_kv_grad.reshape(2 * PATCH, LANE))
    with jax.named_scope("text_key_value_sum"):
        text_pieces, text_ring = ring_sum(text_near, text_far, [kv_ring])
    with jax.named_scope("squares_sum"):
        squares = small_sum(jnp.concatenate([text_square, image_square]))
    text_square, image_square = squares[:text_rows], squares[text_rows:]

    image_kv, kv_out = image_out(pieces, image_square, ())
    with jax.named_scope("image_out_spread"):
        spread = lax.all_to_all(
            image_kv.reshape(dp, CHUNK, LANE), "dp", split_axis=0, concat_axis=0, tiled=True
        )

    text_d, text_inner, text_back = backward(
        where, text_g, w_key, w_value, gain, text_embed, [text_ring, pieces[1], pieces[2]]
    )
    image_d, image_inner, _ = backward(where, image_g, w_key, w_value, gain, embed, [text_back, kv_out, *text_pieces[1:3]])
    with jax.named_scope("inner_sum"):
        inner = small_sum(jnp.concatenate([text_inner, image_inner]))
    d_far, d_near, back_done = image_backward(
        order, image_d, embed, image_square, inner[text_rows:], w_proj, [spread, *text_pieces[3:]]
    )
    with jax.named_scope("d_vis_sum"):
        d_pieces, d_ring = ring_sum(d_near.reshape(RING, -1, DV), d_far)
    packed, _ = take_blocks(owner, spread, [d_ring])
    with jax.named_scope("image_out_collect"):
        arrived = lax.all_to_all(
            packed.reshape(dp, slots, CHUNK, LANE), "dp", split_axis=0, concat_axis=0, tiled=True
        )
    text_grad, _ = text_out(
        filled, text_d, text_embed, text_square, inner[:text_rows], [back_done, *d_pieces[1:3]]
    )
    key_out, value_out = key_value_out(filled, text_pieces, text_square, arrived)
    vision_grad = vision_out(d_pieces, vision, vis_gain, vis_scale)
    return key_out, value_out, text_grad, vision_grad


def solution(mesh):
    placed = (
        P(("dp", "mp"), None),
        P(),
        P(),
        P("dp", "mp"),
        P(None, "mp"),
        P("mp"),
        P("mp", None),
        P("mp", None),
        P("dp", "mp"),
        P("dp", "mp"),
    )
    return jax.shard_map(
        shards,
        mesh=mesh,
        in_specs=placed,
        out_specs=(P("dp", "mp"), P("dp", "mp"), P("dp", "mp"), P(("dp", "mp"), None)),
        check_vma=False,
    )
```

```python
import jax
import jax.numpy as jnp
from jax import lax
from jax.experimental import pallas as pl
from jax.experimental.pallas import tpu as pltpu
from jax.sharding import PartitionSpec as P

D = 8192
DV = 3200
PATCH = 256
LANE = 128
CHUNK = 16
BF = jnp.bfloat16
F32 = jnp.float32
VMEM = pl.BlockSpec(memory_space=pltpu.VMEM)
SMEM = pl.BlockSpec(memory_space=pltpu.SMEM)
HBM = pl.BlockSpec(memory_space=pltpu.HBM)
ANY = pl.BlockSpec(memory_space=pl.ANY)
DMA = pltpu.SemaphoreType.DMA

RING = 4
UP = [(2 * y + c, 2 * ((y + 1) % RING) + c) for y in range(RING) for c in range(2)]
DOWN = [(2 * y + c, 2 * ((y + 3) % RING) + c) for y in range(RING) for c in range(2)]
ACROSS = [(2 * y + c, 2 * ((y + 2) % RING) + c) for y in range(RING) for c in range(2)]
SPLIT = [(2 * y + c, 2 * ((y + 1 + 2 * c) % RING) + c) for y in range(RING) for c in range(2)]
PEER = [(2 * y + c, 2 * y + 1 - c) for y in range(RING) for c in range(2)]


def up(x):
    return lax.ppermute(x, "mp", UP)


def down(x):
    return lax.ppermute(x, "mp", DOWN)


def across(x):
    return lax.ppermute(x, "mp", ACROSS)


def peer(x):
    return lax.ppermute(x, "mp", PEER)


TOKEN = jax.ShapeDtypeStruct((8, LANE), F32)


def call(kernel, name, outs, args, scalars=0, far=(), far_outs=(), scratch=(), flops=0, after=(), token=False):
    size = sum(a.size * a.dtype.itemsize for a in args) + sum(o.size * o.dtype.itemsize for o in outs)
    args, outs = list(args), list(outs)
    ins, results = len(args), len(outs)

    def body(*refs):
        mine = refs[:ins] + refs[ins + len(after) : ins + len(after) + results]
        rest = refs[ins + len(after) + results :]
        if token:
            rest[0][...] = jnp.zeros(TOKEN.shape, F32)
            rest = rest[1:]
        kernel(*mine, *rest)

    return pl.pallas_call(
        body,
        in_specs=[SMEM if i < scalars else HBM if i in far else VMEM for i in range(ins)] + [ANY] * len(after),
        out_specs=[HBM if i in far_outs else VMEM for i in range(results)] + [VMEM] * token,
        out_shape=outs + [TOKEN] * token,
        scratch_shapes=list(scratch),
        compiler_params=pltpu.CompilerParams(vmem_limit_bytes=(52 if far else 8) * 1024 * 1024),
        cost_estimate=pl.CostEstimate(flops=flops, bytes_accessed=size, transcendentals=0),
        name=name,
    )(*args, *after)


def shape(dims, dtype):
    return jax.ShapeDtypeStruct(dims, dtype)


def dot(a, b):
    return jnp.dot(a, b, preferred_element_type=F32)


def dot_t(a, b):
    return lax.dot_general(a, b, (((1,), (1,)), ((), ())), preferred_element_type=F32)


def as_row(column):
    n = column.shape[0]
    return jnp.transpose(jnp.broadcast_to(column, (n, LANE)))[:1]


def as_column(row):
    n = row.shape[1]
    return jnp.transpose(jnp.broadcast_to(row, (LANE, n)))[:, :1]


def lane_block(ref, index, rows=slice(None)):
    return ref[rows, pl.ds(pl.multiple_of(index * LANE, LANE), LANE)]


def vision_norm(vision, gain):
    def kernel(v_ref, g_ref, o_ref, s_ref):
        v = v_ref[...].astype(F32)
        scale = lax.rsqrt(jnp.mean(v * v, axis=1, keepdims=True) + 1e-06)
        s_ref[...] = scale
        o_ref[...] = (v * scale * g_ref[...]).astype(BF)

    rows = vision.shape[0]
    return call(
        kernel, "vision_norm", [shape(vision.shape, BF), shape((rows, 1), F32)], [vision, gain], token=True
    )


def pack_grads(key_grad, value_grad, after):
    rows = key_grad.shape[0]
    slots = rows // PATCH
    per = PATCH // CHUNK
    grads = [g.reshape(slots, per, CHUNK, LANE) for g in (key_grad, value_grad)]

    def kernel(k_ref, v_ref, stack_ref, chunk_ref, sems):
        pairs = []
        for j, ref in enumerate((k_ref, v_ref)):
            for s in range(slots):
                pairs.append((ref.at[s], chunk_ref.at[pl.ds(j * per, per), s]))
            pairs.append((ref, stack_ref.at[j]))
        for wait in load_all(pairs, sems):
            wait()

    stack, chunks, token = call(
        kernel,
        "pack_grads",
        [shape((2, slots, per, CHUNK, LANE), BF), shape((2 * per, slots, CHUNK, LANE), BF)],
        grads,
        far=(0, 1),
        far_outs=(0, 1),
        scratch=[DMA((2 * slots + 2,))],
        after=after,
        token=True,
    )
    return stack.reshape(2 * rows, LANE), chunks, token


def take_blocks(index, x, after):
    count = index.shape[0]

    def kernel(index_ref, x_ref, o_ref):
        for j in range(count):
            o_ref[j] = x_ref[index_ref[j]]

    return call(kernel, "take_blocks", [shape((count,) + x.shape[1:], x.dtype)], [index, x], scalars=1, after=after, token=True)


def load_all(pairs, sems):
    copies = [pltpu.make_async_copy(src, dst, sems.at[i]) for i, (src, dst) in enumerate(pairs)]
    for copy in copies:
        copy.start()
    return [copy.wait for copy in copies]


def text_forward(text, gain, w_key, w_value, after):
    rows, width = text.shape
    blocks = w_key.shape[1] // LANE

    def kernel(t_far, g_ref, k_far, v_far, o_ref, q_ref, t_ref, k_ref, v_ref, scaled, sems):
        waits = load_all([(t_far, t_ref), (k_far, k_ref), (v_far, v_ref)], sems)
        waits[0]()

        @pl.loop(0, rows // LANE)
        def _(i):
            at = pl.ds(pl.multiple_of(i * LANE, LANE), LANE)
            t = t_ref[at].astype(F32)
            scaled[at] = (t * g_ref[...]).astype(BF)
            q_ref[pl.ds(i, 1)] = as_row(jnp.sum(t * t, axis=1, keepdims=True))

        waits[1]()
        waits[2]()

        @pl.loop(0, blocks)
        def _(b):
            w = jnp.concatenate([lane_block(k_ref, b), lane_block(v_ref, b)], axis=1)
            o_ref[b] = dot(scaled[...], w).astype(BF)

    return call(
        kernel,
        "text_forward",
        [shape((blocks, rows, 2 * LANE), BF), shape((rows // LANE, LANE), F32)],
        [text, gain, w_key, w_value],
        far=(0, 2, 3),
        after=after,
        token=True,
        scratch=[
            pltpu.VMEM(text.shape, BF),
            pltpu.VMEM(w_key.shape, BF),
            pltpu.VMEM(w_value.shape, BF),
            pltpu.VMEM((rows, width), BF),
            DMA((3,)),
        ],
        flops=4 * rows * width * w_key.shape[1],
    )


def image_forward(where, order, pieces, w_proj, gain, w_key, w_value, after):
    rows_each = PATCH // 8
    depth, width = w_proj.shape

    def kernel(where_ref, order_ref, *refs):
        piece_refs = refs[: len(pieces)]
        p_far, g_ref, k_far, v_far, e_ref, far_ref, near_ref, q_ref, p_ref, k_ref, v_ref, vis, scaled, sems = refs[
            len(pieces) :
        ]
        cuts = [slice(n * 256, (n + 1) * 256) for n in range(width // 256)]
        waits = load_all(
            [(p_far.at[:, at], p_ref.at[n]) for n, at in enumerate(cuts)] + [(k_far, k_ref), (v_far, v_ref)], sems
        )
        b = 0
        for ref in piece_refs:
            vis[pl.ds(pl.multiple_of(where_ref[b] * rows_each, rows_each), ref.shape[0])] = ref[...]
            b += ref.shape[0] // rows_each

        for n, at in enumerate(cuts):
            waits[n]()
            e_ref[:, at] = dot(vis[...], p_ref[n]).astype(BF)

        @pl.loop(0, PATCH // LANE)
        def _(i):
            at = pl.ds(pl.multiple_of(i * LANE, LANE), LANE)
            e = e_ref[at].astype(F32)
            scaled[at] = (e * g_ref[...]).astype(BF)
            q_ref[pl.ds(i, 1)] = as_row(jnp.sum(e * e, axis=1, keepdims=True))

        waits[-2]()
        waits[-1]()

        @pl.loop(0, RING)
        def _(b):
            there = order_ref[RING + b]
            w = jnp.concatenate([lane_block(k_ref, there), lane_block(v_ref, there)], axis=1)
            far_ref[b] = dot(scaled[...], w).astype(BF)
            own = order_ref[b]
            w = jnp.concatenate([lane_block(k_ref, own), lane_block(v_ref, own)], axis=1)
            near_ref[b] = dot(scaled[...], w)

    return call(
        kernel,
        "image_forward",
        [
            shape((PATCH, width), BF),
            shape((RING, PATCH, 2 * LANE), BF),
            shape((RING, PATCH, 2 * LANE), F32),
            shape((PATCH // LANE, LANE), F32),
        ],
        [where, order, *pieces, w_proj, gain, w_key, w_value],
        scalars=2,
        token=True,
        far=(2 + len(pieces), 4 + len(pieces), 5 + len(pieces)),
        scratch=[
            pltpu.VMEM((width // 256, depth, 256), BF),
            pltpu.VMEM(w_key.shape, BF),
            pltpu.VMEM(w_value.shape, BF),
            pltpu.VMEM((PATCH, depth), BF),
            pltpu.VMEM((PATCH, width), BF),
            DMA((width // 256 + 2,)),
        ],
        flops=2 * PATCH * width * (depth + 2 * w_key.shape[1]),
        after=after,
    )


def backward(order, pieces, w_key, w_value, gain, embed, after):
    rows, width = embed.shape
    cols = w_key.shape[1]
    cuts = width // 256

    def kernel(order_ref, *refs):
        piece_refs = refs[: len(pieces)]
        k_far, v_far, g_ref, e_far, d_out, i_ref, k_ref, v_ref, e_ref, gk, gv, sems, d_held, out_sems = refs[len(pieces) :]
        d_ref = d_held if rows > PATCH else d_out
        outgoing = []
        pairs = []
        b = 0
        for ref in piece_refs:
            for j in range(ref.shape[0] // (2 * rows)):
                at = pl.ds(pl.multiple_of(order_ref[b] * LANE, LANE), LANE)
                pairs.append((ref.at[pl.ds(2 * rows * j, rows)], gk.at[:, at]))
                pairs.append((ref.at[pl.ds(2 * rows * j + rows, rows)], gv.at[:, at]))
                b += 1
        for n in range(cuts):
            at = pl.ds(n * 256, 256)
            pairs += [(k_far.at[at], k_ref.at[at]), (v_far.at[at], v_ref.at[at])]
        pairs.append((e_far, e_ref))
        waits = load_all(pairs, sems)
        for wait in waits[:16]:
            wait()
        for n in range(cuts):
            at = slice(n * 256, (n + 1) * 256)
            waits[16 + 2 * n]()
            waits[17 + 2 * n]()
            d = dot_t(gk[...], k_ref[at]) + dot_t(gv[...], v_ref[at])
            d_ref[:, at] = d * g_ref[:, at]
            if rows > PATCH:
                outgoing.append(pltpu.make_async_copy(d_ref.at[:, at], d_out.at[:, at], out_sems.at[n]))
                outgoing[-1].start()
        waits[-1]()

        @pl.loop(0, rows // LANE)
        def _(i):
            at = pl.ds(pl.multiple_of(i * LANE, LANE), LANE)
            i_ref[pl.ds(i, 1)] = as_row(jnp.sum(d_ref[at] * e_ref[at].astype(F32), axis=1, keepdims=True))

        for copy in outgoing:
            copy.wait()

    n = len(pieces)
    return call(
        kernel,
        "backward",
        [shape((rows, width), F32), shape((rows // LANE, LANE), F32)],
        [order, *pieces, w_key, w_value, gain, embed],
        scalars=1,
        far=tuple(range(1, n + 3)) + (n + 4,),
        scratch=[
            pltpu.VMEM(w_key.shape, BF),
            pltpu.VMEM(w_value.shape, BF),
            pltpu.VMEM(embed.shape, BF),
            pltpu.VMEM((rows, cols), BF),
            pltpu.VMEM((rows, cols), BF),
            DMA((17 + 2 * cuts,)),
            pltpu.VMEM(embed.shape if rows > PATCH else (8, LANE), F32),
            DMA((cuts,)),
        ],
        flops=4 * rows * width * cols,
        after=after,
        far_outs=(0,) if rows > PATCH else (),
        token=True,
    )


def embed_grad(d, e, square_row, inner_row):
    scale = lax.rsqrt(as_column(square_row) / D + 1e-05)
    inner = as_column(inner_row) / D
    return scale * d - e * (scale * scale * scale * inner)


def image_backward(order, image_d, embed, square, inner, w_proj, after):
    depth, width = w_proj.shape
    rows_each = PATCH // 8
    half = PATCH // 2
    cut = 640

    def kernel(order_ref, d_ref, e_ref, q_ref, i_ref, p_far, far_ref, near_ref, p_ref, grad, turned, sems):
        cuts = [slice(n * cut, (n + 1) * cut) for n in range(depth // cut)]
        waits = load_all([(p_far.at[at], p_ref.at[at]) for at in cuts], sems)

        @pl.loop(0, PATCH // LANE)
        def _(i):
            at = pl.ds(pl.multiple_of(i * LANE, LANE), LANE)
            row = pl.ds(i, 1)
            grad[at] = embed_grad(d_ref[at], e_ref[at].astype(F32), q_ref[row], i_ref[row]).astype(BF)

        for b in range(8):
            at = pl.ds(pl.multiple_of(order_ref[b] * rows_each, rows_each), rows_each)
            turned[b * rows_each : (b + 1) * rows_each] = grad[at]

        for n, at in enumerate(cuts):
            waits[n]()
            r = dot_t(turned[...], p_ref[at])
            near_ref[:, at] = r[:half]
            far_ref[:, at] = r[half:].astype(BF)

    return call(
        kernel,
        "image_backward",
        [shape((half, depth), BF), shape((half, depth), F32)],
        [order, image_d, embed, square, inner, w_proj],
        scalars=1,
        far=(5,),
        scratch=[
            pltpu.VMEM(w_proj.shape, BF),
            pltpu.VMEM((PATCH, width), BF),
            pltpu.VMEM((PATCH, width), BF),
            DMA((depth // cut,)),
        ],
        flops=2 * PATCH * width * depth,
        after=after,
        token=True,
    )


def ring_first(near, other, after):
    _, n, c = near.shape
    h = n // 2

    def kernel(a_ref, b_ref, up_ref, down_ref, here_ref, above_ref, below_ref):
        def total(k, at):
            return a_ref[k, at] + b_ref[k, at].astype(F32)

        first, second = slice(0, h), slice(h, n)
        up_ref[first] = total(2, first).astype(BF)
        up_ref[second] = total(1, second).astype(BF)
        down_ref[first] = total(3, first).astype(BF)
        down_ref[second] = total(2, second).astype(BF)
        here_ref[...] = total(0, slice(0, n))
        above_ref[...] = total(1, first)
        below_ref[...] = total(3, second)

    return call(
        kernel,
        "ring_first",
        [shape((n, c), BF), shape((n, c), BF), shape((n, c), F32), shape((h, c), F32), shape((h, c), F32)],
        [near, other],
        after=after,
        token=True,
    )


def ring_sum(near, far, after=()):
    up1, down1, here, above, below, token = ring_first(near, peer(far).reshape(near.shape), after)
    h = above.shape[0]
    up1, down1 = up(up1), down(down1)
    up2 = up((above + up1[:h].astype(F32)).astype(BF))
    down2 = down((below + down1[h:].astype(F32)).astype(BF))
    return (here, up1, down1, up2, down2), token


def ring_total(here_ref, up1_ref, down1_ref, up2_ref, down2_ref):
    h = up2_ref.shape[0]
    first = here_ref[:h] + down1_ref[:h].astype(F32) + up2_ref[...].astype(F32)
    second = here_ref[h:] + up1_ref[h:].astype(F32) + down2_ref[...].astype(F32)
    return first, second


def image_out(pieces, square, after):
    h = PATCH // 2

    def kernel(*refs):
        q_ref, o_ref = refs[5:7]
        for j, t in enumerate(ring_total(*refs[:5])):
            scale = lax.rsqrt(as_column(q_ref[j : j + 1]) / D + 1e-05)
            t = (t * scale).astype(BF)
            o_ref[j * h : (j + 1) * h] = t[:, :LANE]
            o_ref[PATCH + j * h : PATCH + (j + 1) * h] = t[:, LANE:]

    return call(kernel, "image_out", [shape((2 * PATCH, LANE), BF)], [*pieces, square], after=after, token=True)


def vision_out(pieces, vision, gain, scale):
    rows = vision.shape[0]
    h = rows // 2

    def kernel(*refs):
        v_ref, g_ref, s_ref, o_ref = refs[5:]
        for j, t in enumerate(ring_total(*refs[:5])):
            at = slice(j * h, (j + 1) * h)
            v, s = v_ref[at].astype(F32), s_ref[at]
            grad_h = t.astype(BF).astype(F32) * g_ref[...]
            inner = jnp.mean(grad_h * v, axis=1, keepdims=True)
            o_ref[at] = (s * grad_h - v * (s * s * s * inner)).astype(BF)

    return call(kernel, "vision_out", [shape(vision.shape, BF)], [*pieces, vision, gain, scale])[0]


def text_out(filled, text_d, text, square, inner, after):
    rows, width = text.shape
    parts = rows // LANE

    def kernel(f_ref, d_far, t_far, q_ref, i_ref, o_far, d_ref, t_ref, o_ref, sems, out_sems):
        cuts = [pl.ds(i * LANE, LANE) for i in range(parts)]
        waits = load_all([(d_far.at[at], d_ref.at[at]) for at in cuts] + [(t_far.at[at], t_ref.at[at]) for at in cuts], sems)
        outgoing = []
        for i, at in enumerate(cuts):
            waits[i]()
            waits[parts + i]()
            row = pl.ds(i, 1)
            grad = embed_grad(d_ref[at], t_ref[at].astype(F32), q_ref[row], i_ref[row])
            o_ref[at] = jnp.where(f_ref[i // (PATCH // LANE)] > 0, 0.0, grad).astype(BF)
            outgoing.append(pltpu.make_async_copy(o_ref.at[at], o_far.at[at], out_sems.at[i]))
            outgoing[-1].start()
        for copy in outgoing:
            copy.wait()

    return call(
        kernel,
        "text_out",
        [shape((rows, width), BF)],
        [filled, text_d, text, square, inner],
        scalars=1,
        far=(1, 2),
        far_outs=(0,),
        scratch=[
            pltpu.VMEM(text.shape, F32),
            pltpu.VMEM(text.shape, BF),
            pltpu.VMEM(text.shape, BF),
            DMA((2 * parts,)),
            DMA((parts,)),
        ],
        after=after,
        token=True,
    )


def key_value_out(filled, text_kv, square, arrived):
    rows = text_kv.shape[0]
    per = PATCH // CHUNK

    def kernel(f_ref, t_ref, q_ref, a_ref, k_ref, v_ref):
        for s in range(rows // PATCH):
            @pl.when(f_ref[s] > 0)
            def _():
                for c in range(per):
                    at = pl.ds(s * PATCH + c * CHUNK, CHUNK)
                    k_ref[at] = a_ref[c, s]
                    v_ref[at] = a_ref[per + c, s]

            @pl.when(f_ref[s] == 0)
            def _():
                for i in range(PATCH // LANE):
                    j = s * (PATCH // LANE) + i
                    at = pl.ds(j * LANE, LANE)
                    scale = lax.rsqrt(as_column(q_ref[j : j + 1]) / D + 1e-05)
                    t = (t_ref[at].astype(F32) * scale).astype(BF)
                    k_ref[at] = t[:, :LANE]
                    v_ref[at] = t[:, LANE:]

    return call(
        kernel,
        "key_value_out",
        [shape((rows, LANE), BF), shape((rows, LANE), BF)],
        [filled, text_kv, square, arrived],
        scalars=1,
    )


def join(core, x, other):
    rows = x.shape[0]

    def kernel(c_ref, x_ref, other_ref, o_ref):
        for c in range(2):
            @pl.when(c_ref[0] == c)
            def _():
                o_ref[c * rows : (c + 1) * rows] = x_ref[...]
                o_ref[(1 - c) * rows : (2 - c) * rows] = other_ref[...]

    return call(kernel, "join", [shape((2 * rows,) + x.shape[1:], x.dtype)], [core, x, other], scalars=1)[0]


def chip_gather(core, x):
    rows = x.shape[0]
    block = join(core, x, peer(x))
    near = lax.ppermute(block, "mp", SPLIT)
    far = lax.ppermute(lax.dynamic_slice_in_dim(near, core[0] * rows, rows), "mp", SPLIT)
    return [block, near, peer(near), far, peer(far)]


def small_sum(x):
    pair = x + peer(x)
    pair = pair + up(pair)
    return pair + across(pair)


def shards(
    vision,
    vision_gain,
    image_slot,
    text_embed,
    w_proj,
    llm_gain,
    w_key,
    w_value,
    key_grad,
    value_grad,
):
    dp = lax.axis_size("dp")
    here = lax.axis_index("dp")
    m = lax.axis_index("mp")
    y, c = m // 2, m % 2
    slots = text_embed.shape[0] // PATCH
    text_rows = text_embed.shape[0] // LANE

    rel = jnp.arange(8, dtype=jnp.int32)
    order = ((y + rel % RING) % RING) * 2 + (c ^ (rel // RING))
    core = c[None]
    near, next_, far = (y + 3 + 2 * c) % RING, (y + 1 + 2 * c) % RING, (y + 2) % RING
    where = jnp.stack(
        [2 * y, 2 * y + 1, 2 * near, 2 * near + 1, 2 * next_, 2 * next_ + 1, 2 * far + c, 2 * far + 1 - c]
    )
    slot_ids = jnp.arange(dp * slots, dtype=jnp.int32)
    onehot = slot_ids[:, None] == image_slot[None, :]
    owner = jnp.sum(jnp.where(onehot, jnp.arange(dp, dtype=jnp.int32)[None, :], 0), axis=1)
    mine = slot_ids[:slots] + here * slots
    filled = jnp.any(mine[:, None] == image_slot[None, :], axis=1).astype(jnp.int32)
    gain = llm_gain[None]
    vis_gain = vision_gain[None]

    vis_normed, vis_scale, norm_done = vision_norm(vision, vis_gain)
    with jax.named_scope("vision_gather"):
        vis_parts = chip_gather(core, vis_normed)

    grad_stack, grad_chunks, packed_done = pack_grads(key_grad, value_grad, [norm_done])
    with jax.named_scope("slot_grads_spread"):
        spread = lax.all_to_all(grad_chunks, "dp", split_axis=0, concat_axis=0, tiled=True)
    with jax.named_scope("text_grad_gather"):
        text_g = lax.all_gather(grad_stack, "mp", axis=0, tiled=True)
    picked, picked_done = take_blocks(
        image_slot, spread.reshape(dp * slots, CHUNK, LANE), [packed_done, vis_parts[3]]
    )
    with jax.named_scope("slot_grads_collect"):
        image_kv_grad = lax.all_to_all(picked, "dp", split_axis=0, concat_axis=0, tiled=True)

    embed, far, near, image_square, image_done = image_forward(
        where, order, vis_parts, w_proj, gain, w_key, w_value, [picked_done]
    )
    text_part, text_square, text_done = text_forward(text_embed, gain, w_key, w_value, [image_done])
    with jax.named_scope("text_key_value_sum"):
        text_kv = lax.psum_scatter(text_part, "mp", scatter_dimension=0, tiled=False)
    with jax.named_scope("image_key_value_sum"):
        pieces, kv_ring = ring_sum(near, far, [text_done, image_kv_grad])
    with jax.named_scope("image_grad_gather"):
        image_g = chip_gather(core, image_kv_grad.reshape(2 * PATCH, LANE))
    with jax.named_scope("squares_sum"):
        squares = small_sum(jnp.concatenate([text_square, image_square]))
    text_square, image_square = squares[:text_rows], squares[text_rows:]

    image_kv, kv_out = image_out(pieces, image_square, ())
    with jax.named_scope("image_out_spread"):
        spread = lax.all_to_all(
            image_kv.reshape(dp, CHUNK, LANE), "dp", split_axis=0, concat_axis=0, tiled=True
        )

    text_d, text_inner, text_back = backward(
        rel, [text_g], w_key, w_value, gain, text_embed, [kv_ring, pieces[1], pieces[2]]
    )
    image_d, image_inner, _ = backward(where, image_g, w_key, w_value, gain, embed, [text_back, kv_out])
    with jax.named_scope("inner_sum"):
        inner = small_sum(jnp.concatenate([text_inner, image_inner]))
    d_far, d_near, back_done = image_backward(
        order, image_d, embed, image_square, inner[text_rows:], w_proj, [spread]
    )
    with jax.named_scope("d_vis_sum"):
        d_pieces, d_ring = ring_sum(d_near.reshape(RING, -1, DV), d_far)
    packed, _ = take_blocks(owner, spread, [d_ring])
    with jax.named_scope("image_out_collect"):
        arrived = lax.all_to_all(
            packed.reshape(dp, slots, CHUNK, LANE), "dp", split_axis=0, concat_axis=0, tiled=True
        )
    text_grad, _ = text_out(
        filled, text_d, text_embed, text_square, inner[:text_rows], [back_done, *d_pieces[1:3]]
    )
    key_out, value_out = key_value_out(filled, text_kv, text_square, arrived)
    vision_grad = vision_out(d_pieces, vision, vis_gain, vis_scale)
    return key_out, value_out, text_grad, vision_grad


def solution(mesh):
    placed = (
        P(("dp", "mp"), None),
        P(),
        P(),
        P("dp", "mp"),
        P(None, "mp"),
        P("mp"),
        P("mp", None),
        P("mp", None),
        P("dp", "mp"),
        P("dp", "mp"),
    )
    return jax.shard_map(
        shards,
        mesh=mesh,
        in_specs=placed,
        out_specs=(P("dp", "mp"), P("dp", "mp"), P("dp", "mp"), P(("dp", "mp"), None)),
        check_vma=False,
    )
```

```python
import jax
import jax.numpy as jnp
from jax import lax
from jax.experimental import pallas as pl
from jax.experimental.pallas import tpu as pltpu
from jax.sharding import PartitionSpec as P

D = 8192
DV = 3200
PATCH = 256
LANE = 128
CHUNK = 16
BF = jnp.bfloat16
F32 = jnp.float32
VMEM = pl.BlockSpec(memory_space=pltpu.VMEM)
SMEM = pl.BlockSpec(memory_space=pltpu.SMEM)
HBM = pl.BlockSpec(memory_space=pltpu.HBM)
ANY = pl.BlockSpec(memory_space=pl.ANY)
DMA = pltpu.SemaphoreType.DMA

RING = 4
UP = [(2 * y + c, 2 * ((y + 1) % RING) + c) for y in range(RING) for c in range(2)]
DOWN = [(2 * y + c, 2 * ((y + 3) % RING) + c) for y in range(RING) for c in range(2)]
ACROSS = [(2 * y + c, 2 * ((y + 2) % RING) + c) for y in range(RING) for c in range(2)]
SPLIT = [(2 * y + c, 2 * ((y + 1 + 2 * c) % RING) + c) for y in range(RING) for c in range(2)]
PEER = [(2 * y + c, 2 * y + 1 - c) for y in range(RING) for c in range(2)]


def up(x):
    return lax.ppermute(x, "mp", UP)


def down(x):
    return lax.ppermute(x, "mp", DOWN)


def across(x):
    return lax.ppermute(x, "mp", ACROSS)


def peer(x):
    return lax.ppermute(x, "mp", PEER)


TOKEN = jax.ShapeDtypeStruct((8, LANE), F32)


def call(kernel, name, outs, args, scalars=0, far=(), far_outs=(), scratch=(), flops=0, after=(), token=False):
    size = sum(a.size * a.dtype.itemsize for a in args) + sum(o.size * o.dtype.itemsize for o in outs)
    args, outs = list(args), list(outs)
    ins, results = len(args), len(outs)

    def body(*refs):
        mine = refs[:ins] + refs[ins + len(after) : ins + len(after) + results]
        rest = refs[ins + len(after) + results :]
        if token:
            rest[0][...] = jnp.zeros(TOKEN.shape, F32)
            rest = rest[1:]
        kernel(*mine, *rest)

    return pl.pallas_call(
        body,
        in_specs=[SMEM if i < scalars else HBM if i in far else VMEM for i in range(ins)] + [ANY] * len(after),
        out_specs=[HBM if i in far_outs else VMEM for i in range(results)] + [VMEM] * token,
        out_shape=outs + [TOKEN] * token,
        scratch_shapes=list(scratch),
        compiler_params=pltpu.CompilerParams(vmem_limit_bytes=(52 if far else 8) * 1024 * 1024),
        cost_estimate=pl.CostEstimate(flops=flops, bytes_accessed=size, transcendentals=0),
        name=name,
    )(*args, *after)


def shape(dims, dtype):
    return jax.ShapeDtypeStruct(dims, dtype)


def dot(a, b):
    return jnp.dot(a, b, preferred_element_type=F32)


def dot_t(a, b):
    return lax.dot_general(a, b, (((1,), (1,)), ((), ())), preferred_element_type=F32)


def as_row(column):
    n = column.shape[0]
    return jnp.transpose(jnp.broadcast_to(column, (n, LANE)))[:1]


def as_column(row):
    n = row.shape[1]
    return jnp.transpose(jnp.broadcast_to(row, (LANE, n)))[:, :1]


def lane_block(ref, index, rows=slice(None)):
    return ref[rows, pl.ds(pl.multiple_of(index * LANE, LANE), LANE)]


def vision_norm(vision, gain):
    def kernel(v_ref, g_ref, o_ref, s_ref):
        v = v_ref[...].astype(F32)
        scale = lax.rsqrt(jnp.mean(v * v, axis=1, keepdims=True) + 1e-06)
        s_ref[...] = scale
        o_ref[...] = (v * scale * g_ref[...]).astype(BF)

    rows = vision.shape[0]
    return call(
        kernel, "vision_norm", [shape(vision.shape, BF), shape((rows, 1), F32)], [vision, gain], token=True
    )


def pack_grads(key_grad, value_grad, after):
    rows = key_grad.shape[0]
    slots = rows // PATCH
    per = PATCH // CHUNK
    grads = [g.reshape(slots, per, CHUNK, LANE) for g in (key_grad, value_grad)]

    def kernel(k_ref, v_ref, stack_ref, chunk_ref, sems):
        pairs = []
        for j, ref in enumerate((k_ref, v_ref)):
            for s in range(slots):
                pairs.append((ref.at[s], chunk_ref.at[pl.ds(j * per, per), s]))
            pairs.append((ref, stack_ref.at[j]))
        for wait in load_all(pairs, sems):
            wait()

    stack, chunks, token = call(
        kernel,
        "pack_grads",
        [shape((2, slots, per, CHUNK, LANE), BF), shape((2 * per, slots, CHUNK, LANE), BF)],
        grads,
        far=(0, 1),
        far_outs=(0, 1),
        scratch=[DMA((2 * slots + 2,))],
        after=after,
        token=True,
    )
    return stack.reshape(2 * rows, LANE), chunks, token


def take_blocks(index, x, after):
    count = index.shape[0]

    def kernel(index_ref, x_ref, o_ref):
        for j in range(count):
            o_ref[j] = x_ref[index_ref[j]]

    return call(kernel, "take_blocks", [shape((count,) + x.shape[1:], x.dtype)], [index, x], scalars=1, after=after, token=True)


def load_all(pairs, sems):
    copies = [pltpu.make_async_copy(src, dst, sems.at[i]) for i, (src, dst) in enumerate(pairs)]
    for copy in copies:
        copy.start()
    return [copy.wait for copy in copies]


def text_forward(text, gain, w_key, w_value, after):
    rows, width = text.shape
    blocks = w_key.shape[1] // LANE

    def kernel(t_far, g_ref, k_far, v_far, o_ref, q_ref, t_ref, k_ref, v_ref, scaled, sems):
        waits = load_all([(t_far, t_ref), (k_far, k_ref), (v_far, v_ref)], sems)
        waits[0]()

        @pl.loop(0, rows // LANE)
        def _(i):
            at = pl.ds(pl.multiple_of(i * LANE, LANE), LANE)
            t = t_ref[at].astype(F32)
            scaled[at] = (t * g_ref[...]).astype(BF)
            q_ref[pl.ds(i, 1)] = as_row(jnp.sum(t * t, axis=1, keepdims=True))

        waits[1]()
        waits[2]()

        @pl.loop(0, blocks)
        def _(b):
            w = jnp.concatenate([lane_block(k_ref, b), lane_block(v_ref, b)], axis=1)
            o_ref[b] = dot(scaled[...], w).astype(BF)

    return call(
        kernel,
        "text_forward",
        [shape((blocks, rows, 2 * LANE), BF), shape((rows // LANE, LANE), F32)],
        [text, gain, w_key, w_value],
        far=(0, 2, 3),
        after=after,
        token=True,
        scratch=[
            pltpu.VMEM(text.shape, BF),
            pltpu.VMEM(w_key.shape, BF),
            pltpu.VMEM(w_value.shape, BF),
            pltpu.VMEM((rows, width), BF),
            DMA((3,)),
        ],
        flops=4 * rows * width * w_key.shape[1],
    )


def image_forward(where, order, pieces, w_proj, gain, w_key, w_value, after):
    rows_each = PATCH // 8
    depth, width = w_proj.shape

    def kernel(where_ref, order_ref, *refs):
        piece_refs = refs[: len(pieces)]
        p_far, g_ref, k_far, v_far, e_ref, far_ref, near_ref, q_ref, p_ref, k_ref, v_ref, vis, scaled, sems = refs[
            len(pieces) :
        ]
        cuts = [slice(n * 256, (n + 1) * 256) for n in range(width // 256)]
        waits = load_all(
            [(p_far.at[:, at], p_ref.at[n]) for n, at in enumerate(cuts)] + [(k_far, k_ref), (v_far, v_ref)], sems
        )
        b = 0
        for ref in piece_refs:
            vis[pl.ds(pl.multiple_of(where_ref[b] * rows_each, rows_each), ref.shape[0])] = ref[...]
            b += ref.shape[0] // rows_each

        for n, at in enumerate(cuts):
            waits[n]()
            e_ref[:, at] = dot(vis[...], p_ref[n]).astype(BF)

        @pl.loop(0, PATCH // LANE)
        def _(i):
            at = pl.ds(pl.multiple_of(i * LANE, LANE), LANE)
            e = e_ref[at].astype(F32)
            scaled[at] = (e * g_ref[...]).astype(BF)
            q_ref[pl.ds(i, 1)] = as_row(jnp.sum(e * e, axis=1, keepdims=True))

        waits[-2]()
        waits[-1]()

        @pl.loop(0, RING)
        def _(b):
            there = order_ref[RING + b]
            w = jnp.concatenate([lane_block(k_ref, there), lane_block(v_ref, there)], axis=1)
            far_ref[b] = dot(scaled[...], w).astype(BF)
            own = order_ref[b]
            w = jnp.concatenate([lane_block(k_ref, own), lane_block(v_ref, own)], axis=1)
            near_ref[b] = dot(scaled[...], w)

    return call(
        kernel,
        "image_forward",
        [
            shape((PATCH, width), BF),
            shape((RING, PATCH, 2 * LANE), BF),
            shape((RING, PATCH, 2 * LANE), F32),
            shape((PATCH // LANE, LANE), F32),
        ],
        [where, order, *pieces, w_proj, gain, w_key, w_value],
        scalars=2,
        token=True,
        far=(2 + len(pieces), 4 + len(pieces), 5 + len(pieces)),
        scratch=[
            pltpu.VMEM((width // 256, depth, 256), BF),
            pltpu.VMEM(w_key.shape, BF),
            pltpu.VMEM(w_value.shape, BF),
            pltpu.VMEM((PATCH, depth), BF),
            pltpu.VMEM((PATCH, width), BF),
            DMA((width // 256 + 2,)),
        ],
        flops=2 * PATCH * width * (depth + 2 * w_key.shape[1]),
        after=after,
    )


def backward(order, pieces, w_key, w_value, gain, embed, after):
    rows, width = embed.shape
    cols = w_key.shape[1]
    cuts = width // 256

    def kernel(order_ref, *refs):
        piece_refs = refs[: len(pieces)]
        k_far, v_far, g_ref, e_far, d_out, i_ref, k_ref, v_ref, e_ref, gk, gv, sems, d_held, out_sems = refs[len(pieces) :]
        d_ref = d_held if rows > PATCH else d_out
        outgoing = []
        pairs = []
        b = 0
        for ref in piece_refs:
            for j in range(ref.shape[0] // (2 * rows)):
                at = pl.ds(pl.multiple_of(order_ref[b] * LANE, LANE), LANE)
                pairs.append((ref.at[pl.ds(2 * rows * j, rows)], gk.at[:, at]))
                pairs.append((ref.at[pl.ds(2 * rows * j + rows, rows)], gv.at[:, at]))
                b += 1
        for n in range(cuts):
            at = pl.ds(n * 256, 256)
            pairs += [(k_far.at[at], k_ref.at[at]), (v_far.at[at], v_ref.at[at])]
        pairs.append((e_far, e_ref))
        waits = load_all(pairs, sems)
        for wait in waits[:16]:
            wait()
        for n in range(cuts):
            at = slice(n * 256, (n + 1) * 256)
            waits[16 + 2 * n]()
            waits[17 + 2 * n]()
            d = dot_t(gk[...], k_ref[at]) + dot_t(gv[...], v_ref[at])
            d_ref[:, at] = d * g_ref[:, at]
            if rows > PATCH:
                outgoing.append(pltpu.make_async_copy(d_ref.at[:, at], d_out.at[:, at], out_sems.at[n]))
                outgoing[-1].start()
        waits[-1]()

        @pl.loop(0, rows // LANE)
        def _(i):
            at = pl.ds(pl.multiple_of(i * LANE, LANE), LANE)
            i_ref[pl.ds(i, 1)] = as_row(jnp.sum(d_ref[at] * e_ref[at].astype(F32), axis=1, keepdims=True))

        for copy in outgoing:
            copy.wait()

    n = len(pieces)
    return call(
        kernel,
        "backward",
        [shape((rows, width), F32), shape((rows // LANE, LANE), F32)],
        [order, *pieces, w_key, w_value, gain, embed],
        scalars=1,
        far=tuple(range(1, n + 3)) + (n + 4,),
        scratch=[
            pltpu.VMEM(w_key.shape, BF),
            pltpu.VMEM(w_value.shape, BF),
            pltpu.VMEM(embed.shape, BF),
            pltpu.VMEM((rows, cols), BF),
            pltpu.VMEM((rows, cols), BF),
            DMA((17 + 2 * cuts,)),
            pltpu.VMEM(embed.shape if rows > PATCH else (8, LANE), F32),
            DMA((cuts,)),
        ],
        flops=4 * rows * width * cols,
        after=after,
        far_outs=(0,) if rows > PATCH else (),
        token=True,
    )


def embed_grad(d, e, square_row, inner_row):
    scale = lax.rsqrt(as_column(square_row) / D + 1e-05)
    inner = as_column(inner_row) / D
    return scale * d - e * (scale * scale * scale * inner)


def image_backward(order, image_d, embed, square, inner, w_proj, after):
    depth, width = w_proj.shape
    rows_each = PATCH // 8
    half = PATCH // 2
    cut = 640

    def kernel(order_ref, d_ref, e_ref, q_ref, i_ref, p_far, far_ref, near_ref, p_ref, grad, turned, sems):
        cuts = [slice(n * cut, (n + 1) * cut) for n in range(depth // cut)]
        waits = load_all([(p_far.at[at], p_ref.at[at]) for at in cuts], sems)

        @pl.loop(0, PATCH // LANE)
        def _(i):
            at = pl.ds(pl.multiple_of(i * LANE, LANE), LANE)
            row = pl.ds(i, 1)
            grad[at] = embed_grad(d_ref[at], e_ref[at].astype(F32), q_ref[row], i_ref[row]).astype(BF)

        for b in range(8):
            at = pl.ds(pl.multiple_of(order_ref[b] * rows_each, rows_each), rows_each)
            turned[b * rows_each : (b + 1) * rows_each] = grad[at]

        for n, at in enumerate(cuts):
            waits[n]()
            r = dot_t(turned[...], p_ref[at])
            near_ref[:, at] = r[:half]
            far_ref[:, at] = r[half:].astype(BF)

    return call(
        kernel,
        "image_backward",
        [shape((half, depth), BF), shape((half, depth), F32)],
        [order, image_d, embed, square, inner, w_proj],
        scalars=1,
        far=(5,),
        scratch=[
            pltpu.VMEM(w_proj.shape, BF),
            pltpu.VMEM((PATCH, width), BF),
            pltpu.VMEM((PATCH, width), BF),
            DMA((depth // cut,)),
        ],
        flops=2 * PATCH * width * depth,
        after=after,
        token=True,
    )


def ring_first(near, other, after):
    _, n, c = near.shape
    h = n // 2

    def kernel(a_ref, b_ref, up_ref, down_ref, here_ref, above_ref, below_ref):
        def total(k, at):
            return a_ref[k, at] + b_ref[k, at].astype(F32)

        first, second = slice(0, h), slice(h, n)
        up_ref[first] = total(2, first).astype(BF)
        up_ref[second] = total(1, second).astype(BF)
        down_ref[first] = total(3, first).astype(BF)
        down_ref[second] = total(2, second).astype(BF)
        here_ref[...] = total(0, slice(0, n))
        above_ref[...] = total(1, first)
        below_ref[...] = total(3, second)

    return call(
        kernel,
        "ring_first",
        [shape((n, c), BF), shape((n, c), BF), shape((n, c), F32), shape((h, c), F32), shape((h, c), F32)],
        [near, other],
        after=after,
        token=True,
    )


def ring_sum(near, far, after=()):
    up1, down1, here, above, below, token = ring_first(near, peer(far).reshape(near.shape), after)
    h = above.shape[0]
    up1, down1 = up(up1), down(down1)
    up2 = up((above + up1[:h].astype(F32)).astype(BF))
    down2 = down((below + down1[h:].astype(F32)).astype(BF))
    return (here, up1, down1, up2, down2), token


def ring_total(here_ref, up1_ref, down1_ref, up2_ref, down2_ref):
    h = up2_ref.shape[0]
    first = here_ref[:h] + down1_ref[:h].astype(F32) + up2_ref[...].astype(F32)
    second = here_ref[h:] + up1_ref[h:].astype(F32) + down2_ref[...].astype(F32)
    return first, second


def image_out(pieces, square, after):
    h = PATCH // 2

    def kernel(*refs):
        q_ref, o_ref = refs[5:7]
        for j, t in enumerate(ring_total(*refs[:5])):
            scale = lax.rsqrt(as_column(q_ref[j : j + 1]) / D + 1e-05)
            t = (t * scale).astype(BF)
            o_ref[j * h : (j + 1) * h] = t[:, :LANE]
            o_ref[PATCH + j * h : PATCH + (j + 1) * h] = t[:, LANE:]

    return call(kernel, "image_out", [shape((2 * PATCH, LANE), BF)], [*pieces, square], after=after, token=True)


def vision_out(pieces, vision, gain, scale):
    rows = vision.shape[0]
    h = rows // 2

    def kernel(*refs):
        v_ref, g_ref, s_ref, o_ref = refs[5:]
        for j, t in enumerate(ring_total(*refs[:5])):
            at = slice(j * h, (j + 1) * h)
            v, s = v_ref[at].astype(F32), s_ref[at]
            grad_h = t.astype(BF).astype(F32) * g_ref[...]
            inner = jnp.mean(grad_h * v, axis=1, keepdims=True)
            o_ref[at] = (s * grad_h - v * (s * s * s * inner)).astype(BF)

    return call(kernel, "vision_out", [shape(vision.shape, BF)], [*pieces, vision, gain, scale])[0]


def text_out(filled, text_d, text, square, inner, after):
    rows, width = text.shape
    parts = rows // LANE

    def kernel(f_ref, d_far, t_far, q_ref, i_ref, o_far, d_ref, t_ref, o_ref, sems, out_sems):
        cuts = [pl.ds(i * LANE, LANE) for i in range(parts)]
        waits = load_all([(d_far.at[at], d_ref.at[at]) for at in cuts] + [(t_far.at[at], t_ref.at[at]) for at in cuts], sems)
        outgoing = []
        for i, at in enumerate(cuts):
            waits[i]()
            waits[parts + i]()
            row = pl.ds(i, 1)
            grad = embed_grad(d_ref[at], t_ref[at].astype(F32), q_ref[row], i_ref[row])
            o_ref[at] = jnp.where(f_ref[i // (PATCH // LANE)] > 0, 0.0, grad).astype(BF)
            outgoing.append(pltpu.make_async_copy(o_ref.at[at], o_far.at[at], out_sems.at[i]))
            outgoing[-1].start()
        for copy in outgoing:
            copy.wait()

    return call(
        kernel,
        "text_out",
        [shape((rows, width), BF)],
        [filled, text_d, text, square, inner],
        scalars=1,
        far=(1, 2),
        far_outs=(0,),
        scratch=[
            pltpu.VMEM(text.shape, F32),
            pltpu.VMEM(text.shape, BF),
            pltpu.VMEM(text.shape, BF),
            DMA((2 * parts,)),
            DMA((parts,)),
        ],
        after=after,
        token=True,
    )


def key_value_out(filled, text_kv, square, arrived):
    rows = text_kv.shape[0]
    per = PATCH // CHUNK

    def kernel(f_ref, t_ref, q_ref, a_ref, k_ref, v_ref):
        for s in range(rows // PATCH):
            @pl.when(f_ref[s] > 0)
            def _():
                for c in range(per):
                    at = pl.ds(s * PATCH + c * CHUNK, CHUNK)
                    k_ref[at] = a_ref[c, s]
                    v_ref[at] = a_ref[per + c, s]

            @pl.when(f_ref[s] == 0)
            def _():
                for i in range(PATCH // LANE):
                    j = s * (PATCH // LANE) + i
                    at = pl.ds(j * LANE, LANE)
                    scale = lax.rsqrt(as_column(q_ref[j : j + 1]) / D + 1e-05)
                    t = (t_ref[at].astype(F32) * scale).astype(BF)
                    k_ref[at] = t[:, :LANE]
                    v_ref[at] = t[:, LANE:]

    return call(
        kernel,
        "key_value_out",
        [shape((rows, LANE), BF), shape((rows, LANE), BF)],
        [filled, text_kv, square, arrived],
        scalars=1,
    )


def join(core, x, other):
    rows = x.shape[0]

    def kernel(c_ref, x_ref, other_ref, o_ref):
        for c in range(2):
            @pl.when(c_ref[0] == c)
            def _():
                o_ref[c * rows : (c + 1) * rows] = x_ref[...]
                o_ref[(1 - c) * rows : (2 - c) * rows] = other_ref[...]

    return call(kernel, "join", [shape((2 * rows,) + x.shape[1:], x.dtype)], [core, x, other], scalars=1)[0]


def chip_gather(core, x):
    rows = x.shape[0]
    block = join(core, x, peer(x))
    near = lax.ppermute(block, "mp", SPLIT)
    far = lax.ppermute(lax.dynamic_slice_in_dim(near, core[0] * rows, rows), "mp", SPLIT)
    return [block, near, peer(near), far, peer(far)]


def small_sum(x):
    pair = x + peer(x)
    return (pair + up(pair)) + (down(pair) + across(pair))


def shards(
    vision,
    vision_gain,
    image_slot,
    text_embed,
    w_proj,
    llm_gain,
    w_key,
    w_value,
    key_grad,
    value_grad,
):
    dp = lax.axis_size("dp")
    here = lax.axis_index("dp")
    m = lax.axis_index("mp")
    y, c = m // 2, m % 2
    slots = text_embed.shape[0] // PATCH
    text_rows = text_embed.shape[0] // LANE

    rel = jnp.arange(8, dtype=jnp.int32)
    order = ((y + rel % RING) % RING) * 2 + (c ^ (rel // RING))
    core = c[None]
    near, next_, far = (y + 3 + 2 * c) % RING, (y + 1 + 2 * c) % RING, (y + 2) % RING
    where = jnp.stack(
        [2 * y, 2 * y + 1, 2 * near, 2 * near + 1, 2 * next_, 2 * next_ + 1, 2 * far + c, 2 * far + 1 - c]
    )
    slot_ids = jnp.arange(dp * slots, dtype=jnp.int32)
    onehot = slot_ids[:, None] == image_slot[None, :]
    owner = jnp.sum(jnp.where(onehot, jnp.arange(dp, dtype=jnp.int32)[None, :], 0), axis=1)
    mine = slot_ids[:slots] + here * slots
    filled = jnp.any(mine[:, None] == image_slot[None, :], axis=1).astype(jnp.int32)
    gain = llm_gain[None]
    vis_gain = vision_gain[None]

    vis_normed, vis_scale, norm_done = vision_norm(vision, vis_gain)
    with jax.named_scope("vision_gather"):
        vis_parts = chip_gather(core, vis_normed)

    grad_stack, grad_chunks, packed_done = pack_grads(key_grad, value_grad, [norm_done])
    with jax.named_scope("slot_grads_spread"):
        spread = lax.all_to_all(grad_chunks, "dp", split_axis=0, concat_axis=0, tiled=True)
    with jax.named_scope("text_grad_gather"):
        text_g = lax.all_gather(grad_stack, "mp", axis=0, tiled=True)
    picked, picked_done = take_blocks(
        image_slot, spread.reshape(dp * slots, CHUNK, LANE), [packed_done, vis_parts[3]]
    )
    with jax.named_scope("slot_grads_collect"):
        image_kv_grad = lax.all_to_all(picked, "dp", split_axis=0, concat_axis=0, tiled=True)

    embed, far, near, image_square, image_done = image_forward(
        where, order, vis_parts, w_proj, gain, w_key, w_value, [picked_done]
    )
    text_part, text_square, text_done = text_forward(text_embed, gain, w_key, w_value, [image_done])
    with jax.named_scope("text_key_value_sum"):
        text_kv = lax.psum_scatter(text_part, "mp", scatter_dimension=0, tiled=False)
    with jax.named_scope("image_key_value_sum"):
        pieces, kv_ring = ring_sum(near, far, [text_done, image_kv_grad])
    with jax.named_scope("image_grad_gather"):
        image_g = chip_gather(core, image_kv_grad.reshape(2 * PATCH, LANE))
    with jax.named_scope("squares_sum"):
        squares = small_sum(jnp.concatenate([text_square, image_square]))
    text_square, image_square = squares[:text_rows], squares[text_rows:]

    image_kv, kv_out = image_out(pieces, image_square, ())
    with jax.named_scope("image_out_spread"):
        spread = lax.all_to_all(
            image_kv.reshape(dp, CHUNK, LANE), "dp", split_axis=0, concat_axis=0, tiled=True
        )

    text_d, text_inner, text_back = backward(
        rel, [text_g], w_key, w_value, gain, text_embed, [kv_ring, pieces[1], pieces[2]]
    )
    image_d, image_inner, _ = backward(where, image_g, w_key, w_value, gain, embed, [text_back, spread])
    with jax.named_scope("inner_sum"):
        inner = small_sum(jnp.concatenate([text_inner, image_inner]))
    d_far, d_near, back_done = image_backward(
        order, image_d, embed, image_square, inner[text_rows:], w_proj, [kv_out]
    )
    with jax.named_scope("d_vis_sum"):
        d_pieces, d_ring = ring_sum(d_near.reshape(RING, -1, DV), d_far)
    packed, _ = take_blocks(owner, spread, [d_ring])
    with jax.named_scope("image_out_collect"):
        arrived = lax.all_to_all(
            packed.reshape(dp, slots, CHUNK, LANE), "dp", split_axis=0, concat_axis=0, tiled=True
        )
    text_grad, _ = text_out(
        filled, text_d, text_embed, text_square, inner[:text_rows], [back_done, *d_pieces[1:3]]
    )
    key_out, value_out = key_value_out(filled, text_kv, text_square, arrived)
    vision_grad = vision_out(d_pieces, vision, vis_gain, vis_scale)
    return key_out, value_out, text_grad, vision_grad


def solution(mesh):
    placed = (
        P(("dp", "mp"), None),
        P(),
        P(),
        P("dp", "mp"),
        P(None, "mp"),
        P("mp"),
        P("mp", None),
        P("mp", None),
        P("dp", "mp"),
        P("dp", "mp"),
    )
    return jax.shard_map(
        shards,
        mesh=mesh,
        in_specs=placed,
        out_specs=(P("dp", "mp"), P("dp", "mp"), P("dp", "mp"), P(("dp", "mp"), None)),
        check_vma=False,
    )
```

```python
import jax
import jax.numpy as jnp
from jax import lax
from jax.experimental import pallas as pl
from jax.experimental.pallas import tpu as pltpu
from jax.sharding import PartitionSpec as P

D = 8192
DV = 3200
PATCH = 256
LANE = 128
CHUNK = 16
BF = jnp.bfloat16
F32 = jnp.float32
VMEM = pl.BlockSpec(memory_space=pltpu.VMEM)
SMEM = pl.BlockSpec(memory_space=pltpu.SMEM)
HBM = pl.BlockSpec(memory_space=pltpu.HBM)
ANY = pl.BlockSpec(memory_space=pl.ANY)
DMA = pltpu.SemaphoreType.DMA

RING = 4
UP = [(2 * y + c, 2 * ((y + 1) % RING) + c) for y in range(RING) for c in range(2)]
DOWN = [(2 * y + c, 2 * ((y + 3) % RING) + c) for y in range(RING) for c in range(2)]
ACROSS = [(2 * y + c, 2 * ((y + 2) % RING) + c) for y in range(RING) for c in range(2)]
SPLIT = [(2 * y + c, 2 * ((y + 1 + 2 * c) % RING) + c) for y in range(RING) for c in range(2)]
PEER = [(2 * y + c, 2 * y + 1 - c) for y in range(RING) for c in range(2)]


def up(x):
    return lax.ppermute(x, "mp", UP)


def down(x):
    return lax.ppermute(x, "mp", DOWN)


def across(x):
    return lax.ppermute(x, "mp", ACROSS)


def peer(x):
    return lax.ppermute(x, "mp", PEER)


TOKEN = jax.ShapeDtypeStruct((8, LANE), F32)


def call(kernel, name, outs, args, scalars=0, far=(), far_outs=(), scratch=(), flops=0, after=(), token=False):
    size = sum(a.size * a.dtype.itemsize for a in args) + sum(o.size * o.dtype.itemsize for o in outs)
    args, outs = list(args), list(outs)
    ins, results = len(args), len(outs)

    def body(*refs):
        mine = refs[:ins] + refs[ins + len(after) : ins + len(after) + results]
        rest = refs[ins + len(after) + results :]
        if token:
            rest[0][...] = jnp.zeros(TOKEN.shape, F32)
            rest = rest[1:]
        kernel(*mine, *rest)

    return pl.pallas_call(
        body,
        in_specs=[SMEM if i < scalars else HBM if i in far else VMEM for i in range(ins)] + [ANY] * len(after),
        out_specs=[HBM if i in far_outs else VMEM for i in range(results)] + [VMEM] * token,
        out_shape=outs + [TOKEN] * token,
        scratch_shapes=list(scratch),
        compiler_params=pltpu.CompilerParams(vmem_limit_bytes=(52 if far else 8) * 1024 * 1024),
        cost_estimate=pl.CostEstimate(flops=flops, bytes_accessed=size, transcendentals=0),
        name=name,
    )(*args, *after)


def shape(dims, dtype):
    return jax.ShapeDtypeStruct(dims, dtype)


def dot(a, b):
    return jnp.dot(a, b, preferred_element_type=F32)


def dot_t(a, b):
    return lax.dot_general(a, b, (((1,), (1,)), ((), ())), preferred_element_type=F32)


def as_row(column):
    n = column.shape[0]
    return jnp.transpose(jnp.broadcast_to(column, (n, LANE)))[:1]


def as_column(row):
    n = row.shape[1]
    return jnp.transpose(jnp.broadcast_to(row, (LANE, n)))[:, :1]


def lane_block(ref, index, rows=slice(None)):
    return ref[rows, pl.ds(pl.multiple_of(index * LANE, LANE), LANE)]


def vision_norm(vision, gain):
    def kernel(v_ref, g_ref, o_ref, s_ref):
        v = v_ref[...].astype(F32)
        scale = lax.rsqrt(jnp.mean(v * v, axis=1, keepdims=True) + 1e-06)
        s_ref[...] = scale
        o_ref[...] = (v * scale * g_ref[...]).astype(BF)

    rows = vision.shape[0]
    return call(
        kernel, "vision_norm", [shape(vision.shape, BF), shape((rows, 1), F32)], [vision, gain], token=True
    )


def pack_grads(key_grad, value_grad, after):
    rows = key_grad.shape[0]
    slots = rows // PATCH
    per = PATCH // CHUNK
    grads = [g.reshape(slots, per, CHUNK, LANE) for g in (key_grad, value_grad)]

    def kernel(k_ref, v_ref, stack_ref, chunk_ref, sems):
        pairs = []
        for j, ref in enumerate((k_ref, v_ref)):
            for s in range(slots):
                pairs.append((ref.at[s], chunk_ref.at[pl.ds(j * per, per), s]))
            pairs.append((ref, stack_ref.at[j]))
        for wait in load_all(pairs, sems):
            wait()

    stack, chunks, token = call(
        kernel,
        "pack_grads",
        [shape((2, slots, per, CHUNK, LANE), BF), shape((2 * per, slots, CHUNK, LANE), BF)],
        grads,
        far=(0, 1),
        far_outs=(0, 1),
        scratch=[DMA((2 * slots + 2,))],
        after=after,
        token=True,
    )
    return stack.reshape(2 * rows, LANE), chunks, token


def take_blocks(index, x, after):
    count = index.shape[0]

    def kernel(index_ref, x_ref, o_ref):
        for j in range(count):
            o_ref[j] = x_ref[index_ref[j]]

    return call(kernel, "take_blocks", [shape((count,) + x.shape[1:], x.dtype)], [index, x], scalars=1, after=after, token=True)


def load_all(pairs, sems):
    copies = [pltpu.make_async_copy(src, dst, sems.at[i]) for i, (src, dst) in enumerate(pairs)]
    for copy in copies:
        copy.start()
    return [copy.wait for copy in copies]


def text_forward(text, gain, w_key, w_value, after):
    rows, width = text.shape
    blocks = w_key.shape[1] // LANE

    def kernel(t_far, g_ref, k_far, v_far, o_ref, q_ref, t_ref, k_ref, v_ref, scaled, sems):
        waits = load_all([(t_far, t_ref), (k_far, k_ref), (v_far, v_ref)], sems)
        waits[0]()

        @pl.loop(0, rows // LANE)
        def _(i):
            at = pl.ds(pl.multiple_of(i * LANE, LANE), LANE)
            t = t_ref[at].astype(F32)
            scaled[at] = (t * g_ref[...]).astype(BF)
            q_ref[pl.ds(i, 1)] = as_row(jnp.sum(t * t, axis=1, keepdims=True))

        waits[1]()
        waits[2]()

        @pl.loop(0, blocks)
        def _(b):
            w = jnp.concatenate([lane_block(k_ref, b), lane_block(v_ref, b)], axis=1)
            o_ref[b] = dot(scaled[...], w).astype(BF)

    return call(
        kernel,
        "text_forward",
        [shape((blocks, rows, 2 * LANE), BF), shape((rows // LANE, LANE), F32)],
        [text, gain, w_key, w_value],
        far=(0, 2, 3),
        after=after,
        token=True,
        scratch=[
            pltpu.VMEM(text.shape, BF),
            pltpu.VMEM(w_key.shape, BF),
            pltpu.VMEM(w_value.shape, BF),
            pltpu.VMEM((rows, width), BF),
            DMA((3,)),
        ],
        flops=4 * rows * width * w_key.shape[1],
    )


def image_forward(where, order, pieces, w_proj, gain, w_key, w_value, after):
    rows_each = PATCH // 8
    depth, width = w_proj.shape

    def kernel(where_ref, order_ref, *refs):
        piece_refs = refs[: len(pieces)]
        p_far, g_ref, k_far, v_far, e_ref, far_ref, near_ref, q_ref, p_ref, k_ref, v_ref, vis, scaled, sems = refs[
            len(pieces) :
        ]
        cuts = [slice(n * 256, (n + 1) * 256) for n in range(width // 256)]
        waits = load_all(
            [(p_far.at[:, at], p_ref.at[n]) for n, at in enumerate(cuts)] + [(k_far, k_ref), (v_far, v_ref)], sems
        )
        b = 0
        for ref in piece_refs:
            vis[pl.ds(pl.multiple_of(where_ref[b] * rows_each, rows_each), ref.shape[0])] = ref[...]
            b += ref.shape[0] // rows_each

        for n, at in enumerate(cuts):
            waits[n]()
            e_ref[:, at] = dot(vis[...], p_ref[n]).astype(BF)

        @pl.loop(0, PATCH // LANE)
        def _(i):
            at = pl.ds(pl.multiple_of(i * LANE, LANE), LANE)
            e = e_ref[at].astype(F32)
            scaled[at] = (e * g_ref[...]).astype(BF)
            q_ref[pl.ds(i, 1)] = as_row(jnp.sum(e * e, axis=1, keepdims=True))

        waits[-2]()
        waits[-1]()

        @pl.loop(0, RING)
        def _(b):
            there = order_ref[RING + b]
            w = jnp.concatenate([lane_block(k_ref, there), lane_block(v_ref, there)], axis=1)
            far_ref[b] = dot(scaled[...], w).astype(BF)
            own = order_ref[b]
            w = jnp.concatenate([lane_block(k_ref, own), lane_block(v_ref, own)], axis=1)
            near_ref[b] = dot(scaled[...], w)

    return call(
        kernel,
        "image_forward",
        [
            shape((PATCH, width), BF),
            shape((RING, PATCH, 2 * LANE), BF),
            shape((RING, PATCH, 2 * LANE), F32),
            shape((PATCH // LANE, LANE), F32),
        ],
        [where, order, *pieces, w_proj, gain, w_key, w_value],
        scalars=2,
        token=True,
        far=(2 + len(pieces), 4 + len(pieces), 5 + len(pieces)),
        scratch=[
            pltpu.VMEM((width // 256, depth, 256), BF),
            pltpu.VMEM(w_key.shape, BF),
            pltpu.VMEM(w_value.shape, BF),
            pltpu.VMEM((PATCH, depth), BF),
            pltpu.VMEM((PATCH, width), BF),
            DMA((width // 256 + 2,)),
        ],
        flops=2 * PATCH * width * (depth + 2 * w_key.shape[1]),
        after=after,
    )


def backward(order, pieces, w_key, w_value, gain, embed, after):
    rows, width = embed.shape
    cols = w_key.shape[1]
    cuts = width // 256

    def kernel(order_ref, *refs):
        piece_refs = refs[: len(pieces)]
        k_far, v_far, g_ref, e_far, d_out, i_ref, k_ref, v_ref, e_ref, gk, gv, sems, d_held, out_sems = refs[len(pieces) :]
        d_ref = d_held if rows > PATCH else d_out
        outgoing = []
        pairs = []
        b = 0
        for ref in piece_refs:
            for j in range(ref.shape[0] // (2 * rows)):
                at = pl.ds(pl.multiple_of(order_ref[b] * LANE, LANE), LANE)
                pairs.append((ref.at[pl.ds(2 * rows * j, rows)], gk.at[:, at]))
                pairs.append((ref.at[pl.ds(2 * rows * j + rows, rows)], gv.at[:, at]))
                b += 1
        for n in range(cuts):
            at = pl.ds(n * 256, 256)
            pairs += [(k_far.at[at], k_ref.at[at]), (v_far.at[at], v_ref.at[at])]
        pairs.append((e_far, e_ref))
        waits = load_all(pairs, sems)
        for wait in waits[:16]:
            wait()
        for n in range(cuts):
            at = slice(n * 256, (n + 1) * 256)
            waits[16 + 2 * n]()
            waits[17 + 2 * n]()
            d = dot_t(gk[...], k_ref[at]) + dot_t(gv[...], v_ref[at])
            d_ref[:, at] = d * g_ref[:, at]
            if rows > PATCH:
                outgoing.append(pltpu.make_async_copy(d_ref.at[:, at], d_out.at[:, at], out_sems.at[n]))
                outgoing[-1].start()
        waits[-1]()

        @pl.loop(0, rows // LANE)
        def _(i):
            at = pl.ds(pl.multiple_of(i * LANE, LANE), LANE)
            i_ref[pl.ds(i, 1)] = as_row(jnp.sum(d_ref[at] * e_ref[at].astype(F32), axis=1, keepdims=True))

        for copy in outgoing:
            copy.wait()

    n = len(pieces)
    return call(
        kernel,
        "backward",
        [shape((rows, width), F32), shape((rows // LANE, LANE), F32)],
        [order, *pieces, w_key, w_value, gain, embed],
        scalars=1,
        far=tuple(range(1, n + 3)) + (n + 4,),
        scratch=[
            pltpu.VMEM(w_key.shape, BF),
            pltpu.VMEM(w_value.shape, BF),
            pltpu.VMEM(embed.shape, BF),
            pltpu.VMEM((rows, cols), BF),
            pltpu.VMEM((rows, cols), BF),
            DMA((17 + 2 * cuts,)),
            pltpu.VMEM(embed.shape if rows > PATCH else (8, LANE), F32),
            DMA((cuts,)),
        ],
        flops=4 * rows * width * cols,
        after=after,
        far_outs=(0,) if rows > PATCH else (),
        token=True,
    )


def embed_grad(d, e, square_row, inner_row):
    scale = lax.rsqrt(as_column(square_row) / D + 1e-05)
    inner = as_column(inner_row) / D
    return scale * d - e * (scale * scale * scale * inner)


def image_backward(order, image_d, embed, square, inner, w_proj, after):
    depth, width = w_proj.shape
    rows_each = PATCH // 8
    half = PATCH // 2
    cut = 640

    def kernel(order_ref, d_ref, e_ref, q_ref, i_ref, p_far, far_ref, near_ref, p_ref, grad, turned, sems):
        cuts = [slice(n * cut, (n + 1) * cut) for n in range(depth // cut)]
        waits = load_all([(p_far.at[at], p_ref.at[at]) for at in cuts], sems)

        @pl.loop(0, PATCH // LANE)
        def _(i):
            at = pl.ds(pl.multiple_of(i * LANE, LANE), LANE)
            row = pl.ds(i, 1)
            grad[at] = embed_grad(d_ref[at], e_ref[at].astype(F32), q_ref[row], i_ref[row]).astype(BF)

        for b in range(8):
            at = pl.ds(pl.multiple_of(order_ref[b] * rows_each, rows_each), rows_each)
            turned[b * rows_each : (b + 1) * rows_each] = grad[at]

        for n, at in enumerate(cuts):
            waits[n]()
            r = dot_t(turned[...], p_ref[at])
            near_ref[:, at] = r[:half]
            far_ref[:, at] = r[half:].astype(BF)

    return call(
        kernel,
        "image_backward",
        [shape((half, depth), BF), shape((half, depth), F32)],
        [order, image_d, embed, square, inner, w_proj],
        scalars=1,
        far=(5,),
        scratch=[
            pltpu.VMEM(w_proj.shape, BF),
            pltpu.VMEM((PATCH, width), BF),
            pltpu.VMEM((PATCH, width), BF),
            DMA((depth // cut,)),
        ],
        flops=2 * PATCH * width * depth,
        after=after,
        token=True,
    )


def ring_first(near, other, after):
    _, n, c = near.shape
    h = n // 2

    def kernel(a_ref, b_ref, up_ref, down_ref, here_ref, above_ref, below_ref):
        def total(k, at):
            return a_ref[k, at] + b_ref[k, at].astype(F32)

        first, second = slice(0, h), slice(h, n)
        up_ref[first] = total(2, first).astype(BF)
        up_ref[second] = total(1, second).astype(BF)
        down_ref[first] = total(3, first).astype(BF)
        down_ref[second] = total(2, second).astype(BF)
        here_ref[...] = total(0, slice(0, n))
        above_ref[...] = total(1, first)
        below_ref[...] = total(3, second)

    return call(
        kernel,
        "ring_first",
        [shape((n, c), BF), shape((n, c), BF), shape((n, c), F32), shape((h, c), F32), shape((h, c), F32)],
        [near, other],
        after=after,
        token=True,
    )


def ring_sum(near, far, after=()):
    up1, down1, here, above, below, token = ring_first(near, peer(far).reshape(near.shape), after)
    h = above.shape[0]
    up1, down1 = up(up1), down(down1)
    up2 = up((above + up1[:h].astype(F32)).astype(BF))
    down2 = down((below + down1[h:].astype(F32)).astype(BF))
    return (here, up1, down1, up2, down2), token


def ring_total(here_ref, up1_ref, down1_ref, up2_ref, down2_ref):
    h = up2_ref.shape[0]
    first = here_ref[:h] + down1_ref[:h].astype(F32) + up2_ref[...].astype(F32)
    second = here_ref[h:] + up1_ref[h:].astype(F32) + down2_ref[...].astype(F32)
    return first, second


def image_out(pieces, square, after):
    h = PATCH // 2

    def kernel(*refs):
        q_ref, o_ref = refs[5:7]
        for j, t in enumerate(ring_total(*refs[:5])):
            scale = lax.rsqrt(as_column(q_ref[j : j + 1]) / D + 1e-05)
            t = (t * scale).astype(BF)
            o_ref[j * h : (j + 1) * h] = t[:, :LANE]
            o_ref[PATCH + j * h : PATCH + (j + 1) * h] = t[:, LANE:]

    return call(kernel, "image_out", [shape((2 * PATCH, LANE), BF)], [*pieces, square], after=after, token=True)


def vision_out(pieces, vision, gain, scale):
    rows = vision.shape[0]
    h = rows // 2

    def kernel(*refs):
        v_ref, g_ref, s_ref, o_ref = refs[5:]
        for j, t in enumerate(ring_total(*refs[:5])):
            at = slice(j * h, (j + 1) * h)
            v, s = v_ref[at].astype(F32), s_ref[at]
            grad_h = t.astype(BF).astype(F32) * g_ref[...]
            inner = jnp.mean(grad_h * v, axis=1, keepdims=True)
            o_ref[at] = (s * grad_h - v * (s * s * s * inner)).astype(BF)

    return call(kernel, "vision_out", [shape(vision.shape, BF)], [*pieces, vision, gain, scale])[0]


def text_out(filled, text_d, text, square, inner, after):
    rows, width = text.shape
    parts = rows // LANE

    def kernel(f_ref, d_far, t_far, q_ref, i_ref, o_far, d_ref, t_ref, o_ref, sems, out_sems):
        cuts = [pl.ds(i * LANE, LANE) for i in range(parts)]
        waits = load_all([(d_far.at[at], d_ref.at[at]) for at in cuts] + [(t_far.at[at], t_ref.at[at]) for at in cuts], sems)
        outgoing = []
        for i, at in enumerate(cuts):
            waits[i]()
            waits[parts + i]()
            row = pl.ds(i, 1)
            grad = embed_grad(d_ref[at], t_ref[at].astype(F32), q_ref[row], i_ref[row])
            o_ref[at] = jnp.where(f_ref[i // (PATCH // LANE)] > 0, 0.0, grad).astype(BF)
            outgoing.append(pltpu.make_async_copy(o_ref.at[at], o_far.at[at], out_sems.at[i]))
            outgoing[-1].start()
        for copy in outgoing:
            copy.wait()

    return call(
        kernel,
        "text_out",
        [shape((rows, width), BF)],
        [filled, text_d, text, square, inner],
        scalars=1,
        far=(1, 2),
        far_outs=(0,),
        scratch=[
            pltpu.VMEM(text.shape, F32),
            pltpu.VMEM(text.shape, BF),
            pltpu.VMEM(text.shape, BF),
            DMA((2 * parts,)),
            DMA((parts,)),
        ],
        after=after,
        token=True,
    )


def key_value_out(filled, text_kv, square, arrived):
    rows = text_kv.shape[0]
    per = PATCH // CHUNK

    def kernel(f_ref, t_ref, q_ref, a_ref, k_ref, v_ref):
        for s in range(rows // PATCH):
            @pl.when(f_ref[s] > 0)
            def _():
                for c in range(per):
                    at = pl.ds(s * PATCH + c * CHUNK, CHUNK)
                    k_ref[at] = a_ref[c, s]
                    v_ref[at] = a_ref[per + c, s]

            @pl.when(f_ref[s] == 0)
            def _():
                for i in range(PATCH // LANE):
                    j = s * (PATCH // LANE) + i
                    at = pl.ds(j * LANE, LANE)
                    scale = lax.rsqrt(as_column(q_ref[j : j + 1]) / D + 1e-05)
                    t = (t_ref[at].astype(F32) * scale).astype(BF)
                    k_ref[at] = t[:, :LANE]
                    v_ref[at] = t[:, LANE:]

    return call(
        kernel,
        "key_value_out",
        [shape((rows, LANE), BF), shape((rows, LANE), BF)],
        [filled, text_kv, square, arrived],
        scalars=1,
    )


def join(core, x, other):
    rows = x.shape[0]

    def kernel(c_ref, x_ref, other_ref, o_ref):
        for c in range(2):
            @pl.when(c_ref[0] == c)
            def _():
                o_ref[c * rows : (c + 1) * rows] = x_ref[...]
                o_ref[(1 - c) * rows : (2 - c) * rows] = other_ref[...]

    return call(kernel, "join", [shape((2 * rows,) + x.shape[1:], x.dtype)], [core, x, other], scalars=1)[0]


def chip_gather(core, x):
    rows = x.shape[0]
    block = join(core, x, peer(x))
    near = lax.ppermute(block, "mp", SPLIT)
    far = lax.ppermute(lax.dynamic_slice_in_dim(near, core[0] * rows, rows), "mp", SPLIT)
    return [block, near, peer(near), far, peer(far)]


def small_sum(x):
    pair = x + peer(x)
    return (pair + up(pair)) + (down(pair) + across(pair))


def shards(
    vision,
    vision_gain,
    image_slot,
    text_embed,
    w_proj,
    llm_gain,
    w_key,
    w_value,
    key_grad,
    value_grad,
):
    dp = lax.axis_size("dp")
    here = lax.axis_index("dp")
    m = lax.axis_index("mp")
    y, c = m // 2, m % 2
    slots = text_embed.shape[0] // PATCH
    text_rows = text_embed.shape[0] // LANE

    rel = jnp.arange(8, dtype=jnp.int32)
    order = ((y + rel % RING) % RING) * 2 + (c ^ (rel // RING))
    core = c[None]
    near, next_, far = (y + 3 + 2 * c) % RING, (y + 1 + 2 * c) % RING, (y + 2) % RING
    where = jnp.stack(
        [2 * y, 2 * y + 1, 2 * near, 2 * near + 1, 2 * next_, 2 * next_ + 1, 2 * far + c, 2 * far + 1 - c]
    )
    slot_ids = jnp.arange(dp * slots, dtype=jnp.int32)
    onehot = slot_ids[:, None] == image_slot[None, :]
    owner = jnp.sum(jnp.where(onehot, jnp.arange(dp, dtype=jnp.int32)[None, :], 0), axis=1)
    mine = slot_ids[:slots] + here * slots
    filled = jnp.any(mine[:, None] == image_slot[None, :], axis=1).astype(jnp.int32)
    gain = llm_gain[None]
    vis_gain = vision_gain[None]

    vis_normed, vis_scale, norm_done = vision_norm(vision, vis_gain)
    with jax.named_scope("vision_gather"):
        vis_parts = chip_gather(core, vis_normed)

    grad_stack, grad_chunks, packed_done = pack_grads(key_grad, value_grad, [norm_done])
    with jax.named_scope("slot_grads_spread"):
        spread = lax.all_to_all(grad_chunks, "dp", split_axis=0, concat_axis=0, tiled=True)
    with jax.named_scope("text_grad_gather"):
        text_g = lax.all_gather(grad_stack, "mp", axis=0, tiled=True)
    picked, picked_done = take_blocks(
        image_slot, spread.reshape(dp * slots, CHUNK, LANE), [packed_done, vis_parts[3]]
    )
    with jax.named_scope("slot_grads_collect"):
        image_kv_grad = lax.all_to_all(picked, "dp", split_axis=0, concat_axis=0, tiled=True)

    embed, far, near, image_square, image_done = image_forward(
        where, order, vis_parts, w_proj, gain, w_key, w_value, [picked_done]
    )
    text_part, text_square, text_done = text_forward(text_embed, gain, w_key, w_value, [image_done])
    with jax.named_scope("text_key_value_sum"):
        text_kv = lax.psum_scatter(text_part, "mp", scatter_dimension=0, tiled=False)
    with jax.named_scope("image_key_value_sum"):
        pieces, kv_ring = ring_sum(near, far, [text_done, image_kv_grad])
    with jax.named_scope("image_grad_gather"):
        image_g = chip_gather(core, image_kv_grad.reshape(2 * PATCH, LANE))
    with jax.named_scope("squares_sum"):
        squares = small_sum(jnp.concatenate([text_square, image_square]))
    text_square, image_square = squares[:text_rows], squares[text_rows:]

    image_kv, kv_out = image_out(pieces, image_square, ())
    with jax.named_scope("image_out_spread"):
        spread = lax.all_to_all(
            image_kv.reshape(dp, CHUNK, LANE), "dp", split_axis=0, concat_axis=0, tiled=True
        )

    packed, sent_done = take_blocks(owner, spread, ())
    with jax.named_scope("image_out_collect"):
        arrived = lax.all_to_all(
            packed.reshape(dp, slots, CHUNK, LANE), "dp", split_axis=0, concat_axis=0, tiled=True
        )

    text_d, text_inner, text_back = backward(
        rel, [text_g], w_key, w_value, gain, text_embed, [kv_ring, pieces[1], pieces[2]]
    )
    image_d, image_inner, _ = backward(where, image_g, w_key, w_value, gain, embed, [text_back, sent_done])
    with jax.named_scope("inner_sum"):
        inner = small_sum(jnp.concatenate([text_inner, image_inner]))
    d_far, d_near, back_done = image_backward(
        order, image_d, embed, image_square, inner[text_rows:], w_proj, [arrived]
    )
    with jax.named_scope("d_vis_sum"):
        d_pieces, d_ring = ring_sum(d_near.reshape(RING, -1, DV), d_far)
    text_grad, _ = text_out(
        filled, text_d, text_embed, text_square, inner[:text_rows], [back_done, *d_pieces[1:3]]
    )
    key_out, value_out = key_value_out(filled, text_kv, text_square, arrived)
    vision_grad = vision_out(d_pieces, vision, vis_gain, vis_scale)
    return key_out, value_out, text_grad, vision_grad


def solution(mesh):
    placed = (
        P(("dp", "mp"), None),
        P(),
        P(),
        P("dp", "mp"),
        P(None, "mp"),
        P("mp"),
        P("mp", None),
        P("mp", None),
        P("dp", "mp"),
        P("dp", "mp"),
    )
    return jax.shard_map(
        shards,
        mesh=mesh,
        in_specs=placed,
        out_specs=(P("dp", "mp"), P("dp", "mp"), P("dp", "mp"), P(("dp", "mp"), None)),
        check_vma=False,
    )
```
